512 devices in a mesh: wide: 64 (over z, y_lo, core), narrow: 8 (over y_hi, x).
Axes of the slice: x: 4, y: 4 (y_hi: 2, y_lo: 2; y = y_hi * 2 + y_lo), z: 16, core: 2. Of those that a mesh axis runs over, the one named last changes fastest.
Arguments:
- heat_source: float32 [512, 256, 128], P('wide', 'narrow'), may hold values from -8 to 8
- conductivity: float32 [512, 256, 128], P('wide', 'narrow'), may hold values from 0.2 to 5
Outputs:
- solution: float32 [512, 256, 128], P('wide', 'narrow')
The draws below stay inside these ranges and needn't reach their ends.
All inputs are finite; a program needn't handle non-finite values.
Results may differ from the reference program's by a relative error of at most 0.0049.
Values sent between devices are 32-bit elements; how exact they have to be, the bound alone decides.
A program may use at most 64 MiB of HBM per device.

```python
import math
import jax
import jax.numpy as jnp

DEGREE = 3
CITERS = 4
NX = 512
NY = 256
NZ = 128


def draw_heat_source(key, part):
    rough = jax.random.normal(key, (NX, NY, NZ), jnp.float32)
    value = rough
    return jnp.clip(value, -8.0, 8.0)


def level_of(own_key, extent, pieces, least, largest):
    factor_of = 1.0
    for axis_at, shards_of in pieces:
        draws = jax.random.uniform(jax.random.fold_in(jax.random.fold_in(own_key, 6), axis_at), (shards_of,), jnp.float32, least / len(pieces), largest / len(pieces))
        factor_of = factor_of * jnp.repeat(jnp.exp(draws), extent[axis_at] // shards_of).reshape((-1,) + (1,) * (len(extent) - 1 - axis_at))
    return factor_of


def setup_inputs(seed: int = 0) -> dict:
    streams_of = jax.random.split(jax.random.key(seed), 3)
    return {
        "heat_source": draw_heat_source(jax.random.fold_in(streams_of[2], 71), 0),
        "conductivity": jnp.clip(jnp.exp(math.log(5.0) - 3.218876 * jax.random.uniform(streams_of[1], (NX, NY, NZ), jnp.float32) ** level_of(streams_of[1], (NX, NY, NZ), ((0, 64), (1, 8)), -0.2, 0.2)), 0.2, 5.0),
    }


mass_shift = 0.002
cheb_low = 0.25
cheb_high = 2.0


def level_ops(cond_grid, level_scale):
    padded_cond = jnp.pad(cond_grid, 1)
    center = padded_cond[1:-1, 1:-1, 1:-1]
    face_coef = [
        0.5 * (center + padded_cond[2:, 1:-1, 1:-1]),
        0.5 * (center + padded_cond[:-2, 1:-1, 1:-1]),
        0.5 * (center + padded_cond[1:-1, 2:, 1:-1]),
        0.5 * (center + padded_cond[1:-1, :-2, 1:-1]),
        0.5 * (center + padded_cond[1:-1, 1:-1, 2:]),
        0.5 * (center + padded_cond[1:-1, 1:-1, :-2]),
    ]
    coef_total = face_coef[0] + face_coef[1] + face_coef[2] + face_coef[3] + face_coef[4] + face_coef[5]
    diagonal = mass_shift + level_scale * coef_total

    def operate(field):
        padded = jnp.pad(field, 1)
        beside = face_coef[0] * padded[2:, 1:-1, 1:-1] + face_coef[1] * padded[:-2, 1:-1, 1:-1]
        beside = beside + face_coef[2] * padded[1:-1, 2:, 1:-1] + face_coef[3] * padded[1:-1, :-2, 1:-1]
        beside = beside + face_coef[4] * padded[1:-1, 1:-1, 2:] + face_coef[5] * padded[1:-1, 1:-1, :-2]
        return diagonal * field - level_scale * beside

    return operate, diagonal


def restrict(field):
    size_x, size_y, size_z = field.shape
    return field.reshape(size_x // 2, 2, size_y // 2, 2, size_z // 2, 2).mean(axis=(1, 3, 5))


def prolong(field):
    size_x, size_y, size_z = field.shape
    wider = jnp.broadcast_to(field[:, None, :, None, :, None], (size_x, 2, size_y, 2, size_z, 2))
    return wider.reshape(2 * size_x, 2 * size_y, 2 * size_z)


def smooth(operate, diagonal, source, iterate):
    midpoint = 0.5 * (cheb_high + cheb_low)
    half_width = 0.5 * (cheb_high - cheb_low)
    sigma_one = midpoint / half_width
    damping = 1.0 / sigma_one
    if iterate is None:
        scaled = source / diagonal
        iterate = jnp.zeros_like(source)
    else:
        scaled = (source - operate(iterate)) / diagonal
    update = scaled / midpoint
    iterate = iterate + update
    for turn_index in range(DEGREE - 1):
        damp_next = 1.0 / (2.0 * sigma_one - damping)
        scaled = (source - operate(iterate)) / diagonal
        update = damp_next * damping * update + (2.0 * damp_next / half_width) * scaled
        iterate = iterate + update
        damping = damp_next
    return iterate


def coarse_solve(operate, diagonal, source):
    iterate = jnp.zeros_like(source)
    residual = source
    scaled = residual / diagonal
    direction = scaled
    inner_now = jnp.sum(residual * scaled)
    for turn_index in range(CITERS):
        image = operate(direction)
        step_size = inner_now / jnp.sum(direction * image)
        iterate = iterate + step_size * direction
        residual = residual - step_size * image
        if turn_index + 1 < CITERS:
            scaled = residual / diagonal
            inner_next = jnp.sum(residual * scaled)
            direction = scaled + (inner_next / inner_now) * direction
            inner_now = inner_next
    return iterate


def reference(heat_source, conductivity):
    cond_one = restrict(conductivity)
    cond_two = restrict(cond_one)
    op_zero, diag_zero = level_ops(conductivity, 1.0)
    op_one, diag_one = level_ops(cond_one, 0.25)
    op_two, diag_two = level_ops(cond_two, 1.0 / 16.0)
    fine_iter = smooth(op_zero, diag_zero, heat_source, None)
    src_one = restrict(heat_source - op_zero(fine_iter))
    mid_iter = smooth(op_one, diag_one, src_one, None)
    src_two = restrict(src_one - op_one(mid_iter))
    coarse_iter = coarse_solve(op_two, diag_two, src_two)
    mid_iter = smooth(op_one, diag_one, src_one, mid_iter + prolong(coarse_iter))
    return smooth(op_zero, diag_zero, heat_source, fine_iter + prolong(mid_iter))
```

```python
import functools
import jax
import jax.numpy as jnp
from jax import lax
from jax.experimental import pallas as pl
from jax.experimental.pallas import tpu as pltpu
from jax.sharding import PartitionSpec as P

MASS = 0.002
LOW, HIGH = 0.25, 2.0
THETA = 0.5 * (HIGH + LOW)
DELTA = 0.5 * (HIGH - LOW)
SIGMA = THETA / DELTA
RHO1 = 1.0 / SIGMA
RHO2 = 1.0 / (2.0 * SIGMA - RHO1)
RHO3 = 1.0 / (2.0 * SIGMA - RHO2)
KEEP1, GAIN1 = RHO2 * RHO1, 2.0 * RHO2 / DELTA
KEEP2, GAIN2 = RHO3 * RHO2, 2.0 * RHO3 / DELTA
F32 = jnp.float32
LANES = 128
MESH = pl.DeviceIdType.MESH


class Level:
    def __init__(self, planes, first, own, rows, own_rows, repeat, scale):
        self.planes, self.first, self.own = planes, first, own
        self.rows, self.own_rows, self.repeat, self.scale = rows, own_rows, repeat, scale


FINE = Level(16, 4, 8, 48, 32, 1, 1.0)
MID = Level(20, 8, 4, 32, 16, 2, 0.25)
COARSE = Level(14, 6, 2, 24, 8, 4, 1.0 / 16.0)

FIELDS = ("k", "raw", "cx", "cyu", "cyd", "czr", "czl", "inv", "diag", "src", "hat", "upd", "it")


def planes(lo, hi, fn, unroll=2):
    count = hi - lo
    while count % unroll:
        unroll -= 1

    def step(i, carry):
        for k in range(unroll):
            fn(lo + i * unroll + k)
        return carry

    lax.fori_loop(0, count // unroll, step, 0)


def roll_rows(x, by):
    return pltpu.roll(x, by % x.shape[0], 0)


def roll_lanes(x, by):
    return pltpu.roll(x, by % LANES, 1)


def lane_of(rows):
    return lax.broadcasted_iota(jnp.int32, (rows, LANES), 1)


def row_of(rows):
    return lax.broadcasted_iota(jnp.int32, (rows, LANES), 0)


def near_sum(lv, f, ref, p, centers):
    cxu, cxd = f["cx"][p], f["cx"][p - 1]
    cyu, cyd, czr, czl = f["cyu"][p], f["cyd"][p], f["czr"][p], f["czl"][p]
    sums = []
    for v, c in enumerate(centers):
        at = ref.at[v] if len(ref.shape) == 4 else ref
        sums.append(
            cxu * at[p + 1]
            + cxd * at[p - 1]
            + cyu * roll_rows(c, -1)
            + cyd * roll_rows(c, 1)
            + czr * roll_lanes(c, -lv.repeat)
            + czl * roll_lanes(c, lv.repeat)
        )
    return sums


def mask_planes(lv, f, w, n, wide, narrow, raw="k"):
    rows = row_of(lv.rows) + (n * lv.own_rows - 8)
    inside = (rows >= 0) & (rows < lv.own_rows * narrow)

    def one(p):
        at = w * lv.own + p - lv.first
        ok = inside & (at >= 0) & (at < lv.own * wide)
        f["k"][p] = jnp.where(ok, f[raw][p] * lv.scale, 0.0)

    planes(0, lv.planes, one)


def coefficients(lv, f, w, n, wide, narrow, lo, hi):
    rows = row_of(lv.rows) + (n * lv.own_rows - 8)
    inside = (rows >= 0) & (rows < lv.own_rows * narrow)
    lane = lane_of(lv.rows)
    last = lane >= LANES - lv.repeat
    edge = last | (lane < lv.repeat)
    f["cx"][lo - 1] = 0.5 * (f["k"][lo - 1] + f["k"][lo])

    def one(p):
        k = f["k"][p]
        cxu = 0.5 * (k + f["k"][p + 1])
        cxd = 0.5 * (k + f["k"][p - 1])
        cyu = 0.5 * (k + roll_rows(k, -1))
        cyd = roll_rows(cyu, 1)
        czr = jnp.where(last, 0.0, 0.5 * (k + roll_lanes(k, -lv.repeat)))
        czl = roll_lanes(czr, lv.repeat)
        d = MASS + (cxu + cxd + cyu + cyd + czr + czl + jnp.where(edge, 0.5 * k, 0.0))
        at = w * lv.own + p - lv.first
        ok = inside & (at >= 0) & (at < lv.own * wide)
        f["cx"][p] = cxu
        f["cyu"][p] = cyu
        f["cyd"][p] = cyd
        f["czr"][p] = czr
        f["czl"][p] = czl
        f["diag"][p] = d
        f["inv"][p] = jnp.where(ok, 1.0 / d, 0.0)

    planes(lo, hi, one)


def restrict(lv, read, mix, out):
    for j in range(lv.own // 2):
        mix[j] = read(2 * j) + read(2 * j + 1)
    half = lv.own_rows // 2
    even = lax.rem(lane_of(half) // lv.repeat, 2) == 0
    for j in range(lv.own // 2):
        x = mix[j, pl.ds(0, half, stride=2), :] + mix[j, pl.ds(1, half, stride=2), :]
        x = x + jnp.where(even, roll_lanes(x, -lv.repeat), roll_lanes(x, lv.repeat))
        out(j, 0.125 * x)


def smooth_down(lv, f, lo, hi):
    def first(p):
        hat = f["src"][p] * f["inv"][p]
        f["hat"][p] = hat
        f["upd"][p] = hat * (1.0 / THETA)

    planes(lo, hi, first)

    def second(p):
        x = f["upd"][p]
        (s,) = near_sum(lv, f, f["upd"], p, [x])
        z = f["hat"][p] + f["inv"][p] * s - x
        f["tmp"][p] = x + (KEEP1 * x + GAIN1 * z)

    planes(lo + 1, hi - 1, second)

    def third(p):
        x = f["tmp"][p]
        (s,) = near_sum(lv, f, f["tmp"], p, [x])
        z = f["hat"][p] + f["inv"][p] * s - x
        f["it"][p] = x + (KEEP2 * (x - f["upd"][p]) + GAIN2 * z)

    planes(lo + 2, hi - 2, third)


def smooth_up(lv, f, a, b, e, lo, hi):
    count = a.shape[0]

    def sweep(p, old, new, keep, gain):
        centers = [old[v, p] for v in range(count)]
        sums = near_sum(lv, f, old, p, centers)
        inv = f["inv"][p]
        for v in range(count):
            z = inv * sums[v] - centers[v]
            if v == 0:
                z = z + f["hat"][p]
            u = gain * z if keep is None else keep * e[v, p] + gain * z
            if new is not None:
                e[v, p] = u
            (b if new is None else new)[v, p] = centers[v] + u

    planes(lo + 1, hi - 1, lambda p: sweep(p, a, b, None, 1.0 / THETA), 1)
    planes(lo + 2, hi - 2, lambda p: sweep(p, b, a, KEEP1, GAIN1), 1)
    planes(lo + 3, hi - 3, lambda p: sweep(p, a, None, KEEP2, GAIN2), 1)


def solve4(m):
    small = m[1] < 0.5 * m[0]
    pick = lambda a, b: jnp.where(small, a, b)
    g = [pick(m[k + 1], m[8 + k] - m[9 + k]) for k in range(7)]
    rhs = [pick(m[k], m[8 + k]) for k in range(4)]
    rows = [[g[i + j] for j in range(4)] for i in range(4)]
    inv = []
    for i in range(4):
        piv = rows[i][i]
        good = piv > 1e-7 * g[2 * i]
        inv.append(jnp.where(good, 1.0 / jnp.where(good, piv, 1.0), 0.0))
        for r in range(i + 1, 4):
            factor = rows[i][r] * inv[i]
            rows[r] = [rows[r][j] - factor * rows[i][j] if j >= r else None for j in range(4)]
            rhs[r] = rhs[r] - factor * rhs[i]
    y = [None] * 4
    for i in (3, 2, 1, 0):
        t = rhs[i]
        for j in range(i + 1, 4):
            t = t - rows[i][j] * y[j]
        y[i] = t * inv[i]
    turned = [
        y[0] + y[1] + y[2] + y[3],
        -(y[1] + 2.0 * y[2] + 3.0 * y[3]),
        y[2] + 3.0 * y[3],
        -y[3],
    ]
    return [pick(a, b) for a, b in zip(y, turned)]


HALO_MID = [(dw, dn) for dw in (1, -1, 0, 2, -2) for dn in (0, 1, -1) if (dw, dn) != (0, 0)]
HALO_COARSE = [(dw, dn) for dw in (0, 1, -1, 2, -2, 3, -3) for dn in (1, -1, 0) if (dw, dn) != (0, 0)]
HALO_FINE = [(dw, dn) for dw in (1, -1, 0) for dn in (0, 1, -1) if (dw, dn) != (0, 0)]


def kernel(wide, narrow, names, heat, cond, out, *refs):
    s = dict(zip(names, refs))
    send_sem, recv_sem = s["send_sem"], s["recv_sem"]
    local_sem = s["local_sem"]
    w, n = lax.axis_index("wide"), lax.axis_index("narrow")
    z, q = w // 4, lax.rem(w, 4)
    stacks = wide // 4

    f0 = {k: s["f0_" + k] for k in FIELDS + ("tmp",)}
    f1 = {k: s["f1_" + k] for k in FIELDS + ("tmp",)}
    f2 = {k: s["f2_" + k] for k in FIELDS + ("tmp",) if "f2_" + k in s}

    def near(dw, dn):
        return (lax.rem(w + (dw + wide), wide), lax.rem(n + (dn + narrow), narrow))

    plane_peers = [
        (z * 4 + lax.rem(q + dq, 4), lax.rem(n + dn, narrow))
        for dn in sorted(range(narrow), key=lambda d: -min(d, narrow - d))
        for dq in (2, 3, 1, 0)
        if (dq, dn) != (0, 0)
    ]
    stack_peers = [
        (lax.rem(z + dz, stacks) * 4 + q, n)
        for dz in sorted(range(1, stacks), key=lambda d: -min(d, stacks - d))
    ]

    own_heat = pltpu.make_async_copy(heat, f0["src"].at[4:12, 8:40], local_sem.at[0])
    own_cond = pltpu.make_async_copy(cond, f0["k"].at[4:12, 8:40], local_sem.at[1])
    own_cond.start()
    own_heat.start()

    barrier = pltpu.get_barrier_semaphore()
    greeted = stack_peers + plane_peers + [near(*d) for d in HALO_COARSE]
    for peer in greeted:
        pl.semaphore_signal(barrier, inc=1, device_id=peer, device_id_type=MESH)

    used = [0]

    def send(src, dst, peer):
        i = used[0]
        used[0] += 1
        copy = pltpu.make_async_remote_copy(
            src_ref=src,
            dst_ref=dst,
            send_sem=send_sem.at[i],
            recv_sem=recv_sem.at[i],
            device_id=peer,
            device_id_type=MESH,
        )
        copy.start()
        return copy

    def send_rows(lv, ref_from, ref_to, halo, depth):
        copies = []
        for dw, dn in halo:
            a, c, b = lv.first, lv.own, lv.first - dw * lv.own
            if depth < lv.own and dw:
                a, b = (lv.first + lv.own - depth, lv.first - depth) if dw > 0 else (lv.first, lv.first + lv.own)
                c = depth
            ra, rc, rb = (8, lv.own_rows, 8) if dn == 0 else (lv.own_rows, 8, 0) if dn > 0 else (8, 8, 8 + lv.own_rows)
            copies.append(
                send(ref_from.at[a : a + c, ra : ra + rc], ref_to.at[b : b + c, rb : rb + rc], near(dw, dn))
            )
        return copies

    own_cond.wait()
    own_heat.wait()
    low4 = row_of(8) < 4
    pack, got = s["pack"], s["got"]

    def pack_plane(p):
        h, c = f0["src"][p + 4, 32:40], f0["k"][p + 4, 32:40]
        pack[0, p] = jnp.where(low4, roll_rows(h, 4), c)
        h, c = f0["src"][p + 4, 8:16], f0["k"][p + 4, 8:16]
        pack[1, p] = jnp.where(low4, c, roll_rows(h, 4))

    planes(0, 8, pack_plane)

    def put1(j, x):
        f1["raw"][MID.first + j, 8:24] = x

    restrict(FINE, lambda p: f0["k"][4 + p, 8:40], s["mix0"], put1)

    def put2(j, x):
        f2["raw"][COARSE.first + j, 8:16] = x

    restrict(MID, lambda p: f1["raw"][8 + p, 8:24], s["mix1"], put2)

    pl.semaphore_wait(barrier, len(greeted))

    first = [
        send(cond.at[4:8], f0["k"].at[0:4, 8:40], near(1, 0)),
        send(cond.at[0:4], f0["k"].at[12:16, 8:40], near(-1, 0)),
        send(heat.at[5:8], f0["src"].at[1:4, 8:40], near(1, 0)),
        send(heat.at[0:3], f0["src"].at[12:15, 8:40], near(-1, 0)),
        send(pack.at[0], got.at[0, 4:12], near(0, 1)),
        send(pack.at[1], got.at[1, 4:12], near(0, -1)),
        send(pack.at[0, 4:8], got.at[0, 0:4], near(1, 1)),
        send(pack.at[1, 4:8], got.at[1, 0:4], near(1, -1)),
        send(pack.at[0, 0:4], got.at[0, 12:16], near(-1, 1)),
        send(pack.at[1, 0:4], got.at[1, 12:16], near(-1, -1)),
    ]
    conds = send_rows(MID, f1["raw"], f1["raw"], HALO_MID, MID.own)
    conds2 = send_rows(COARSE, f2["raw"], f2["raw"], HALO_COARSE, COARSE.own)
    for c in first:
        c.wait_recv()

    def unpack(p):
        f0["k"][p, 0:8] = jnp.where(low4, 0.0, got[0, p])
        f0["k"][p, 40:48] = jnp.where(low4, got[1, p], 0.0)
        f0["src"][p, 0:8] = roll_rows(got[0, p], 4)
        f0["src"][p, 40:48] = roll_rows(got[1, p], 4)

    planes(0, 16, unpack)
    mask_planes(FINE, f0, w, n, wide, narrow)
    coefficients(FINE, f0, w, n, wide, narrow, 1, 15)
    smooth_down(FINE, f0, 1, 15)

    def residual(lv, f):
        def one(p):
            x = f["it"][p]
            (t,) = near_sum(lv, f, f["it"], p, [x])
            f["tmp"][p] = f["src"][p] + t - f["diag"][p] * x

        planes(lv.first, lv.first + lv.own, one)

    residual(FINE, f0)

    def put_src1(j, x):
        f1["src"][MID.first + j, 8:24] = x

    restrict(FINE, lambda p: f0["tmp"][4 + p, 8:40], s["mix0"], put_src1)
    srcs = send_rows(MID, f1["src"], f1["src"], HALO_MID, MID.own)
    its = send_rows(FINE, f0["it"], s["edge"], HALO_FINE, 3)
    for c in conds:
        c.wait_recv()
    mask_planes(MID, f1, w, n, wide, narrow, "raw")
    coefficients(MID, f1, w, n, wide, narrow, 1, 19)
    for c in conds2:
        c.wait_recv()
    mask_planes(COARSE, f2, w, n, wide, narrow, "raw")
    coefficients(COARSE, f2, w, n, wide, narrow, 1, 13)
    for c in srcs:
        c.wait_recv()
    smooth_down(MID, f1, 1, 19)
    residual(MID, f1)
    u, zed = s["basis"], s["zed"]

    def put_z(j, x):
        zed[COARSE.first + j, 8:16] = x * f2["inv"][COARSE.first + j, 8:16]

    restrict(MID, lambda p: f1["tmp"][8 + p, 8:24], s["mix1"], put_z)
    zs = send_rows(COARSE, zed, zed, HALO_COARSE, COARSE.own)
    for c in zs:
        c.wait_recv()

    rows2 = row_of(24) + (n * 8 - 8)
    in_rows = (rows2 >= 0) & (rows2 < 8 * narrow)

    def clean(p):
        at = w * 2 + p - 6
        u[0, p] = jnp.where(in_rows & (at >= 0) & (at < 2 * wide), zed[p], 0.0)

    planes(0, 14, clean)
    for k in range(4):
        lo, hi = (1 + k, 13 - k) if k < 3 else (6, 8)

        def one(p, k=k):
            x = u[k, p]
            (t,) = near_sum(COARSE, f2, u.at[k], p, [x])
            u[k + 1, p] = x - f2["inv"][p] * t

        planes(lo, hi, one)

    row8 = row_of(8)
    sums = [jnp.zeros((8, LANES), F32) for _ in range(16)]
    for p in (6, 7):
        d = f2["diag"][p, 8:16]
        b = [u[k, p, 8:16] for k in range(5)]
        c = [
            b[0],
            b[0] - b[1],
            b[0] - 2.0 * b[1] + b[2],
            b[0] - 3.0 * (b[1] - b[2]) - b[3],
            b[0] - 4.0 * (b[1] + b[3]) + 6.0 * b[2] + b[4],
        ]
        for at, vs in ((0, b), (8, c)):
            for k in range(8):
                sums[at + k] = sums[at + k] + vs[k // 2] * d * vs[(k + 1) // 2]
    tiles = []
    for half in (0, 8):
        m = jnp.zeros((8, LANES), F32)
        for k in range(8):
            m = jnp.where(row8 == k, jnp.sum(sums[half + k], axis=0, keepdims=True), m)
        tiles.append(jnp.sum(m, axis=1, keepdims=True))
    lane8 = lane_of(8)
    spread = jnp.where(lane8 == row8, tiles[0], 0.0) + jnp.where(lane8 == row8 + 8, tiles[1], 0.0)
    mine, all1, all2 = s["mine"], s["all1"], s["all2"]
    mine[0] = jnp.sum(spread, axis=0, keepdims=True)
    rank = q * narrow + n
    all1[rank] = mine[0]

    def send_sum(src, dst, peers, at):
        copies = []
        for i, peer in enumerate(peers):
            copy = pltpu.make_async_remote_copy(
                src_ref=src,
                dst_ref=dst,
                send_sem=s["sum_send"].at[at + i],
                recv_sem=s["sum_recv"].at[at + i],
                device_id=peer,
                device_id_type=MESH,
            )
            copy.start()
            copies.append(copy)
        return copies

    sums1 = send_sum(mine.at[0], all1.at[rank], plane_peers, 0)

    xa, xb, xe = s["mid_a"], s["mid_b"], s["mid_e"]

    def start_mid(p):
        xa[0, p] = f1["it"][p]
        for k in range(4):
            t = u[k, p // 2 + 2, 4:20]
            xa[1 + k, p, pl.ds(0, 16, stride=2), :] = t
            xa[1 + k, p, pl.ds(1, 16, stride=2), :] = t

    planes(3, 17, start_mid)
    smooth_up(MID, f1, xa, xb, xe, 3, 17)

    for c in sums1:
        c.wait_recv()
    mine[1] = jnp.sum(all1[...], axis=0)
    all2[z] = mine[1]
    sums2 = send_sum(mine.at[1], all2.at[z], stack_peers, len(plane_peers))

    for c in its:
        c.wait_recv()
    ya, yb, ye = s["fine_a"], s["fine_b"], s["fine_e"]
    edge = s["edge"]

    def own_edge(p):
        edge[p, 8:40] = f0["it"][p, 8:40]

    planes(4, 12, own_edge)

    def start_fine(p):
        for k in range(5):
            t = xb[k, p // 2 + 6, 4:28]
            ya[k, p, pl.ds(0, 24, stride=2), :] = t
            ya[k, p, pl.ds(1, 24, stride=2), :] = t
        ya[0, p] = ya[0, p] + jnp.where(f0["inv"][p] > 0.0, edge[p], 0.0)

    planes(1, 15, start_fine)
    smooth_up(FINE, f0, ya, yb, ye, 1, 15)

    for c in first + conds + conds2 + srcs + its + zs + sums1:
        c.wait_send()
    for c in sums2:
        c.wait_recv()
    total = jnp.sum(all2[...], axis=0)
    wide_total = jnp.broadcast_to(total, (8, LANES))
    ta = jnp.sum(jnp.where(lane8 == row8, wide_total, 0.0), axis=1, keepdims=True)
    tb = jnp.sum(jnp.where(lane8 == row8 + 8, wide_total, 0.0), axis=1, keepdims=True)
    ta, tb = jnp.broadcast_to(ta, (8, LANES)), jnp.broadcast_to(tb, (8, LANES))
    y = solve4([ta[k : k + 1] for k in range(8)] + [tb[k : k + 1] for k in range(8)])

    def combine(p):
        x = yb[0, p + 4, 8:40]
        for k in range(4):
            x = x + y[k] * yb[1 + k, p + 4, 8:40]
        out[p] = x

    planes(0, 8, combine)
    for c in sums2:
        c.wait_send()


def solution(mesh):
    wide, narrow = mesh.shape["wide"], mesh.shape["narrow"]

    def field(lv, *lead):
        return pltpu.VMEM((*lead, lv.planes, lv.rows, LANES), F32)

    scratch = {}
    for tag, lv in (("f0_", FINE), ("f1_", MID)):
        for k in FIELDS + ("tmp",):
            scratch[tag + k] = field(lv)
    for k in ("k", "raw", "cx", "cyu", "cyd", "czr", "czl", "inv", "diag"):
        scratch["f2_" + k] = field(COARSE)
    scratch["basis"] = field(COARSE, 5)
    scratch["zed"] = field(COARSE)
    scratch["edge"] = field(FINE)
    for k in ("a", "b", "e"):
        scratch["mid_" + k] = field(MID, 5)
        scratch["fine_" + k] = field(FINE, 5)
    scratch["pack"] = pltpu.VMEM((2, 8, 8, LANES), F32)
    scratch["got"] = pltpu.VMEM((2, 16, 8, LANES), F32)
    scratch["mix0"] = pltpu.VMEM((4, 32, LANES), F32)
    scratch["mix1"] = pltpu.VMEM((2, 16, LANES), F32)
    scratch["mine"] = pltpu.VMEM((2, 1, LANES), F32)
    scratch["all1"] = pltpu.VMEM((4 * narrow, 1, LANES), F32)
    scratch["all2"] = pltpu.VMEM((wide // 4, 1, LANES), F32)
    messages = 10 + 2 * len(HALO_MID) + 2 * len(HALO_COARSE) + len(HALO_FINE)
    scratch["send_sem"] = pltpu.SemaphoreType.DMA((messages,))
    scratch["recv_sem"] = pltpu.SemaphoreType.DMA((messages,))
    scratch["sum_send"] = pltpu.SemaphoreType.DMA((4 * narrow + wide // 4,))
    scratch["sum_recv"] = pltpu.SemaphoreType.DMA((4 * narrow + wide // 4,))
    scratch["local_sem"] = pltpu.SemaphoreType.DMA((2,))

    def body(heat, cond):
        return pl.pallas_call(
            functools.partial(kernel, wide, narrow, tuple(scratch)),
            out_shape=jax.ShapeDtypeStruct((8, 32, LANES), F32),
            in_specs=[pl.BlockSpec(memory_space=pl.ANY)] * 2,
            out_specs=pl.BlockSpec(memory_space=pltpu.VMEM),
            scratch_shapes=list(scratch.values()),
            compiler_params=pltpu.CompilerParams(
                collective_id=0, has_side_effects=True, vmem_limit_bytes=40 * 2**20
            ),
            cost_estimate=pl.CostEstimate(flops=50_000_000, bytes_accessed=400_000, transcendentals=0),
            name="vcycle",
        )(heat, cond)

    spec = P("wide", "narrow", None)
    return jax.shard_map(body, mesh=mesh, in_specs=(spec, spec), out_specs=spec, check_vma=False)
```

```python
import functools
import jax
import jax.numpy as jnp
from jax import lax
from jax.experimental import pallas as pl
from jax.experimental.pallas import tpu as pltpu
from jax.sharding import PartitionSpec as P

MASS = 0.002
LOW, HIGH = 0.25, 2.0
THETA = 0.5 * (HIGH + LOW)
DELTA = 0.5 * (HIGH - LOW)
SIGMA = THETA / DELTA
RHO1 = 1.0 / SIGMA
RHO2 = 1.0 / (2.0 * SIGMA - RHO1)
RHO3 = 1.0 / (2.0 * SIGMA - RHO2)
KEEP1, GAIN1 = RHO2 * RHO1, 2.0 * RHO2 / DELTA
KEEP2, GAIN2 = RHO3 * RHO2, 2.0 * RHO3 / DELTA
F32 = jnp.float32
LANES = 128
MESH = pl.DeviceIdType.MESH


class Level:
    def __init__(self, planes, first, own, rows, own_rows, repeat, scale):
        self.planes, self.first, self.own = planes, first, own
        self.rows, self.own_rows, self.repeat, self.scale = rows, own_rows, repeat, scale


FINE = Level(16, 4, 8, 48, 32, 1, 1.0)
MID = Level(20, 8, 4, 32, 16, 2, 0.25)
COARSE = Level(14, 6, 2, 24, 8, 4, 1.0 / 16.0)

FIELDS = ("k", "cx", "cyu", "cyd", "czr", "czl", "inv", "diag", "src", "hat", "upd", "it", "tmp")


def planes(lo, hi, fn, unroll=2):
    count = hi - lo
    while count % unroll:
        unroll -= 1
    if unroll == count:
        for p in range(lo, hi):
            fn(p)
        return

    def step(i, carry):
        for k in range(unroll):
            fn(lo + i * unroll + k)
        return carry

    lax.fori_loop(0, count // unroll, step, 0)


def roll_rows(x, by):
    return pltpu.roll(x, by % x.shape[0], 0)


def roll_lanes(x, by):
    return pltpu.roll(x, by % LANES, 1)


def lane_of(rows):
    return lax.broadcasted_iota(jnp.int32, (rows, LANES), 1)


def row_of(rows):
    return lax.broadcasted_iota(jnp.int32, (rows, LANES), 0)


def near_sum(lv, f, ref, p, centers):
    cxu, cxd = f["cx"][p], f["cx"][p - 1]
    cyu, cyd, czr, czl = f["cyu"][p], f["cyd"][p], f["czr"][p], f["czl"][p]
    sums = []
    for v, c in enumerate(centers):
        at = ref.at[v] if len(ref.shape) == 4 else ref
        sums.append(
            cxu * at[p + 1]
            + cxd * at[p - 1]
            + cyu * roll_rows(c, -1)
            + cyd * roll_rows(c, 1)
            + czr * roll_lanes(c, -lv.repeat)
            + czl * roll_lanes(c, lv.repeat)
        )
    return sums


def inside_rows(lv, n, narrow):
    rows = row_of(lv.rows) + (n * lv.own_rows - 8)
    return (rows >= 0) & (rows < lv.own_rows * narrow)


def inside(lv, in_rows, p, w, wide):
    at = w * lv.own + p - lv.first
    return in_rows & (at >= 0) & (at < lv.own * wide)


def pack2(lv, x, y):
    return jnp.where(lax.rem(lane_of(x.shape[0]) // (lv.repeat // 2), 2) == 0, x, y)


def unpack2(lv, xy):
    half = lv.repeat // 2
    first = lax.rem(lane_of(xy.shape[0]) // half, 2) == 0
    return jnp.where(first, xy, roll_lanes(xy, half)), jnp.where(first, roll_lanes(xy, -half), xy)


def coefficients(lv, f, in_rows, w, wide, lo, hi, unroll=2):
    lane = lane_of(lv.rows)
    last = lane >= LANES - lv.repeat
    edge = last | (lane < lv.repeat)
    f["cx"][lo - 1] = 0.5 * (f["k"][lo - 1] + f["k"][lo])

    def one(p):
        k = f["k"][p]
        cxu = 0.5 * (k + f["k"][p + 1])
        cxd = 0.5 * (k + f["k"][p - 1])
        cyu = 0.5 * (k + roll_rows(k, -1))
        cyd = roll_rows(cyu, 1)
        czr = jnp.where(last, 0.0, 0.5 * (k + roll_lanes(k, -lv.repeat)))
        czl = roll_lanes(czr, lv.repeat)
        d = MASS + (cxu + cxd + cyu + cyd + czr + czl + jnp.where(edge, 0.5 * k, 0.0))
        f["cx"][p] = cxu
        f["cyu"][p] = cyu
        f["cyd"][p] = cyd
        f["czr"][p] = czr
        f["czl"][p] = czl
        f["diag"][p] = d
        f["inv"][p] = jnp.where(inside(lv, in_rows, p, w, wide), 1.0 / d, 0.0)

    planes(lo, hi, one, unroll)


def restrict(lv, read, mix):
    for j in range(lv.own // 2):
        mix[j] = read(2 * j) + read(2 * j + 1)
    half = lv.own_rows // 2
    even = lax.rem(lane_of(half) // lv.repeat, 2) == 0
    found = []
    for j in range(lv.own // 2):
        x = mix[j, pl.ds(0, half, stride=2), :] + mix[j, pl.ds(1, half, stride=2), :]
        x = x + jnp.where(even, roll_lanes(x, -lv.repeat), roll_lanes(x, lv.repeat))
        found.append(0.125 * x)
    return found


def smooth_down(lv, f, lo, hi, unroll=2):
    def first(p):
        hat = f["src"][p] * f["inv"][p]
        f["hat"][p] = hat
        f["upd"][p] = hat * (1.0 / THETA)

    planes(lo, hi, first, unroll)

    def second(p):
        x = f["upd"][p]
        (s,) = near_sum(lv, f, f["upd"], p, [x])
        z = f["hat"][p] + f["inv"][p] * s - x
        f["tmp"][p] = x + (KEEP1 * x + GAIN1 * z)

    planes(lo + 1, hi - 1, second, unroll)

    def third(p):
        x = f["tmp"][p]
        (s,) = near_sum(lv, f, f["tmp"], p, [x])
        z = f["hat"][p] + f["inv"][p] * s - x
        f["it"][p] = x + (KEEP2 * (x - f["upd"][p]) + GAIN2 * z)

    planes(lo + 2, hi - 2, third, unroll)


def smooth_up(lv, f, a, b, e, lo, hi):
    count = a.shape[0]

    def sweep(p, old, new, keep, gain):
        centers = [old[v, p] for v in range(count)]
        sums = near_sum(lv, f, old, p, centers)
        inv = f["inv"][p]
        for v in range(count):
            z = inv * sums[v] - centers[v]
            if v == 0:
                z = z + f["hat"][p]
            u = gain * z if keep is None else keep * e[v, p] + gain * z
            if new is not None:
                e[v, p] = u
            (b if new is None else new)[v, p] = centers[v] + u

    planes(lo + 1, hi - 1, lambda p: sweep(p, a, b, None, 1.0 / THETA), 1)
    planes(lo + 2, hi - 2, lambda p: sweep(p, b, a, KEEP1, GAIN1), 1)
    planes(lo + 3, hi - 3, lambda p: sweep(p, a, None, KEEP2, GAIN2), 1)


def solve4(m):
    small = m[1] < 0.5 * m[0]
    pick = lambda a, b: jnp.where(small, a, b)
    g = [pick(m[k + 1], m[8 + k] - m[9 + k]) for k in range(7)]
    rhs = [pick(m[k], m[8 + k]) for k in range(4)]
    rows = [[g[i + j] for j in range(4)] for i in range(4)]
    inv = []
    for i in range(4):
        piv = rows[i][i]
        good = piv > 1e-7 * g[2 * i]
        inv.append(jnp.where(good, 1.0 / jnp.where(good, piv, 1.0), 0.0))
        for r in range(i + 1, 4):
            factor = rows[i][r] * inv[i]
            rows[r] = [rows[r][j] - factor * rows[i][j] if j >= r else None for j in range(4)]
            rhs[r] = rhs[r] - factor * rhs[i]
    y = [None] * 4
    for i in (3, 2, 1, 0):
        t = rhs[i]
        for j in range(i + 1, 4):
            t = t - rows[i][j] * y[j]
        y[i] = t * inv[i]
    turned = [
        y[0] + y[1] + y[2] + y[3],
        -(y[1] + 2.0 * y[2] + 3.0 * y[3]),
        y[2] + 3.0 * y[3],
        -y[3],
    ]
    return [pick(a, b) for a, b in zip(y, turned)]


def halo(reach):
    return [(dw, dn) for dw in reach for dn in (1, -1, 0) if (dw, dn) != (0, 0)]


NEAR_MID, FAR_MID = halo((1, -1, 0)), halo((2, -2))
NEAR_COARSE, FAR_COARSE = halo((1, -1, 0, 2, -2)), halo((3, -3))
HALO_FINE = halo((1, -1, 0))


def kernel(wide, narrow, names, heat, cond, out, *refs):
    s = dict(zip(names, refs))
    w, n = lax.axis_index("wide"), lax.axis_index("narrow")
    z, ylo, core = w // 4, lax.rem(w // 2, 2), lax.rem(w, 2)
    yhi, x = n // 4, lax.rem(n, 4)
    stacks = wide // 4

    f0 = {k: s["f0_" + k] for k in FIELDS}
    f1 = {k: s["f1_" + k] for k in FIELDS}
    f2 = {k: s["f2_" + k] for k in FIELDS if "f2_" + k in s}

    def near(dw, dn):
        return (lax.rem(w + (dw + wide), wide), lax.rem(n + (dn + narrow), narrow))

    def stack(dz):
        return (lax.rem(w + (4 * dz + wide), wide), n)

    def plane_peer(dx, dhi, dlo, dc):
        to = z * 4 + lax.rem(ylo + dlo, 2) * 2 + lax.rem(core + dc, 2)
        return (to, lax.rem(yhi + dhi, 2) * 4 + lax.rem(x + dx, 4))

    plane_peers = [
        plane_peer(*d)
        for d in sorted(
            [(dx, dhi, dlo, dc) for dx in range(4) for dhi in range(2) for dlo in range(2) for dc in range(2)],
            key=lambda d: -min(d[0], 4 - d[0]) - (1 if d[2] else 2 * d[1]),
        )
        if any(d)
    ]
    stack_peers = [stack(d) for d in sorted(range(1, stacks), key=lambda d: -min(d, stacks - d))]

    barrier = pltpu.get_barrier_semaphore()
    greeted = NEAR_COARSE + FAR_COARSE
    for d in greeted:
        pl.semaphore_signal(barrier, inc=1, device_id=near(*d), device_id_type=MESH)
    own_heat = pltpu.make_async_copy(heat, f0["src"].at[4:12, 8:40], s["local_sem"].at[0])
    own_cond = pltpu.make_async_copy(cond, f0["k"].at[4:12, 8:40], s["local_sem"].at[1])
    own_cond.start()
    own_heat.start()

    used = [0]
    sent = []

    def send(src, dst, peer):
        i = used[0]
        used[0] += 1
        copy = pltpu.make_async_remote_copy(
            src_ref=src,
            dst_ref=dst,
            send_sem=s["send_sem"].at[i],
            recv_sem=s["recv_sem"].at[i],
            device_id=peer,
            device_id_type=MESH,
        )
        copy.start()
        sent.append(copy)
        return copy

    def send_rows(ref_from, ref_to, first, own, own_rows, reach, depth):
        copies = []
        for dw, dn in reach:
            a, c, b = first, own, first - dw * own
            if depth < own and dw:
                a, b = (first + own - depth, first - depth) if dw > 0 else (first, first + own)
                c = depth
            ra, rc, rb = (8, own_rows, 8) if dn == 0 else (own_rows, 8, 0) if dn > 0 else (8, 8, 8 + own_rows)
            copies.append(
                send(ref_from.at[a : a + c, ra : ra + rc], ref_to.at[b : b + c, rb : rb + rc], near(dw, dn))
            )
        return copies

    def send_mid(ref, reach):
        return send_rows(ref, ref, 4, 2, 16, reach, 2)

    def send_coarse(ref, reach):
        return send_rows(ref, ref, 3, 1, 8, reach, 1)

    def arrive(copies):
        for c in copies:
            c.wait_recv()

    tokens = [s["token0"], s["token1"], s["token2"]]

    def pass_token(i):
        for way in (1, -1):
            pl.semaphore_signal(tokens[i], inc=1, device_id=stack(way * 2**i), device_id_type=MESH)

    def take_token(i):
        pl.semaphore_wait(tokens[i], 2)

    pl.semaphore_wait(barrier, len(greeted))
    first = [
        send(cond.at[4:8], f0["k"].at[0:4, 8:40], near(1, 0)),
        send(cond.at[0:4], f0["k"].at[12:16, 8:40], near(-1, 0)),
        send(heat.at[5:8], f0["src"].at[1:4, 8:40], near(1, 0)),
        send(heat.at[0:3], f0["src"].at[12:15, 8:40], near(-1, 0)),
    ]
    own_cond.wait()
    own_heat.wait()
    low4 = row_of(8) < 4
    pack, got = s["pack"], s["got"]

    def pack_plane(p):
        h, c = f0["src"][p + 4, 32:40], f0["k"][p + 4, 32:40]
        pack[0, p] = jnp.where(low4, roll_rows(h, 4), c)
        h, c = f0["src"][p + 4, 8:16], f0["k"][p + 4, 8:16]
        pack[1, p] = jnp.where(low4, c, roll_rows(h, 4))

    planes(0, 8, pack_plane, 8)
    first += [
        send(pack.at[0], got.at[0, 4:12], near(0, 1)),
        send(pack.at[1], got.at[1, 4:12], near(0, -1)),
        send(pack.at[0, 4:8], got.at[0, 0:4], near(1, 1)),
        send(pack.at[1, 4:8], got.at[1, 0:4], near(1, -1)),
        send(pack.at[0, 0:4], got.at[0, 12:16], near(-1, 1)),
        send(pack.at[1, 0:4], got.at[1, 12:16], near(-1, -1)),
    ]

    k1p, k2p, s1p, z2p = s["k1p"], s["k2p"], s["s1p"], s["z2p"]
    one_up = restrict(FINE, lambda p: f0["k"][4 + p, 8:40], s["mix0"])
    two_up = restrict(MID, lambda p: one_up[p], s["mix1"])
    for j in range(2):
        k1p[4 + j, 8:24] = pack2(MID, one_up[2 * j], one_up[2 * j + 1])
    k2p[3, 8:16] = pack2(COARSE, two_up[0], two_up[1])

    in0, in1, in2 = (inside_rows(lv, n, narrow) for lv in (FINE, MID, COARSE))

    def unpack_cond(lv, packed, f, in_rows, p):
        for k, v in enumerate(unpack2(lv, packed[p])):
            ok = inside(lv, in_rows, 2 * p + k, w, wide)
            f["k"][2 * p + k] = jnp.where(ok, v * lv.scale, 0.0)

    arrive(first)
    pass_token(0)
    cond1 = send_mid(k1p, NEAR_MID)

    def unpack(p):
        ok = inside(FINE, in0, p, w, wide)
        lo, hi = f0["k"].at[p, 0:8], f0["k"].at[p, 40:48]
        lo[...] = jnp.where(low4, 0.0, got[0, p])
        hi[...] = jnp.where(low4, got[1, p], 0.0)
        f0["src"][p, 0:8] = roll_rows(got[0, p], 4)
        f0["src"][p, 40:48] = roll_rows(got[1, p], 4)
        f0["k"][p] = jnp.where(ok, f0["k"][p], 0.0)

    planes(0, 16, unpack, 4)
    coefficients(FINE, f0, in0, w, wide, 1, 15)
    smooth_down(FINE, f0, 1, 15)

    def residual(lv, f, unroll):
        def one(p):
            x = f["it"][p]
            (t,) = near_sum(lv, f, f["it"], p, [x])
            f["tmp"][p] = f["src"][p] + t - f["diag"][p] * x

        planes(lv.first, lv.first + lv.own, one, unroll)

    residual(FINE, f0, 2)
    r1 = restrict(FINE, lambda p: f0["tmp"][4 + p, 8:40], s["mix0"])
    for j in range(2):
        s1p[4 + j, 8:24] = pack2(MID, r1[2 * j], r1[2 * j + 1])
    src1 = send_mid(s1p, NEAR_MID)
    cond2 = send_coarse(k2p, NEAR_COARSE)
    its = send_rows(f0["it"], s["edge"], 4, 8, 32, HALO_FINE, 3)
    cond1_far = send_mid(k1p, FAR_MID)
    arrive(cond1)
    for p in range(2, 8):
        unpack_cond(MID, k1p, f1, in1, p)
    coefficients(MID, f1, in1, w, wide, 5, 15, 10)
    arrive(src1)
    take_token(0)
    pass_token(1)

    def unpack_src(p):
        f1["src"][2 * p], f1["src"][2 * p + 1] = unpack2(MID, s1p[p])

    for p in range(2, 8):
        unpack_src(p)
    smooth_down(MID, f1, 5, 15, 10)
    residual(MID, f1, 4)
    r2 = restrict(MID, lambda p: f1["tmp"][8 + p, 8:24], s["mix1"])
    arrive(cond2)
    for p in range(1, 6):
        unpack_cond(COARSE, k2p, f2, in2, p)
    coefficients(COARSE, f2, in2, w, wide, 3, 11, 8)
    z2p[3, 8:16] = pack2(COARSE, r2[0] * f2["inv"][6, 8:16], r2[1] * f2["inv"][7, 8:16])
    z2 = send_coarse(z2p, NEAR_COARSE)
    z2_far = send_coarse(z2p, FAR_COARSE)
    cond2_far = send_coarse(k2p, FAR_COARSE)
    src1_far = send_mid(s1p, FAR_MID)
    arrive(z2)
    take_token(1)
    pass_token(2)
    u = s["basis"]

    def unpack_z(p):
        for k, v in enumerate(unpack2(COARSE, z2p[p])):
            u[0, 2 * p + k] = jnp.where(inside(COARSE, in2, 2 * p + k, w, wide), v, 0.0)

    def apply_b(k, p):
        v = u[k, p]
        (t,) = near_sum(COARSE, f2, u.at[k], p, [v])
        u[k + 1, p] = v - f2["inv"][p] * t

    for p in range(1, 6):
        unpack_z(p)
    for k in range(4):
        for p in range(3 + k, 11 - k):
            apply_b(k, p)

    row8, lane8 = row_of(8), lane_of(8)
    sums = [jnp.zeros((8, LANES), F32) for _ in range(16)]
    for p in (6, 7):
        d = f2["diag"][p, 8:16]
        b = [u[k, p, 8:16] for k in range(5)]
        c = [
            b[0],
            b[0] - b[1],
            b[0] - 2.0 * b[1] + b[2],
            b[0] - 3.0 * (b[1] - b[2]) - b[3],
            b[0] - 4.0 * (b[1] + b[3]) + 6.0 * b[2] + b[4],
        ]
        for at, vs in ((0, b), (8, c)):
            for k in range(8):
                sums[at + k] = sums[at + k] + vs[k // 2] * d * vs[(k + 1) // 2]
    tiles = []
    for half in (0, 8):
        m = jnp.zeros((8, LANES), F32)
        for k in range(8):
            m = jnp.where(row8 == k, jnp.sum(sums[half + k], axis=0, keepdims=True), m)
        tiles.append(jnp.sum(m, axis=1, keepdims=True))
    spread = jnp.where(lane8 == row8, tiles[0], 0.0) + jnp.where(lane8 == row8 + 8, tiles[1], 0.0)
    mine, all1, all2 = s["mine"], s["all1"], s["all2"]
    mine[0] = jnp.sum(spread, axis=0, keepdims=True)
    rank = lax.rem(w, 4) * narrow + n
    all1[rank] = mine[0]

    def send_sum(src, dst, peers, at):
        copies = []
        for i, peer in enumerate(peers):
            copy = pltpu.make_async_remote_copy(
                src_ref=src,
                dst_ref=dst,
                send_sem=s["sum_send"].at[at + i],
                recv_sem=s["sum_recv"].at[at + i],
                device_id=peer,
                device_id_type=MESH,
            )
            copy.start()
            copies.append(copy)
        return copies

    sums1 = send_sum(mine.at[0], all1.at[rank], plane_peers, 0)

    arrive(cond2_far + z2_far)
    for p in (0, 6):
        unpack_cond(COARSE, k2p, f2, in2, p)
        unpack_z(p)
    coefficients(COARSE, f2, in2, w, wide, 1, 3)
    coefficients(COARSE, f2, in2, w, wide, 11, 13)
    for k in range(3):
        for p in (1 + k, 2 + k, 11 - k, 12 - k):
            apply_b(k, p)
    arrive(cond1_far + src1_far)
    for p in (0, 1, 8, 9):
        unpack_cond(MID, k1p, f1, in1, p)
        unpack_src(p)
    coefficients(MID, f1, in1, w, wide, 1, 5, 4)
    coefficients(MID, f1, in1, w, wide, 15, 19, 4)
    smooth_down(MID, f1, 1, 19)

    xa, xb, xe = s["mid_a"], s["mid_b"], s["mid_e"]

    def start_mid(p):
        xa[0, p] = f1["it"][p]
        for k in range(4):
            t = u[k, p // 2 + 2, 4:20]
            xa[1 + k, p, pl.ds(0, 16, stride=2), :] = t
            xa[1 + k, p, pl.ds(1, 16, stride=2), :] = t

    planes(3, 17, start_mid)
    smooth_up(MID, f1, xa, xb, xe, 3, 17)

    arrive(sums1)
    mine[1] = jnp.sum(all1[...], axis=0)
    all2[z] = mine[1]
    take_token(2)
    sums2 = send_sum(mine.at[1], all2.at[z], stack_peers, len(plane_peers))

    arrive(its)
    ya, yb, ye = s["fine_a"], s["fine_b"], s["fine_e"]
    edge = s["edge"]

    def own_edge(p):
        edge[p, 8:40] = f0["it"][p, 8:40]

    planes(4, 12, own_edge)

    def start_fine(p):
        for k in range(5):
            t = xb[k, p // 2 + 6, 4:28]
            ya[k, p, pl.ds(0, 24, stride=2), :] = t
            ya[k, p, pl.ds(1, 24, stride=2), :] = t
        ya[0, p] = ya[0, p] + jnp.where(f0["inv"][p] > 0.0, edge[p], 0.0)

    planes(1, 15, start_fine)
    smooth_up(FINE, f0, ya, yb, ye, 1, 15)
    for c in sent + sums1:
        c.wait_send()
    arrive(sums2)
    total = jnp.broadcast_to(jnp.sum(all2[...], axis=0), (8, LANES))
    ta = jnp.sum(jnp.where(lane8 == row8, total, 0.0), axis=1, keepdims=True)
    tb = jnp.sum(jnp.where(lane8 == row8 + 8, total, 0.0), axis=1, keepdims=True)
    ta, tb = jnp.broadcast_to(ta, (8, LANES)), jnp.broadcast_to(tb, (8, LANES))
    y = solve4([ta[k : k + 1] for k in range(8)] + [tb[k : k + 1] for k in range(8)])

    def combine(p):
        v = yb[0, p + 4, 8:40]
        for k in range(4):
            v = v + y[k] * yb[1 + k, p + 4, 8:40]
        out[p] = v

    planes(0, 8, combine, 4)
    for c in sums2:
        c.wait_send()


def solution(mesh):
    wide, narrow = mesh.shape["wide"], mesh.shape["narrow"]

    def field(lv, *lead):
        return pltpu.VMEM((*lead, lv.planes, lv.rows, LANES), F32)

    scratch = {}
    for tag, lv in (("f0_", FINE), ("f1_", MID)):
        for k in FIELDS:
            scratch[tag + k] = field(lv)
    for k in ("k", "cx", "cyu", "cyd", "czr", "czl", "inv", "diag"):
        scratch["f2_" + k] = field(COARSE)
    scratch["basis"] = field(COARSE, 5)
    scratch["edge"] = field(FINE)
    for k in ("a", "b", "e"):
        scratch["mid_" + k] = field(MID, 5)
        scratch["fine_" + k] = field(FINE, 5)
    scratch["pack"] = pltpu.VMEM((2, 8, 8, LANES), F32)
    scratch["got"] = pltpu.VMEM((2, 16, 8, LANES), F32)
    scratch["mix0"] = pltpu.VMEM((4, 32, LANES), F32)
    scratch["mix1"] = pltpu.VMEM((2, 16, LANES), F32)
    for k in ("k1p", "s1p"):
        scratch[k] = pltpu.VMEM((10, 32, LANES), F32)
    for k in ("k2p", "z2p"):
        scratch[k] = pltpu.VMEM((7, 24, LANES), F32)
    scratch["mine"] = pltpu.VMEM((2, 1, LANES), F32)
    scratch["all1"] = pltpu.VMEM((4 * narrow, 1, LANES), F32)
    scratch["all2"] = pltpu.VMEM((wide // 4, 1, LANES), F32)
    messages = 10 + len(HALO_FINE) + 2 * len(NEAR_MID + FAR_MID + NEAR_COARSE + FAR_COARSE)
    scratch["send_sem"] = pltpu.SemaphoreType.DMA((messages,))
    scratch["recv_sem"] = pltpu.SemaphoreType.DMA((messages,))
    scratch["sum_send"] = pltpu.SemaphoreType.DMA((4 * narrow + wide // 4,))
    scratch["sum_recv"] = pltpu.SemaphoreType.DMA((4 * narrow + wide // 4,))
    scratch["local_sem"] = pltpu.SemaphoreType.DMA((2,))
    for i in range(3):
        scratch[f"token{i}"] = pltpu.SemaphoreType.REGULAR

    def body(heat, cond):
        return pl.pallas_call(
            functools.partial(kernel, wide, narrow, tuple(scratch)),
            out_shape=jax.ShapeDtypeStruct((8, 32, LANES), F32),
            in_specs=[pl.BlockSpec(memory_space=pltpu.HBM)] * 2,
            out_specs=pl.BlockSpec(memory_space=pltpu.VMEM),
            scratch_shapes=list(scratch.values()),
            compiler_params=pltpu.CompilerParams(
                collective_id=0, has_side_effects=True, vmem_limit_bytes=60 * 2**20
            ),
            cost_estimate=pl.CostEstimate(flops=50_000_000, bytes_accessed=400_000, transcendentals=0),
            name="vcycle",
        )(heat, cond)

    spec = P("wide", "narrow", None)
    return jax.shard_map(body, mesh=mesh, in_specs=(spec, spec), out_specs=spec, check_vma=False)
```

```python
import functools
import jax
import jax.numpy as jnp
from jax import lax
from jax.experimental import pallas as pl
from jax.experimental.pallas import tpu as pltpu
from jax.sharding import PartitionSpec as P

MASS = 0.002
LOW, HIGH = 0.25, 2.0
THETA = 0.5 * (HIGH + LOW)
DELTA = 0.5 * (HIGH - LOW)
SIGMA = THETA / DELTA
RHO1 = 1.0 / SIGMA
RHO2 = 1.0 / (2.0 * SIGMA - RHO1)
RHO3 = 1.0 / (2.0 * SIGMA - RHO2)
KEEP1, GAIN1 = RHO2 * RHO1, 2.0 * RHO2 / DELTA
KEEP2, GAIN2 = RHO3 * RHO2, 2.0 * RHO3 / DELTA
F32 = jnp.float32
LANES = 128
MESH = pl.DeviceIdType.MESH


class Level:
    def __init__(self, planes, first, own, rows, own_rows, repeat, scale):
        self.planes, self.first, self.own = planes, first, own
        self.rows, self.own_rows, self.repeat, self.scale = rows, own_rows, repeat, scale


FINE = Level(16, 4, 8, 48, 32, 1, 1.0)
MID = Level(20, 8, 4, 32, 16, 2, 0.25)
COARSE = Level(14, 6, 2, 24, 8, 4, 1.0 / 16.0)

FIELDS = ("k", "cx", "cyu", "cyd", "czr", "czl", "inv", "diag", "src", "hat", "upd", "it", "tmp", "res")


def planes(lo, hi, fn, unroll=2):
    count = hi - lo
    while count % unroll:
        unroll -= 1
    if unroll == count:
        for p in range(lo, hi):
            fn(p)
        return

    def step(i, carry):
        for k in range(unroll):
            fn(lo + i * unroll + k)
        return carry

    lax.fori_loop(0, count // unroll, step, 0)


def roll_rows(x, by):
    return pltpu.roll(x, by % x.shape[0], 0)


def roll_lanes(x, by):
    return pltpu.roll(x, by % LANES, 1)


def lane_of(rows):
    return lax.broadcasted_iota(jnp.int32, (rows, LANES), 1)


def row_of(rows):
    return lax.broadcasted_iota(jnp.int32, (rows, LANES), 0)


def near_sum(lv, f, ref, p, centers):
    cxu, cxd = f["cx"][p], f["cx"][p - 1]
    cyu, cyd, czr, czl = f["cyu"][p], f["cyd"][p], f["czr"][p], f["czl"][p]
    sums = []
    for v, c in enumerate(centers):
        at = ref.at[v] if len(ref.shape) == 4 else ref
        sums.append(
            cxu * at[p + 1]
            + cxd * at[p - 1]
            + cyu * roll_rows(c, -1)
            + cyd * roll_rows(c, 1)
            + czr * roll_lanes(c, -lv.repeat)
            + czl * roll_lanes(c, lv.repeat)
        )
    return sums


def inside_rows(lv, n, narrow):
    rows = row_of(lv.rows) + (n * lv.own_rows - 8)
    return (rows >= 0) & (rows < lv.own_rows * narrow)


def inside(lv, in_rows, p, w, wide):
    at = w * lv.own + p - lv.first
    return in_rows & (at >= 0) & (at < lv.own * wide)


def pack2(lv, x, y):
    return jnp.where(lax.rem(lane_of(x.shape[0]) // (lv.repeat // 2), 2) == 0, x, y)


def unpack2(lv, xy):
    half = lv.repeat // 2
    first = lax.rem(lane_of(xy.shape[0]) // half, 2) == 0
    return jnp.where(first, xy, roll_lanes(xy, half)), jnp.where(first, roll_lanes(xy, -half), xy)


def coefficients(lv, f, in_rows, w, wide, lo, hi, unroll=2):
    lane = lane_of(lv.rows)
    last = lane >= LANES - lv.repeat
    edge = last | (lane < lv.repeat)
    f["cx"][lo - 1] = 0.5 * (f["k"][lo - 1] + f["k"][lo])

    def one(p):
        k = f["k"][p]
        cxu = 0.5 * (k + f["k"][p + 1])
        cxd = 0.5 * (k + f["k"][p - 1])
        cyu = 0.5 * (k + roll_rows(k, -1))
        cyd = roll_rows(cyu, 1)
        czr = jnp.where(last, 0.0, 0.5 * (k + roll_lanes(k, -lv.repeat)))
        czl = roll_lanes(czr, lv.repeat)
        d = MASS + (cxu + cxd + cyu + cyd + czr + czl + jnp.where(edge, 0.5 * k, 0.0))
        f["cx"][p] = cxu
        f["cyu"][p] = cyu
        f["cyd"][p] = cyd
        f["czr"][p] = czr
        f["czl"][p] = czl
        f["diag"][p] = d
        f["inv"][p] = jnp.where(inside(lv, in_rows, p, w, wide), 1.0 / d, 0.0)

    planes(lo, hi, one, unroll)


def restrict(lv, read, mix):
    for j in range(lv.own // 2):
        mix[j] = read(2 * j) + read(2 * j + 1)
    half = lv.own_rows // 2
    even = lax.rem(lane_of(half) // lv.repeat, 2) == 0
    found = []
    for j in range(lv.own // 2):
        x = mix[j, pl.ds(0, half, stride=2), :] + mix[j, pl.ds(1, half, stride=2), :]
        x = x + jnp.where(even, roll_lanes(x, -lv.repeat), roll_lanes(x, lv.repeat))
        found.append(0.125 * x)
    return found


def smooth_down(lv, f, steps, unroll=2):
    def first(p):
        hat = f["src"][p] * f["inv"][p]
        f["hat"][p] = hat
        f["upd"][p] = hat * (1.0 / THETA)

    def second(p):
        x = f["upd"][p]
        (s,) = near_sum(lv, f, f["upd"], p, [x])
        z = f["hat"][p] + f["inv"][p] * s - x
        f["tmp"][p] = x + (KEEP1 * x + GAIN1 * z)

    def third(p):
        x = f["tmp"][p]
        (s,) = near_sum(lv, f, f["tmp"], p, [x])
        z = f["hat"][p] + f["inv"][p] * s - x
        f["it"][p] = x + (KEEP2 * (x - f["upd"][p]) + GAIN2 * z)

    for step, ranges in zip((first, second, third), steps):
        for lo, hi in ranges:
            planes(lo, hi, step, unroll)


def sweep_up(f, lv, old, new, e, lo, hi, keep, gain, own=None):
    count = old.shape[0]

    def one(p):
        centers = [old[v, p] for v in range(count)]
        sums = near_sum(lv, f, old, p, centers)
        inv = f["inv"][p]
        for v in range(count):
            z = inv * sums[v] - centers[v]
            if v == 0:
                z = z + f["hat"][p]
            u = gain * z if keep is None else keep * e[v, p] + gain * z
            if own is None:
                e[v, p] = u
                new[v, p] = centers[v] + u
            else:
                new[v, p, own] = (centers[v] + u)[own]

    planes(lo, hi, one, 1)


def solve4(m):
    small = m[1] < 0.5 * m[0]
    pick = lambda a, b: jnp.where(small, a, b)
    g = [pick(m[k + 1], m[8 + k] - m[9 + k]) for k in range(7)]
    rhs = [pick(m[k], m[8 + k]) for k in range(4)]
    rows = [[g[i + j] for j in range(4)] for i in range(4)]
    inv = []
    for i in range(4):
        piv = rows[i][i]
        good = piv > 1e-7 * g[2 * i]
        inv.append(jnp.where(good, 1.0 / jnp.where(good, piv, 1.0), 0.0))
        for r in range(i + 1, 4):
            factor = rows[i][r] * inv[i]
            rows[r] = [rows[r][j] - factor * rows[i][j] if j >= r else None for j in range(4)]
            rhs[r] = rhs[r] - factor * rhs[i]
    y = [None] * 4
    for i in (3, 2, 1, 0):
        t = rhs[i]
        for j in range(i + 1, 4):
            t = t - rows[i][j] * y[j]
        y[i] = t * inv[i]
    turned = [
        y[0] + y[1] + y[2] + y[3],
        -(y[1] + 2.0 * y[2] + 3.0 * y[3]),
        y[2] + 3.0 * y[3],
        -y[3],
    ]
    return [pick(a, b) for a, b in zip(y, turned)]


def halo(reach):
    return [(dw, dn) for dw in reach for dn in (1, -1, 0) if (dw, dn) != (0, 0)]


NEAR_MID, FAR_MID = halo((1, -1, 0)), halo((2, -2))
NEAR_COARSE, FAR_COARSE = halo((1, -1, 0, 2, -2)), halo((3, -3))
HALO_FINE = halo((1, -1, 0))


def kernel(wide, narrow, names, heat, cond, out, *refs):
    s = dict(zip(names, refs))
    w, n = lax.axis_index("wide"), lax.axis_index("narrow")
    z, ylo, core = w // 4, lax.rem(w // 2, 2), lax.rem(w, 2)
    yhi, x = n // 4, lax.rem(n, 4)
    stacks = wide // 4

    f0 = {k: s["f0_" + k] for k in FIELDS}
    f1 = {k: s["f1_" + k] for k in FIELDS}
    f2 = {k: s["f2_" + k] for k in FIELDS if "f2_" + k in s}

    def near(dw, dn):
        return (lax.rem(w + (dw + wide), wide), lax.rem(n + (dn + narrow), narrow))

    def stack(dz):
        return (lax.rem(w + (4 * dz + wide), wide), n)

    def plane_peer(dx, dhi, dlo, dc):
        to = z * 4 + lax.rem(ylo + dlo, 2) * 2 + lax.rem(core + dc, 2)
        return (to, lax.rem(yhi + dhi, 2) * 4 + lax.rem(x + dx, 4))

    plane_peers = [
        plane_peer(*d)
        for d in sorted(
            [(dx, dhi, dlo, dc) for dx in range(4) for dhi in range(2) for dlo in range(2) for dc in range(2)],
            key=lambda d: -min(d[0], 4 - d[0]) - (1 if d[2] else 2 * d[1]),
        )
        if any(d)
    ]
    stack_peers = [stack(d) for d in sorted(range(1, stacks), key=lambda d: -min(d, stacks - d))]

    barrier = pltpu.get_barrier_semaphore()
    greeted = [(1, 1), (1, -1), (-1, 1), (-1, -1), (0, 1), (0, -1), (1, 0), (-1, 0), (4, 0), (-4, 0)]
    for d in greeted:
        pl.semaphore_signal(barrier, inc=1, device_id=near(*d), device_id_type=MESH)
    own_heat = pltpu.make_async_copy(heat, f0["src"].at[4:12, 8:40], s["local_sem"].at[0])
    own_cond = pltpu.make_async_copy(cond, f0["k"].at[4:12, 8:40], s["local_sem"].at[1])
    own_cond.start()
    own_heat.start()

    used = [0]
    sent = []

    def send(src, dst, peer):
        i = used[0]
        used[0] += 1
        copy = pltpu.make_async_remote_copy(
            src_ref=src,
            dst_ref=dst,
            send_sem=s["send_sem"].at[i],
            recv_sem=s["recv_sem"].at[i],
            device_id=peer,
            device_id_type=MESH,
        )
        copy.start()
        sent.append(copy)
        return copy

    def send_rows(ref_from, ref_to, first, own, own_rows, reach, depth):
        copies = []
        for dw, dn in reach:
            a, c, b = first, own, first - dw * own
            if depth < own and dw:
                a, b = (first + own - depth, first - depth) if dw > 0 else (first, first + own)
                c = depth
            ra, rc, rb = (8, own_rows, 8) if dn == 0 else (own_rows, 8, 0) if dn > 0 else (8, 8, 8 + own_rows)
            copies.append(
                send(ref_from.at[a : a + c, ra : ra + rc], ref_to.at[b : b + c, rb : rb + rc], near(dw, dn))
            )
        return copies

    def send_mid(ref, reach):
        return send_rows(ref, ref, 4, 2, 16, reach, 2)

    def send_coarse(ref, reach):
        return send_rows(ref, ref, 3, 1, 8, reach, 1)

    def arrive(copies):
        for c in copies:
            c.wait_recv()

    tokens = [s["token0"], s["token1"], s["token2"]]

    def pass_token(i):
        for way in (1, -1):
            pl.semaphore_signal(tokens[i], inc=1, device_id=stack(way * 2**i), device_id_type=MESH)

    def take_token(i):
        pl.semaphore_wait(tokens[i], 2)

    own_cond.wait()
    own_heat.wait()
    low4 = row_of(8) < 4
    pack, got = s["pack"], s["got"]

    def pack_plane(p):
        h, c = f0["src"][p + 4, 32:40], f0["k"][p + 4, 32:40]
        pack[0, p] = jnp.where(low4, roll_rows(h, 4), c)
        h, c = f0["src"][p + 4, 8:16], f0["k"][p + 4, 8:16]
        pack[1, p] = jnp.where(low4, c, roll_rows(h, 4))

    planes(0, 8, pack_plane, 8)
    pl.semaphore_wait(barrier, len(greeted))
    first = [
        send(pack.at[0, 4:8], got.at[0, 0:4], near(1, 1)),
        send(pack.at[1, 4:8], got.at[1, 0:4], near(1, -1)),
        send(pack.at[0, 0:4], got.at[0, 12:16], near(-1, 1)),
        send(pack.at[1, 0:4], got.at[1, 12:16], near(-1, -1)),
        send(cond.at[4:8], f0["k"].at[0:4, 8:40], near(1, 0)),
        send(cond.at[0:4], f0["k"].at[12:16, 8:40], near(-1, 0)),
        send(pack.at[0], got.at[0, 4:12], near(0, 1)),
        send(pack.at[1], got.at[1, 4:12], near(0, -1)),
        send(heat.at[5:8], f0["src"].at[1:4, 8:40], near(1, 0)),
        send(heat.at[0:3], f0["src"].at[12:15, 8:40], near(-1, 0)),
    ]

    k1p, k2p, s1p, z2p = s["k1p"], s["k2p"], s["s1p"], s["z2p"]
    one_up = restrict(FINE, lambda p: f0["k"][4 + p, 8:40], s["mix0"])
    two_up = restrict(MID, lambda p: one_up[p], s["mix1"])
    for j in range(2):
        k1p[4 + j, 8:24] = pack2(MID, one_up[2 * j], one_up[2 * j + 1])
    k2p[3, 8:16] = pack2(COARSE, two_up[0], two_up[1])

    in0, in1, in2 = (inside_rows(lv, n, narrow) for lv in (FINE, MID, COARSE))

    def unpack_cond(lv, packed, f, in_rows, p):
        for k, v in enumerate(unpack2(lv, packed[p])):
            ok = inside(lv, in_rows, 2 * p + k, w, wide)
            f["k"][2 * p + k] = jnp.where(ok, v * lv.scale, 0.0)

    arrive(first)
    pass_token(0)
    cond1 = send_mid(k1p, NEAR_MID)

    def unpack(p):
        ok = inside(FINE, in0, p, w, wide)
        lo, hi = f0["k"].at[p, 0:8], f0["k"].at[p, 40:48]
        lo[...] = jnp.where(low4, 0.0, got[0, p])
        hi[...] = jnp.where(low4, got[1, p], 0.0)
        f0["src"][p, 0:8] = roll_rows(got[0, p], 4)
        f0["src"][p, 40:48] = roll_rows(got[1, p], 4)
        f0["k"][p] = jnp.where(ok, f0["k"][p], 0.0)

    planes(0, 16, unpack, 4)
    coefficients(FINE, f0, in0, w, wide, 1, 15)
    smooth_down(FINE, f0, ([(1, 15)], [(2, 14)], [(3, 13)]))

    def residual(lv, f, unroll):
        own = slice(8, 8 + lv.own_rows)

        def one(p):
            x = f["it"][p]
            (t,) = near_sum(lv, f, f["it"], p, [x])
            f["res"][p, own] = (f["src"][p] + t - f["diag"][p] * x)[own]

        planes(lv.first, lv.first + lv.own, one, unroll)

    residual(FINE, f0, 2)
    r1 = restrict(FINE, lambda p: f0["res"][4 + p, 8:40], s["mix0"])
    for j in range(2):
        s1p[4 + j, 8:24] = pack2(MID, r1[2 * j], r1[2 * j + 1])
    src1 = send_mid(s1p, NEAR_MID)
    cond2 = send_coarse(k2p, NEAR_COARSE)
    its = send_rows(f0["it"], s["edge"], 4, 8, 32, HALO_FINE, 3)
    cond1_far = send_mid(k1p, FAR_MID)
    arrive(cond1)
    for p in range(2, 8):
        unpack_cond(MID, k1p, f1, in1, p)
    coefficients(MID, f1, in1, w, wide, 5, 15, 10)
    arrive(src1)
    take_token(0)
    pass_token(1)

    def unpack_src(p):
        f1["src"][2 * p], f1["src"][2 * p + 1] = unpack2(MID, s1p[p])

    for p in range(2, 8):
        unpack_src(p)
    smooth_down(MID, f1, ([(5, 15)], [(6, 14)], [(7, 13)]), 10)
    residual(MID, f1, 4)
    r2 = restrict(MID, lambda p: f1["res"][8 + p, 8:24], s["mix1"])
    arrive(cond2)
    for p in range(1, 6):
        unpack_cond(COARSE, k2p, f2, in2, p)
    coefficients(COARSE, f2, in2, w, wide, 3, 11, 8)
    z2p[3, 8:16] = pack2(COARSE, r2[0] * f2["inv"][6, 8:16], r2[1] * f2["inv"][7, 8:16])
    z2 = send_coarse(z2p, NEAR_COARSE)
    z2_far = send_coarse(z2p, FAR_COARSE)
    cond2_far = send_coarse(k2p, FAR_COARSE)
    src1_far = send_mid(s1p, FAR_MID)
    arrive(z2)
    take_token(1)
    pass_token(2)
    u = s["basis"]

    def unpack_z(p):
        for k, v in enumerate(unpack2(COARSE, z2p[p])):
            u[0, 2 * p + k] = jnp.where(inside(COARSE, in2, 2 * p + k, w, wide), v, 0.0)

    def apply_b(k, p):
        v = u[k, p]
        (t,) = near_sum(COARSE, f2, u.at[k], p, [v])
        u[k + 1, p] = v - f2["inv"][p] * t

    for p in range(1, 6):
        unpack_z(p)
    for k in range(4):
        for p in range(3 + k, 11 - k):
            apply_b(k, p)

    row8, lane8 = row_of(8), lane_of(8)
    sums = [jnp.zeros((8, LANES), F32) for _ in range(16)]
    for p in (6, 7):
        d = f2["diag"][p, 8:16]
        b = [u[k, p, 8:16] for k in range(5)]
        c = [
            b[0],
            b[0] - b[1],
            b[0] - 2.0 * b[1] + b[2],
            b[0] - 3.0 * (b[1] - b[2]) - b[3],
            b[0] - 4.0 * (b[1] + b[3]) + 6.0 * b[2] + b[4],
        ]
        for at, vs in ((0, b), (8, c)):
            for k in range(8):
                sums[at + k] = sums[at + k] + vs[k // 2] * d * vs[(k + 1) // 2]
    tiles = []
    for half in (0, 8):
        m = jnp.zeros((8, LANES), F32)
        for k in range(8):
            m = jnp.where(row8 == k, jnp.sum(sums[half + k], axis=0, keepdims=True), m)
        tiles.append(jnp.sum(m, axis=1, keepdims=True))
    spread = jnp.where(lane8 == row8, tiles[0], 0.0) + jnp.where(lane8 == row8 + 8, tiles[1], 0.0)
    mine, all1, all2 = s["mine"], s["all1"], s["all2"]
    mine[0] = jnp.sum(spread, axis=0, keepdims=True)
    rank = lax.rem(w, 4) * narrow + n
    all1[rank] = mine[0]

    def send_sum(src, dst, peers, at):
        copies = []
        for i, peer in enumerate(peers):
            copy = pltpu.make_async_remote_copy(
                src_ref=src,
                dst_ref=dst,
                send_sem=s["sum_send"].at[at + i],
                recv_sem=s["sum_recv"].at[at + i],
                device_id=peer,
                device_id_type=MESH,
            )
            copy.start()
            copies.append(copy)
        return copies

    sums1 = send_sum(mine.at[0], all1.at[rank], plane_peers, 0)

    arrive(cond2_far + z2_far)
    for p in (0, 6):
        unpack_cond(COARSE, k2p, f2, in2, p)
        unpack_z(p)
    coefficients(COARSE, f2, in2, w, wide, 1, 3)
    coefficients(COARSE, f2, in2, w, wide, 11, 13)
    for k in range(3):
        for p in (1 + k, 2 + k, 11 - k, 12 - k):
            apply_b(k, p)
    arrive(cond1_far + src1_far)
    for p in (0, 1, 8, 9):
        unpack_cond(MID, k1p, f1, in1, p)
        unpack_src(p)
    coefficients(MID, f1, in1, w, wide, 1, 5, 4)
    coefficients(MID, f1, in1, w, wide, 15, 19, 4)
    smooth_down(
        MID, f1, ([(1, 5), (15, 19)], [(2, 6), (14, 18)], [(3, 7), (13, 17)]), 4
    )

    xa, xb, xe = s["mid_a"], s["mid_b"], s["mid_e"]

    def start_mid(p):
        xa[0, p] = f1["it"][p]
        for k in range(4):
            t = u[k, p // 2 + 2, 4:20]
            xa[1 + k, p, pl.ds(0, 16, stride=2), :] = t
            xa[1 + k, p, pl.ds(1, 16, stride=2), :] = t

    planes(3, 17, start_mid)
    sweep_up(f1, MID, xa, xb, xe, 4, 16, None, 1.0 / THETA)
    arrive(sums1)
    mine[1] = jnp.sum(all1[...], axis=0)
    all2[z] = mine[1]
    take_token(2)
    sums2 = send_sum(mine.at[1], all2.at[z], stack_peers, len(plane_peers))

    sweep_up(f1, MID, xb, xa, xe, 5, 15, KEEP1, GAIN1)
    sweep_up(f1, MID, xa, xb, xe, 6, 14, KEEP2, GAIN2)
    arrive(its)
    ya, yb, ye = s["fine_a"], s["fine_b"], s["fine_e"]
    edge = s["edge"]

    def own_edge(p):
        edge[p, 8:40] = f0["it"][p, 8:40]

    planes(4, 12, own_edge)

    def start_fine(p):
        for k in range(5):
            t = xb[k, p // 2 + 6, 4:28]
            ya[k, p, pl.ds(0, 24, stride=2), :] = t
            ya[k, p, pl.ds(1, 24, stride=2), :] = t
        ya[0, p] = ya[0, p] + jnp.where(f0["inv"][p] > 0.0, edge[p], 0.0)

    planes(1, 15, start_fine)
    sweep_up(f0, FINE, ya, yb, ye, 2, 14, None, 1.0 / THETA)
    sweep_up(f0, FINE, yb, ya, ye, 3, 13, KEEP1, GAIN1)
    sweep_up(f0, FINE, ya, yb, ye, 4, 12, KEEP2, GAIN2, slice(8, 40))
    for c in sent + sums1:
        c.wait_send()
    arrive(sums2)
    total = jnp.broadcast_to(jnp.sum(all2[...], axis=0), (8, LANES))
    ta = jnp.sum(jnp.where(lane8 == row8, total, 0.0), axis=1, keepdims=True)
    tb = jnp.sum(jnp.where(lane8 == row8 + 8, total, 0.0), axis=1, keepdims=True)
    ta, tb = jnp.broadcast_to(ta, (8, LANES)), jnp.broadcast_to(tb, (8, LANES))
    y = solve4([ta[k : k + 1] for k in range(8)] + [tb[k : k + 1] for k in range(8)])

    def combine(p):
        v = yb[0, p + 4, 8:40]
        for k in range(4):
            v = v + y[k] * yb[1 + k, p + 4, 8:40]
        out[p] = v

    planes(0, 8, combine, 4)
    for c in sums2:
        c.wait_send()


def solution(mesh):
    wide, narrow = mesh.shape["wide"], mesh.shape["narrow"]

    def field(lv, *lead):
        return pltpu.VMEM((*lead, lv.planes, lv.rows, LANES), F32)

    scratch = {}
    for tag, lv in (("f0_", FINE), ("f1_", MID)):
        for k in FIELDS:
            scratch[tag + k] = field(lv)
    for k in ("k", "cx", "cyu", "cyd", "czr", "czl", "inv", "diag"):
        scratch["f2_" + k] = field(COARSE)
    scratch["basis"] = field(COARSE, 5)
    scratch["edge"] = field(FINE)
    for k in ("a", "b", "e"):
        scratch["mid_" + k] = field(MID, 5)
        scratch["fine_" + k] = field(FINE, 5)
    scratch["pack"] = pltpu.VMEM((2, 8, 8, LANES), F32)
    scratch["got"] = pltpu.VMEM((2, 16, 8, LANES), F32)
    scratch["mix0"] = pltpu.VMEM((4, 32, LANES), F32)
    scratch["mix1"] = pltpu.VMEM((2, 16, LANES), F32)
    for k in ("k1p", "s1p"):
        scratch[k] = pltpu.VMEM((10, 32, LANES), F32)
    for k in ("k2p", "z2p"):
        scratch[k] = pltpu.VMEM((7, 24, LANES), F32)
    scratch["mine"] = pltpu.VMEM((2, 1, LANES), F32)
    scratch["all1"] = pltpu.VMEM((4 * narrow, 1, LANES), F32)
    scratch["all2"] = pltpu.VMEM((wide // 4, 1, LANES), F32)
    messages = 10 + len(HALO_FINE) + 2 * len(NEAR_MID + FAR_MID + NEAR_COARSE + FAR_COARSE)
    scratch["send_sem"] = pltpu.SemaphoreType.DMA((messages,))
    scratch["recv_sem"] = pltpu.SemaphoreType.DMA((messages,))
    scratch["sum_send"] = pltpu.SemaphoreType.DMA((4 * narrow + wide // 4,))
    scratch["sum_recv"] = pltpu.SemaphoreType.DMA((4 * narrow + wide // 4,))
    scratch["local_sem"] = pltpu.SemaphoreType.DMA((2,))
    for i in range(3):
        scratch[f"token{i}"] = pltpu.SemaphoreType.REGULAR

    def body(heat, cond):
        heat = pltpu.with_memory_space_constraint(heat, pltpu.HBM)
        cond = pltpu.with_memory_space_constraint(cond, pltpu.HBM)
        return pl.pallas_call(
            functools.partial(kernel, wide, narrow, tuple(scratch)),
            out_shape=pltpu.VMEM((8, 32, LANES), F32),
            in_specs=[pl.BlockSpec(memory_space=pltpu.HBM)] * 2,
            out_specs=pl.BlockSpec(memory_space=pltpu.VMEM),
            scratch_shapes=list(scratch.values()),
            compiler_params=pltpu.CompilerParams(
                collective_id=0, has_side_effects=True, vmem_limit_bytes=40 * 2**20
            ),
            cost_estimate=pl.CostEstimate(flops=50_000_000, bytes_accessed=400_000, transcendentals=0),
            name="vcycle",
        )(heat, cond)

    spec = P("wide", "narrow", None)
    return jax.shard_map(body, mesh=mesh, in_specs=(spec, spec), out_specs=spec, check_vma=False)
```

```python
import functools
import jax
import jax.numpy as jnp
from jax import lax
from jax.experimental import pallas as pl
from jax.experimental.pallas import tpu as pltpu
from jax.sharding import PartitionSpec as P

MASS = 0.002
LOW, HIGH = 0.25, 2.0
THETA = 0.5 * (HIGH + LOW)
DELTA = 0.5 * (HIGH - LOW)
SIGMA = THETA / DELTA
RHO1 = 1.0 / SIGMA
RHO2 = 1.0 / (2.0 * SIGMA - RHO1)
RHO3 = 1.0 / (2.0 * SIGMA - RHO2)
KEEP1, GAIN1 = RHO2 * RHO1, 2.0 * RHO2 / DELTA
KEEP2, GAIN2 = RHO3 * RHO2, 2.0 * RHO3 / DELTA
F32 = jnp.float32
LANES = 128
MESH = pl.DeviceIdType.MESH


class Level:
    def __init__(self, planes, first, own, rows, own_rows, repeat, scale):
        self.planes, self.first, self.own = planes, first, own
        self.rows, self.own_rows, self.repeat, self.scale = rows, own_rows, repeat, scale


FINE = Level(16, 4, 8, 48, 32, 1, 1.0)
MID = Level(20, 8, 4, 32, 16, 2, 0.25)
COARSE = Level(14, 6, 2, 24, 8, 4, 1.0 / 16.0)

FIELDS = ("k", "cx", "cyu", "cyd", "czr", "czl", "inv", "diag", "src", "hat", "upd", "it", "tmp", "res")


def planes(lo, hi, fn, unroll=99):
    count = hi - lo
    unroll = min(unroll, count)
    while count % unroll:
        unroll -= 1
    if unroll == count:
        for p in range(lo, hi):
            fn(p)
        return

    def step(i, carry):
        for k in range(unroll):
            fn(lo + i * unroll + k)
        return carry

    lax.fori_loop(0, count // unroll, step, 0)


def roll_rows(x, by):
    return pltpu.roll(x, by % x.shape[0], 0)


def roll_lanes(x, by):
    return pltpu.roll(x, by % LANES, 1)


def lane_of(rows):
    return lax.broadcasted_iota(jnp.int32, (rows, LANES), 1)


def row_of(rows):
    return lax.broadcasted_iota(jnp.int32, (rows, LANES), 0)


def near_sum(lv, f, ref, p, centers):
    cxu, cxd = f["cx"][p], f["cx"][p - 1]
    cyu, cyd, czr, czl = f["cyu"][p], f["cyd"][p], f["czr"][p], f["czl"][p]
    sums = []
    for v, c in enumerate(centers):
        at = ref.at[v] if len(ref.shape) == 4 else ref
        sums.append(
            cxu * at[p + 1]
            + cxd * at[p - 1]
            + cyu * roll_rows(c, -1)
            + cyd * roll_rows(c, 1)
            + czr * roll_lanes(c, -lv.repeat)
            + czl * roll_lanes(c, lv.repeat)
        )
    return sums


def inside_rows(lv, n, narrow):
    rows = row_of(lv.rows) + (n * lv.own_rows - 8)
    return (rows >= 0) & (rows < lv.own_rows * narrow)


def inside(lv, in_rows, p, w, wide):
    if isinstance(p, int) and lv.first <= p < lv.first + lv.own:
        return in_rows
    at = w * lv.own + p - lv.first
    return in_rows & (at >= 0) & (at < lv.own * wide)


def pack2(lv, x, y):
    return jnp.where(lax.rem(lane_of(x.shape[0]) // (lv.repeat // 2), 2) == 0, x, y)


def unpack2(lv, xy):
    half = lv.repeat // 2
    first = lax.rem(lane_of(xy.shape[0]) // half, 2) == 0
    return jnp.where(first, xy, roll_lanes(xy, half)), jnp.where(first, roll_lanes(xy, -half), xy)


def coefficients(lv, f, in_rows, w, wide, lo, hi, unroll=99):
    lane = lane_of(lv.rows)
    last = lane >= LANES - lv.repeat
    edge = last | (lane < lv.repeat)
    f["cx"][lo - 1] = 0.5 * (f["k"][lo - 1] + f["k"][lo])

    def one(p):
        k = f["k"][p]
        cxu = 0.5 * (k + f["k"][p + 1])
        cxd = 0.5 * (k + f["k"][p - 1])
        cyu = 0.5 * (k + roll_rows(k, -1))
        cyd = roll_rows(cyu, 1)
        czr = jnp.where(last, 0.0, 0.5 * (k + roll_lanes(k, -lv.repeat)))
        czl = roll_lanes(czr, lv.repeat)
        d = MASS + (cxu + cxd + cyu + cyd + czr + czl + jnp.where(edge, 0.5 * k, 0.0))
        f["cx"][p] = cxu
        f["cyu"][p] = cyu
        f["cyd"][p] = cyd
        f["czr"][p] = czr
        f["czl"][p] = czl
        f["diag"][p] = d
        f["inv"][p] = jnp.where(inside(lv, in_rows, p, w, wide), 1.0 / d, 0.0)

    planes(lo, hi, one, unroll)


def restrict(lv, read, mix):
    for j in range(lv.own // 2):
        mix[j] = read(2 * j) + read(2 * j + 1)
    half = lv.own_rows // 2
    even = lax.rem(lane_of(half) // lv.repeat, 2) == 0
    found = []
    for j in range(lv.own // 2):
        x = mix[j, pl.ds(0, half, stride=2), :] + mix[j, pl.ds(1, half, stride=2), :]
        x = x + jnp.where(even, roll_lanes(x, -lv.repeat), roll_lanes(x, lv.repeat))
        found.append(0.125 * x)
    return found


def smooth_down(lv, f, steps, unroll=99):
    def first(p):
        hat = f["src"][p] * f["inv"][p]
        f["hat"][p] = hat
        f["upd"][p] = hat * (1.0 / THETA)

    def second(p):
        x = f["upd"][p]
        (s,) = near_sum(lv, f, f["upd"], p, [x])
        z = f["hat"][p] + f["inv"][p] * s - x
        f["tmp"][p] = x + (KEEP1 * x + GAIN1 * z)

    def third(p):
        x = f["tmp"][p]
        (s,) = near_sum(lv, f, f["tmp"], p, [x])
        z = f["hat"][p] + f["inv"][p] * s - x
        f["it"][p] = x + (KEEP2 * (x - f["upd"][p]) + GAIN2 * z)

    for step, ranges in zip((first, second, third), steps):
        for lo, hi in ranges:
            planes(lo, hi, step, unroll)


def sweep_up(f, lv, old, new, e, lo, hi, keep, gain, own=None, unroll=2):
    count = old.shape[0]

    def one(p):
        centers = [old[v, p] for v in range(count)]
        sums = near_sum(lv, f, old, p, centers)
        inv = f["inv"][p]
        for v in range(count):
            z = inv * sums[v] - centers[v]
            if v == 0:
                z = z + f["hat"][p]
            u = gain * z if keep is None else keep * e[v, p] + gain * z
            if own is None:
                e[v, p] = u
                new[v, p] = centers[v] + u
            else:
                new[v, p, own] = (centers[v] + u)[own]

    planes(lo, hi, one, unroll)


def solve4(m):
    small = m[1] < 0.5 * m[0]
    pick = lambda a, b: jnp.where(small, a, b)
    g = [pick(m[k + 1], m[8 + k] - m[9 + k]) for k in range(7)]
    rhs = [pick(m[k], m[8 + k]) for k in range(4)]
    rows = [[g[i + j] for j in range(4)] for i in range(4)]
    inv = []
    for i in range(4):
        piv = rows[i][i]
        good = piv > 1e-7 * g[2 * i]
        inv.append(jnp.where(good, 1.0 / jnp.where(good, piv, 1.0), 0.0))
        for r in range(i + 1, 4):
            factor = rows[i][r] * inv[i]
            rows[r] = [rows[r][j] - factor * rows[i][j] if j >= r else None for j in range(4)]
            rhs[r] = rhs[r] - factor * rhs[i]
    y = [None] * 4
    for i in (3, 2, 1, 0):
        t = rhs[i]
        for j in range(i + 1, 4):
            t = t - rows[i][j] * y[j]
        y[i] = t * inv[i]
    turned = [
        y[0] + y[1] + y[2] + y[3],
        -(y[1] + 2.0 * y[2] + 3.0 * y[3]),
        y[2] + 3.0 * y[3],
        -y[3],
    ]
    return [pick(a, b) for a, b in zip(y, turned)]


def halo(reach):
    return [(dw, dn) for dn in (1, -1, 0) for dw in reach if (dw, dn) != (0, 0)]


NEAR_MID, FAR_MID = halo((1, -1, 0)), halo((2, -2))
NEAR_COARSE, FAR_COARSE = halo((1, -1, 0, 2, -2)), halo((3, -3))
HALO_FINE = halo((1, -1, 0))


def kernel(wide, narrow, names, heat, cond, out, *refs):
    s = dict(zip(names, refs))
    w, n = lax.axis_index("wide"), lax.axis_index("narrow")
    z, ylo, core = w // 4, lax.rem(w // 2, 2), lax.rem(w, 2)
    yhi, x = n // 4, lax.rem(n, 4)
    stacks = wide // 4

    f0 = {k: s["f0_" + k] for k in FIELDS}
    f1 = {k: s["f1_" + k] for k in FIELDS}
    f2 = {k: s["f2_" + k] for k in FIELDS if "f2_" + k in s}

    def near(dw, dn):
        return (lax.rem(w + (dw + wide), wide), lax.rem(n + (dn + narrow), narrow))

    def stack(dz):
        return (lax.rem(w + (4 * dz + wide), wide), n)

    def plane_peer(dx, dhi, dlo, dc):
        to = z * 4 + lax.rem(ylo + dlo, 2) * 2 + lax.rem(core + dc, 2)
        return (to, lax.rem(yhi + dhi, 2) * 4 + lax.rem(x + dx, 4))

    plane_peers = [
        plane_peer(*d)
        for d in sorted(
            [(dx, dhi, dlo, dc) for dx in range(4) for dhi in range(2) for dlo in range(2) for dc in range(2)],
            key=lambda d: -min(d[0], 4 - d[0]) - (1 if d[2] else 2 * d[1]),
        )
        if any(d)
    ]
    stack_peers = [stack(d) for d in sorted(range(1, stacks), key=lambda d: -min(d, stacks - d))]

    barrier = pltpu.get_barrier_semaphore()
    greeted = [(1, 1), (1, -1), (-1, 1), (-1, -1), (0, 1), (0, -1), (1, 0), (-1, 0), (4, 0), (-4, 0)]
    for d in greeted:
        pl.semaphore_signal(barrier, inc=1, device_id=near(*d), device_id_type=MESH)
    own_heat = pltpu.make_async_copy(heat, f0["src"].at[4:12, 8:40], s["local_sem"].at[0])
    own_cond = pltpu.make_async_copy(cond, f0["k"].at[4:12, 8:40], s["local_sem"].at[1])
    own_cond.start()
    own_heat.start()

    used = [0]
    sent = []

    def send(src, dst, peer):
        i = used[0]
        used[0] += 1
        copy = pltpu.make_async_remote_copy(
            src_ref=src,
            dst_ref=dst,
            send_sem=s["send_sem"].at[i],
            recv_sem=s["recv_sem"].at[i],
            device_id=peer,
            device_id_type=MESH,
        )
        copy.start()
        sent.append(copy)
        return copy

    def send_rows(ref_from, ref_to, first, own, own_rows, reach, depth):
        copies = []
        for dw, dn in reach:
            a, c, b = first, own, first - dw * own
            if depth < own and dw:
                a, b = (first + own - depth, first - depth) if dw > 0 else (first, first + own)
                c = depth
            ra, rc, rb = (8, own_rows, 8) if dn == 0 else (own_rows, 8, 0) if dn > 0 else (8, 8, 8 + own_rows)
            copies.append(
                send(ref_from.at[a : a + c, ra : ra + rc], ref_to.at[b : b + c, rb : rb + rc], near(dw, dn))
            )
        return copies

    def send_mid(ref, reach):
        return send_rows(ref, ref, 4, 2, 16, reach, 2)

    def send_coarse(ref, reach):
        return send_rows(ref, ref, 3, 1, 8, reach, 1)

    def arrive(copies):
        for c in copies:
            c.wait_recv()

    tokens = [s["token0"], s["token1"], s["token2"]]

    def pass_token(i):
        for way in (1, -1):
            pl.semaphore_signal(tokens[i], inc=1, device_id=stack(way * 2**i), device_id_type=MESH)

    def take_token(i):
        pl.semaphore_wait(tokens[i], 2)

    own_cond.wait()
    own_heat.wait()
    low4 = row_of(8) < 4
    pack, got = s["pack"], s["got"]

    def pack_plane(p):
        h, c = f0["src"][p + 4, 32:40], f0["k"][p + 4, 32:40]
        pack[0, p] = jnp.where(low4, roll_rows(h, 4), c)
        h, c = f0["src"][p + 4, 8:16], f0["k"][p + 4, 8:16]
        pack[1, p] = jnp.where(low4, c, roll_rows(h, 4))

    planes(0, 8, pack_plane, 8)
    pl.semaphore_wait(barrier, len(greeted))
    first = [
        send(pack.at[0, 4:8], got.at[0, 0:4], near(1, 1)),
        send(pack.at[1, 4:8], got.at[1, 0:4], near(1, -1)),
        send(pack.at[0, 0:4], got.at[0, 12:16], near(-1, 1)),
        send(pack.at[1, 0:4], got.at[1, 12:16], near(-1, -1)),
        send(cond.at[4:8], f0["k"].at[0:4, 8:40], near(1, 0)),
        send(cond.at[0:4], f0["k"].at[12:16, 8:40], near(-1, 0)),
        send(pack.at[0], got.at[0, 4:12], near(0, 1)),
        send(pack.at[1], got.at[1, 4:12], near(0, -1)),
        send(heat.at[5:8], f0["src"].at[1:4, 8:40], near(1, 0)),
        send(heat.at[0:3], f0["src"].at[12:15, 8:40], near(-1, 0)),
    ]

    k1p, k2p, s1p, z2p = s["k1p"], s["k2p"], s["s1p"], s["z2p"]
    one_up = restrict(FINE, lambda p: f0["k"][4 + p, 8:40], s["mix0"])
    two_up = restrict(MID, lambda p: one_up[p], s["mix1"])
    for j in range(2):
        k1p[4 + j, 8:24] = pack2(MID, one_up[2 * j], one_up[2 * j + 1])
    k2p[3, 8:16] = pack2(COARSE, two_up[0], two_up[1])

    in0, in1, in2 = (inside_rows(lv, n, narrow) for lv in (FINE, MID, COARSE))

    def unpack_cond(lv, packed, f, in_rows, p):
        for k, v in enumerate(unpack2(lv, packed[p])):
            ok = inside(lv, in_rows, 2 * p + k, w, wide)
            f["k"][2 * p + k] = jnp.where(ok, v * lv.scale, 0.0)

    arrive(first[:8])
    pass_token(0)
    cond1 = send_mid(k1p, NEAR_MID)

    in_low, in_high = in0[0:8] & ~low4, in0[40:48] & low4

    def unpack(p):
        f0["k"][p, 0:8] = jnp.where(in_low, got[0, p], 0.0)
        f0["k"][p, 40:48] = jnp.where(in_high, got[1, p], 0.0)
        f0["src"][p, 0:8] = roll_rows(got[0, p], 4)
        f0["src"][p, 40:48] = roll_rows(got[1, p], 4)
        if not 4 <= p < 12:
            at = w * 8 + p - 4
            f0["k"][p] = jnp.where((at >= 0) & (at < 8 * wide), f0["k"][p], 0.0)

    planes(0, 16, unpack)
    coefficients(FINE, f0, in0, w, wide, 1, 15)
    arrive(first[8:])
    smooth_down(FINE, f0, ([(1, 15)], [(2, 14)], [(3, 13)]))

    def residual(lv, f, unroll):
        own = slice(8, 8 + lv.own_rows)

        def one(p):
            x = f["it"][p]
            (t,) = near_sum(lv, f, f["it"], p, [x])
            f["res"][p, own] = (f["src"][p] + t - f["diag"][p] * x)[own]

        planes(lv.first, lv.first + lv.own, one, unroll)

    residual(FINE, f0, 8)
    r1 = restrict(FINE, lambda p: f0["res"][4 + p, 8:40], s["mix0"])
    for j in range(2):
        s1p[4 + j, 8:24] = pack2(MID, r1[2 * j], r1[2 * j + 1])
    src1 = send_mid(s1p, NEAR_MID)
    cond2 = send_coarse(k2p, NEAR_COARSE)
    its = send_rows(f0["it"], s["edge"], 4, 8, 32, HALO_FINE, 3)
    cond1_far = send_mid(k1p, FAR_MID)
    arrive(cond1)
    for p in range(2, 8):
        unpack_cond(MID, k1p, f1, in1, p)
    coefficients(MID, f1, in1, w, wide, 5, 15, 10)
    arrive(src1)
    take_token(0)
    pass_token(1)

    def unpack_src(p):
        f1["src"][2 * p], f1["src"][2 * p + 1] = unpack2(MID, s1p[p])

    for p in range(2, 8):
        unpack_src(p)
    smooth_down(MID, f1, ([(5, 15)], [(6, 14)], [(7, 13)]), 10)
    residual(MID, f1, 4)
    r2 = restrict(MID, lambda p: f1["res"][8 + p, 8:24], s["mix1"])
    arrive(cond2)
    for p in range(1, 6):
        unpack_cond(COARSE, k2p, f2, in2, p)
    coefficients(COARSE, f2, in2, w, wide, 3, 11, 8)
    z2p[3, 8:16] = pack2(COARSE, r2[0] * f2["inv"][6, 8:16], r2[1] * f2["inv"][7, 8:16])
    z2 = send_coarse(z2p, NEAR_COARSE)
    z2_far = send_coarse(z2p, FAR_COARSE)
    cond2_far = send_coarse(k2p, FAR_COARSE)
    src1_far = send_mid(s1p, FAR_MID)
    arrive(z2)
    take_token(1)
    pass_token(2)
    u = s["basis"]

    def unpack_z(p):
        for k, v in enumerate(unpack2(COARSE, z2p[p])):
            u[0, 2 * p + k] = jnp.where(inside(COARSE, in2, 2 * p + k, w, wide), v, 0.0)

    def apply_b(k, p):
        v = u[k, p]
        (t,) = near_sum(COARSE, f2, u.at[k], p, [v])
        u[k + 1, p] = v - f2["inv"][p] * t

    for p in range(1, 6):
        unpack_z(p)
    for k in range(4):
        for p in range(3 + k, 11 - k):
            apply_b(k, p)

    row8, lane8 = row_of(8), lane_of(8)
    sums = [jnp.zeros((8, LANES), F32) for _ in range(16)]
    for p in (6, 7):
        d = f2["diag"][p, 8:16]
        b = [u[k, p, 8:16] for k in range(5)]
        c = [
            b[0],
            b[0] - b[1],
            b[0] - 2.0 * b[1] + b[2],
            b[0] - 3.0 * (b[1] - b[2]) - b[3],
            b[0] - 4.0 * (b[1] + b[3]) + 6.0 * b[2] + b[4],
        ]
        for at, vs in ((0, b), (8, c)):
            for k in range(8):
                sums[at + k] = sums[at + k] + vs[k // 2] * d * vs[(k + 1) // 2]
    tiles = []
    for half in (0, 8):
        m = jnp.zeros((8, LANES), F32)
        for k in range(8):
            m = jnp.where(row8 == k, jnp.sum(sums[half + k], axis=0, keepdims=True), m)
        tiles.append(jnp.sum(m, axis=1, keepdims=True))
    spread = jnp.where(lane8 == row8, tiles[0], 0.0) + jnp.where(lane8 == row8 + 8, tiles[1], 0.0)
    mine, all1, all2 = s["mine"], s["all1"], s["all2"]
    mine[0] = jnp.sum(spread, axis=0, keepdims=True)
    rank = lax.rem(w, 4) * narrow + n
    all1[rank] = mine[0]

    def send_sum(src, dst, peers, at, stage):
        copies = []
        for i, peer in enumerate(peers):
            copy = pltpu.make_async_remote_copy(
                src_ref=src,
                dst_ref=dst,
                send_sem=s["sum_send"].at[at + i],
                recv_sem=s["sum_recv"].at[stage],
                device_id=peer,
                device_id_type=MESH,
            )
            copy.start()
            copies.append(copy)
        return copies

    sums1 = send_sum(mine.at[0], all1.at[rank], plane_peers, 0, 0)

    arrive(cond2_far + z2_far)
    for p in (0, 6):
        unpack_cond(COARSE, k2p, f2, in2, p)
        unpack_z(p)
    coefficients(COARSE, f2, in2, w, wide, 1, 3)
    coefficients(COARSE, f2, in2, w, wide, 11, 13)
    for k in range(3):
        for p in (1 + k, 2 + k, 11 - k, 12 - k):
            apply_b(k, p)
    arrive(cond1_far + src1_far)
    for p in (0, 1, 8, 9):
        unpack_cond(MID, k1p, f1, in1, p)
        unpack_src(p)
    coefficients(MID, f1, in1, w, wide, 1, 5, 4)
    coefficients(MID, f1, in1, w, wide, 15, 19, 4)
    smooth_down(
        MID, f1, ([(1, 5), (15, 19)], [(2, 6), (14, 18)], [(3, 7), (13, 17)]), 4
    )

    xa, xb, xe = s["mid_a"], s["mid_b"], s["mid_e"]

    def start_mid(p):
        xa[0, p] = f1["it"][p]
        for k in range(4):
            t = u[k, p // 2 + 2, 4:20]
            xa[1 + k, p, pl.ds(0, 16, stride=2), :] = t
            xa[1 + k, p, pl.ds(1, 16, stride=2), :] = t

    planes(3, 17, start_mid, 2)
    sweep_up(f1, MID, xa, xb, xe, 4, 16, None, 1.0 / THETA)
    others = all1.at[pl.ds(0, len(plane_peers))]
    pltpu.make_async_copy(others, others, s["sum_recv"].at[0]).wait()
    mine[1] = jnp.sum(all1[...], axis=0)
    all2[z] = mine[1]
    take_token(2)
    sums2 = send_sum(mine.at[1], all2.at[z], stack_peers, len(plane_peers), 1)

    sweep_up(f1, MID, xb, xa, xe, 5, 15, KEEP1, GAIN1)
    sweep_up(f1, MID, xa, xb, xe, 6, 14, KEEP2, GAIN2)
    arrive(its)
    ya, yb, ye = s["fine_a"], s["fine_b"], s["fine_e"]
    edge = s["edge"]

    def own_edge(p):
        edge[p, 8:40] = f0["it"][p, 8:40]

    planes(4, 12, own_edge)

    def start_fine(p):
        for k in range(5):
            t = xb[k, p // 2 + 6, 4:28]
            ya[k, p, pl.ds(0, 24, stride=2), :] = t
            ya[k, p, pl.ds(1, 24, stride=2), :] = t
        ya[0, p] = ya[0, p] + jnp.where(f0["inv"][p] > 0.0, edge[p], 0.0)

    planes(1, 15, start_fine, 2)
    sweep_up(f0, FINE, ya, yb, ye, 2, 14, None, 1.0 / THETA)
    sweep_up(f0, FINE, yb, ya, ye, 3, 13, KEEP1, GAIN1)
    sweep_up(f0, FINE, ya, yb, ye, 4, 12, KEEP2, GAIN2, slice(8, 40))
    for c in sent + sums1:
        c.wait_send()
    others = all2.at[pl.ds(0, len(stack_peers))]
    pltpu.make_async_copy(others, others, s["sum_recv"].at[1]).wait()
    total = jnp.broadcast_to(jnp.sum(all2[...], axis=0), (8, LANES))
    ta = jnp.sum(jnp.where(lane8 == row8, total, 0.0), axis=1, keepdims=True)
    tb = jnp.sum(jnp.where(lane8 == row8 + 8, total, 0.0), axis=1, keepdims=True)
    ta, tb = jnp.broadcast_to(ta, (8, LANES)), jnp.broadcast_to(tb, (8, LANES))
    y = solve4([ta[k : k + 1] for k in range(8)] + [tb[k : k + 1] for k in range(8)])

    def combine(p):
        v = yb[0, p + 4, 8:40]
        for k in range(4):
            v = v + y[k] * yb[1 + k, p + 4, 8:40]
        out[p] = v

    planes(0, 8, combine, 4)
    for c in sums2:
        c.wait_send()


def solution(mesh):
    wide, narrow = mesh.shape["wide"], mesh.shape["narrow"]

    def field(lv, *lead):
        return pltpu.VMEM((*lead, lv.planes, lv.rows, LANES), F32)

    scratch = {}
    for tag, lv in (("f0_", FINE), ("f1_", MID)):
        for k in FIELDS:
            scratch[tag + k] = field(lv)
    for k in ("k", "cx", "cyu", "cyd", "czr", "czl", "inv", "diag"):
        scratch["f2_" + k] = field(COARSE)
    scratch["basis"] = field(COARSE, 5)
    scratch["edge"] = field(FINE)
    for k in ("a", "b", "e"):
        scratch["mid_" + k] = field(MID, 5)
        scratch["fine_" + k] = field(FINE, 5)
    scratch["pack"] = pltpu.VMEM((2, 8, 8, LANES), F32)
    scratch["got"] = pltpu.VMEM((2, 16, 8, LANES), F32)
    scratch["mix0"] = pltpu.VMEM((4, 32, LANES), F32)
    scratch["mix1"] = pltpu.VMEM((2, 16, LANES), F32)
    for k in ("k1p", "s1p"):
        scratch[k] = pltpu.VMEM((10, 32, LANES), F32)
    for k in ("k2p", "z2p"):
        scratch[k] = pltpu.VMEM((7, 24, LANES), F32)
    scratch["mine"] = pltpu.VMEM((2, 1, LANES), F32)
    scratch["all1"] = pltpu.VMEM((4 * narrow, 1, LANES), F32)
    scratch["all2"] = pltpu.VMEM((wide // 4, 1, LANES), F32)
    messages = 10 + len(HALO_FINE) + 2 * len(NEAR_MID + FAR_MID + NEAR_COARSE + FAR_COARSE)
    scratch["send_sem"] = pltpu.SemaphoreType.DMA((messages,))
    scratch["recv_sem"] = pltpu.SemaphoreType.DMA((messages,))
    scratch["sum_send"] = pltpu.SemaphoreType.DMA((4 * narrow + wide // 4,))
    scratch["sum_recv"] = pltpu.SemaphoreType.DMA((2,))
    scratch["local_sem"] = pltpu.SemaphoreType.DMA((2,))
    for i in range(3):
        scratch[f"token{i}"] = pltpu.SemaphoreType.REGULAR

    def body(heat, cond):
        heat = pltpu.with_memory_space_constraint(heat, pltpu.HBM)
        cond = pltpu.with_memory_space_constraint(cond, pltpu.HBM)
        return pl.pallas_call(
            functools.partial(kernel, wide, narrow, tuple(scratch)),
            out_shape=pltpu.VMEM((8, 32, LANES), F32),
            in_specs=[pl.BlockSpec(memory_space=pltpu.HBM)] * 2,
            out_specs=pl.BlockSpec(memory_space=pltpu.VMEM),
            scratch_shapes=list(scratch.values()),
            compiler_params=pltpu.CompilerParams(
                collective_id=0, has_side_effects=True, vmem_limit_bytes=40 * 2**20
            ),
            cost_estimate=pl.CostEstimate(flops=50_000_000, bytes_accessed=400_000, transcendentals=0),
            name="vcycle",
        )(heat, cond)

    spec = P("wide", "narrow", None)
    return jax.shard_map(body, mesh=mesh, in_specs=(spec, spec), out_specs=spec, check_vma=False)
```

```python
import functools
import jax
import jax.numpy as jnp
from jax import lax
from jax.experimental import pallas as pl
from jax.experimental.pallas import tpu as pltpu
from jax.sharding import PartitionSpec as P

MASS = 0.002
LOW, HIGH = 0.25, 2.0
THETA = 0.5 * (HIGH + LOW)
DELTA = 0.5 * (HIGH - LOW)
SIGMA = THETA / DELTA
RHO1 = 1.0 / SIGMA
RHO2 = 1.0 / (2.0 * SIGMA - RHO1)
RHO3 = 1.0 / (2.0 * SIGMA - RHO2)
KEEP1, GAIN1 = RHO2 * RHO1, 2.0 * RHO2 / DELTA
KEEP2, GAIN2 = RHO3 * RHO2, 2.0 * RHO3 / DELTA
F32 = jnp.float32
LANES = 128
MESH = pl.DeviceIdType.MESH


class Level:
    def __init__(self, planes, first, own, rows, own_rows, repeat, scale):
        self.planes, self.first, self.own = planes, first, own
        self.rows, self.own_rows, self.repeat, self.scale = rows, own_rows, repeat, scale


FINE = Level(16, 4, 8, 48, 32, 1, 1.0)
MID = Level(20, 8, 4, 32, 16, 2, 0.25)
COARSE = Level(14, 6, 2, 24, 8, 4, 1.0 / 16.0)

FIELDS = ("k", "cx", "cyu", "cyd", "czr", "czl", "inv", "diag", "src", "hat", "upd", "it", "tmp", "res")


def planes(lo, hi, fn, unroll=99):
    count = hi - lo
    unroll = min(unroll, count)
    while count % unroll:
        unroll -= 1
    if unroll == count:
        for p in range(lo, hi):
            fn(p)
        return

    def step(i, carry):
        for k in range(unroll):
            fn(lo + i * unroll + k)
        return carry

    lax.fori_loop(0, count // unroll, step, 0)


def roll_rows(x, by):
    return pltpu.roll(x, by % x.shape[0], 0)


def roll_lanes(x, by):
    return pltpu.roll(x, by % LANES, 1)


def lane_of(rows):
    return lax.broadcasted_iota(jnp.int32, (rows, LANES), 1)


def row_of(rows):
    return lax.broadcasted_iota(jnp.int32, (rows, LANES), 0)


def near_sum(lv, f, ref, p, centers):
    cxu, cxd = f["cx"][p], f["cx"][p - 1]
    cyu, cyd, czr, czl = f["cyu"][p], f["cyd"][p], f["czr"][p], f["czl"][p]
    sums = []
    for v, c in enumerate(centers):
        at = ref.at[v] if len(ref.shape) == 4 else ref
        sums.append(
            cxu * at[p + 1]
            + cxd * at[p - 1]
            + cyu * roll_rows(c, -1)
            + cyd * roll_rows(c, 1)
            + czr * roll_lanes(c, -lv.repeat)
            + czl * roll_lanes(c, lv.repeat)
        )
    return sums


def inside_rows(lv, n, narrow):
    rows = row_of(lv.rows) + (n * lv.own_rows - 8)
    return (rows >= 0) & (rows < lv.own_rows * narrow)


def inside(lv, in_rows, p, w, wide):
    if isinstance(p, int) and lv.first <= p < lv.first + lv.own:
        return in_rows
    at = w * lv.own + p - lv.first
    return in_rows & (at >= 0) & (at < lv.own * wide)


def pack2(lv, x, y):
    return jnp.where(lax.rem(lane_of(x.shape[0]) // (lv.repeat // 2), 2) == 0, x, y)


def unpack2(lv, xy):
    half = lv.repeat // 2
    first = lax.rem(lane_of(xy.shape[0]) // half, 2) == 0
    return jnp.where(first, xy, roll_lanes(xy, half)), jnp.where(first, roll_lanes(xy, -half), xy)


def coefficients(lv, f, in_rows, w, wide, lo, hi, unroll=99):
    lane = lane_of(lv.rows)
    last = lane >= LANES - lv.repeat
    edge = last | (lane < lv.repeat)
    f["cx"][lo - 1] = 0.5 * (f["k"][lo - 1] + f["k"][lo])

    def one(p):
        k = f["k"][p]
        cxu = 0.5 * (k + f["k"][p + 1])
        cxd = 0.5 * (k + f["k"][p - 1])
        cyu = 0.5 * (k + roll_rows(k, -1))
        cyd = roll_rows(cyu, 1)
        czr = jnp.where(last, 0.0, 0.5 * (k + roll_lanes(k, -lv.repeat)))
        czl = roll_lanes(czr, lv.repeat)
        d = MASS + (cxu + cxd + cyu + cyd + czr + czl + jnp.where(edge, 0.5 * k, 0.0))
        f["cx"][p] = cxu
        f["cyu"][p] = cyu
        f["cyd"][p] = cyd
        f["czr"][p] = czr
        f["czl"][p] = czl
        f["diag"][p] = d
        f["inv"][p] = jnp.where(inside(lv, in_rows, p, w, wide), 1.0 / d, 0.0)

    planes(lo, hi, one, unroll)


def restrict(lv, read, mix):
    for j in range(lv.own // 2):
        mix[j] = read(2 * j) + read(2 * j + 1)
    half = lv.own_rows // 2
    even = lax.rem(lane_of(half) // lv.repeat, 2) == 0
    found = []
    for j in range(lv.own // 2):
        x = mix[j, pl.ds(0, half, stride=2), :] + mix[j, pl.ds(1, half, stride=2), :]
        x = x + jnp.where(even, roll_lanes(x, -lv.repeat), roll_lanes(x, lv.repeat))
        found.append(0.125 * x)
    return found


def smooth_down(lv, f, steps, unroll=99):
    def first(p):
        hat = f["src"][p] * f["inv"][p]
        f["hat"][p] = hat
        f["upd"][p] = hat * (1.0 / THETA)

    def second(p):
        x = f["upd"][p]
        (s,) = near_sum(lv, f, f["upd"], p, [x])
        z = f["hat"][p] + f["inv"][p] * s - x
        f["tmp"][p] = x + (KEEP1 * x + GAIN1 * z)

    def third(p):
        x = f["tmp"][p]
        (s,) = near_sum(lv, f, f["tmp"], p, [x])
        z = f["hat"][p] + f["inv"][p] * s - x
        f["it"][p] = x + (KEEP2 * (x - f["upd"][p]) + GAIN2 * z)

    for step, ranges in zip((first, second, third), steps):
        for lo, hi in ranges:
            planes(lo, hi, step, unroll)


def sweep_up(f, lv, old, new, e, lo, hi, keep, gain, own=None, unroll=2):
    count = old.shape[0]

    def one(p):
        centers = [old[v, p] for v in range(count)]
        sums = near_sum(lv, f, old, p, centers)
        inv = f["inv"][p]
        for v in range(count):
            z = inv * sums[v] - centers[v]
            if v == 0:
                z = z + f["hat"][p]
            u = gain * z if keep is None else keep * e[v, p] + gain * z
            if own is None:
                e[v, p] = u
                new[v, p] = centers[v] + u
            else:
                new[v, p, own] = (centers[v] + u)[own]

    planes(lo, hi, one, unroll)


def solve4(m):
    small = m[1] < 0.5 * m[0]
    pick = lambda a, b: jnp.where(small, a, b)
    g = [pick(m[k + 1], m[8 + k] - m[9 + k]) for k in range(7)]
    rhs = [pick(m[k], m[8 + k]) for k in range(4)]
    rows = [[g[i + j] for j in range(4)] for i in range(4)]
    inv = []
    for i in range(4):
        piv = rows[i][i]
        good = piv > 1e-7 * g[2 * i]
        inv.append(jnp.where(good, 1.0 / jnp.where(good, piv, 1.0), 0.0))
        for r in range(i + 1, 4):
            factor = rows[i][r] * inv[i]
            rows[r] = [rows[r][j] - factor * rows[i][j] if j >= r else None for j in range(4)]
            rhs[r] = rhs[r] - factor * rhs[i]
    y = [None] * 4
    for i in (3, 2, 1, 0):
        t = rhs[i]
        for j in range(i + 1, 4):
            t = t - rows[i][j] * y[j]
        y[i] = t * inv[i]
    turned = [
        y[0] + y[1] + y[2] + y[3],
        -(y[1] + 2.0 * y[2] + 3.0 * y[3]),
        y[2] + 3.0 * y[3],
        -y[3],
    ]
    return [pick(a, b) for a, b in zip(y, turned)]


def halo(reach):
    return [(dw, dn) for dn in (1, -1, 0) for dw in reach if (dw, dn) != (0, 0)]


NEAR_MID, FAR_MID = halo((1, -1, 0)), halo((2, -2))
NEAR_COARSE, FAR_COARSE = halo((1, -1, 0, 2, -2)), halo((3, -3))
HALO_FINE = halo((1, -1, 0))


def kernel(wide, narrow, names, heat, cond, out, *refs):
    s = dict(zip(names, refs))
    w, n = lax.axis_index("wide"), lax.axis_index("narrow")
    z, ylo, core = w // 4, lax.rem(w // 2, 2), lax.rem(w, 2)
    yhi, x = n // 4, lax.rem(n, 4)
    stacks = wide // 4

    f0 = {k: s["f0_" + k] for k in FIELDS}
    f1 = {k: s["f1_" + k] for k in FIELDS}
    f2 = {k: s["f2_" + k] for k in FIELDS if "f2_" + k in s}

    def near(dw, dn):
        return (lax.rem(w + (dw + wide), wide), lax.rem(n + (dn + narrow), narrow))

    def stack(dz):
        return (lax.rem(w + (4 * dz + wide), wide), n)

    def plane_peer(dx, dhi, dlo, dc):
        to = z * 4 + lax.rem(ylo + dlo, 2) * 2 + lax.rem(core + dc, 2)
        return (to, lax.rem(yhi + dhi, 2) * 4 + lax.rem(x + dx, 4))

    plane_peers = [
        plane_peer(*d)
        for d in sorted(
            [(dx, dhi, dlo, dc) for dx in range(4) for dhi in range(2) for dlo in range(2) for dc in range(2)],
            key=lambda d: -min(d[0], 4 - d[0]) - (1 if d[2] else 2 * d[1]),
        )
        if any(d)
    ]
    stack_peers = [stack(d) for d in sorted(range(1, stacks), key=lambda d: -min(d, stacks - d))]

    barrier = pltpu.get_barrier_semaphore()
    greeted = HALO_FINE + [d for d in NEAR_COARSE + FAR_COARSE if d not in HALO_FINE] + [(8, 0), (-8, 0), (4, 0), (-4, 0)]
    for d in greeted:
        pl.semaphore_signal(barrier, inc=1, device_id=near(*d), device_id_type=MESH)
    own_heat = pltpu.make_async_copy(heat, f0["src"].at[4:12, 8:40], s["local_sem"].at[0])
    own_cond = pltpu.make_async_copy(cond, f0["k"].at[4:12, 8:40], s["local_sem"].at[1])
    own_cond.start()
    own_heat.start()
    share = {k: s["share_" + k] for k in ("src", "hat", "upd", "tmp", "it", "res")}
    for ref in share.values():
        ref[4:16] = jnp.zeros((12, 32, LANES), F32)

    used = [0]
    sent = []

    def send(src, dst, peer):
        i = used[0]
        used[0] += 1
        copy = pltpu.make_async_remote_copy(
            src_ref=src,
            dst_ref=dst,
            send_sem=s["send_sem"].at[i],
            recv_sem=s["recv_sem"].at[i],
            device_id=peer,
            device_id_type=MESH,
        )
        copy.start()
        sent.append(copy)
        return copy

    def send_rows(ref_from, ref_to, first, own, own_rows, reach, depth):
        copies = []
        for dw, dn in reach:
            a, c, b = first, own, first - dw * own
            if depth < own and dw:
                a, b = (first + own - depth, first - depth) if dw > 0 else (first, first + own)
                c = depth
            ra, rc, rb = (8, own_rows, 8) if dn == 0 else (own_rows, 8, 0) if dn > 0 else (8, 8, 8 + own_rows)
            copies.append(
                send(ref_from.at[a : a + c, ra : ra + rc], ref_to.at[b : b + c, rb : rb + rc], near(dw, dn))
            )
        return copies

    def send_mid(ref, reach):
        return send_rows(ref, ref, 4, 2, 16, reach, 2)

    def send_coarse(ref, reach):
        return send_rows(ref, ref, 3, 1, 8, reach, 1)

    def arrive(copies):
        for c in copies:
            c.wait_recv()

    tokens = [s["token0"], s["token1"], s["token2"]]
    heard = [[stack(2), stack(-2)], [stack(4), stack(-4)], [near(0, 2), near(0, -2)]]

    def pass_token(i):
        for peer in heard[i]:
            pl.semaphore_signal(tokens[i], inc=1, device_id=peer, device_id_type=MESH)

    def take_token(i):
        pl.semaphore_wait(tokens[i], 2)

    own_cond.wait()
    own_heat.wait()
    low4 = row_of(8) < 4
    pack, got = s["pack"], s["got"]

    def pack_plane(p):
        h, c = f0["src"][p + 4, 32:40], f0["k"][p + 4, 32:40]
        pack[0, p] = jnp.where(low4, roll_rows(h, 4), c)
        h, c = f0["src"][p + 4, 8:16], f0["k"][p + 4, 8:16]
        pack[1, p] = jnp.where(low4, c, roll_rows(h, 4))

    planes(0, 8, pack_plane, 8)
    pl.semaphore_wait(barrier, len(greeted))
    first = [
        send(pack.at[0, 4:8], got.at[0, 0:4], near(1, 1)),
        send(pack.at[1, 4:8], got.at[1, 0:4], near(1, -1)),
        send(pack.at[0, 0:4], got.at[0, 12:16], near(-1, 1)),
        send(pack.at[1, 0:4], got.at[1, 12:16], near(-1, -1)),
        send(cond.at[4:8], f0["k"].at[0:4, 8:40], near(1, 0)),
        send(cond.at[0:4], f0["k"].at[12:16, 8:40], near(-1, 0)),
        send(pack.at[0], got.at[0, 4:12], near(0, 1)),
        send(pack.at[1], got.at[1, 4:12], near(0, -1)),
        send(heat.at[5:8], f0["src"].at[1:4, 8:40], near(1, 0)),
        send(heat.at[0:3], f0["src"].at[12:15, 8:40], near(-1, 0)),
    ]

    k1p, k2p, s1p, z2p = s["k1p"], s["k2p"], s["s1p"], s["z2p"]
    one_up = restrict(FINE, lambda p: f0["k"][4 + p, 8:40], s["mix0"])
    two_up = restrict(MID, lambda p: one_up[p], s["mix1"])
    for j in range(2):
        k1p[4 + j, 8:24] = pack2(MID, one_up[2 * j], one_up[2 * j + 1])
    k2p[3, 8:16] = pack2(COARSE, two_up[0], two_up[1])

    cond1 = send_mid(k1p, NEAR_MID)
    cond2 = send_coarse(k2p, NEAR_COARSE + FAR_COARSE)
    cond1_far = send_mid(k1p, FAR_MID)
    in0, in1, in2 = (inside_rows(lv, n, narrow) for lv in (FINE, MID, COARSE))

    def unpack_cond(lv, packed, f, in_rows, p):
        for k, v in enumerate(unpack2(lv, packed[p])):
            ok = inside(lv, in_rows, 2 * p + k, w, wide)
            f["k"][2 * p + k] = jnp.where(ok, v * lv.scale, 0.0)

    arrive(first[:8])
    pass_token(0)
    pass_token(2)

    in_low, in_high = in0[0:8] & ~low4, in0[40:48] & low4

    def unpack(p):
        f0["k"][p, 0:8] = jnp.where(in_low, got[0, p], 0.0)
        f0["k"][p, 40:48] = jnp.where(in_high, got[1, p], 0.0)
        f0["src"][p, 0:8] = roll_rows(got[0, p], 4)
        f0["src"][p, 40:48] = roll_rows(got[1, p], 4)
        if not 4 <= p < 12:
            at = w * 8 + p - 4
            f0["k"][p] = jnp.where((at >= 0) & (at < 8 * wide), f0["k"][p], 0.0)

    planes(0, 16, unpack)
    coefficients(FINE, f0, in0, w, wide, 1, 15)
    arrive(first[8:])
    arrive(cond1)
    for p in range(2, 8):
        unpack_cond(MID, k1p, f1, in1, p)
    coefficients(MID, f1, in1, w, wide, 5, 15)
    smooth_down(FINE, f0, ([(1, 15)], [(2, 14)], [(3, 13)]))

    def residual(lv, f, unroll):
        own = slice(8, 8 + lv.own_rows)

        def one(p):
            x = f["it"][p]
            (t,) = near_sum(lv, f, f["it"], p, [x])
            f["res"][p, own] = (f["src"][p] + t - f["diag"][p] * x)[own]

        planes(lv.first, lv.first + lv.own, one, unroll)

    residual(FINE, f0, 8)
    r1 = restrict(FINE, lambda p: f0["res"][4 + p, 8:40], s["mix0"])
    for j in range(2):
        s1p[4 + j, 8:24] = pack2(MID, r1[2 * j], r1[2 * j + 1])

    for j in range(4):
        p, own = MID.first + j, slice(8, 24)
        hat = r1[j] * f1["inv"][p, own]
        share["src"][p, own] = r1[j]
        share["hat"][p, own] = hat
        share["upd"][p, own] = hat * (1.0 / THETA)
    sf = dict(f1, **share)
    smooth_down(MID, sf, ([], [(7, 13)], [(6, 14)]))
    for p in range(5, 15):
        v = sf["it"][p]
        (t,) = near_sum(MID, f1, sf["it"], p, [v])
        v = sf["src"][p] + t - f1["diag"][p] * v
        sf["res"][p] = v if 8 <= p < 12 else jnp.where(f1["inv"][p] > 0.0, v, 0.0)
    for p in range(8, 12):
        for tile in (slice(0, 8), slice(24, 32)):
            sf["res"][p, tile] = jnp.where(f1["inv"][p, tile] > 0.0, sf["res"][p, tile], 0.0)
    mix2 = s["mix2"]
    lane16 = lax.rem(lane_of(16), 4)
    part = []
    for j in range(6):
        mix2[j] = sf["res"][4 + 2 * j] + sf["res"][5 + 2 * j]
    for j in range(6):
        v = mix2[j, pl.ds(0, 16, stride=2), :] + mix2[j, pl.ds(1, 16, stride=2), :]
        part.append(0.125 * (v + jnp.where(lane16 < 2, roll_lanes(v, -2), roll_lanes(v, 2))))
    ct, cr = s["ct"], s["cr"]
    for i in range(2):
        a, b, c, d = part[2 * i : 2 * i + 4]
        ct[i] = jnp.where(lane16 < 2, jnp.where(lane16 == 0, a, b), jnp.where(lane16 == 2, c, d))

    def slot(dw, dn):
        return (dw + 3) * 3 + dn + 1

    parts = []
    for dw, dn in NEAR_COARSE + FAR_COARSE:
        to = cr.at[slot(-dw, -dn)]
        which = pl.ds(1, 1) if dw >= 2 else pl.ds(0, 1) if dw <= -2 else pl.ds(0, 2)
        parts.append(send(ct.at[which], to.at[which], near(dw, dn)))
    src1 = send_mid(s1p, NEAR_MID)
    its = send_rows(f0["it"], s["edge"], 4, 8, 32, HALO_FINE, 3)
    src1_far = send_mid(s1p, FAR_MID)
    arrive(cond2)
    for p in range(7):
        unpack_cond(COARSE, k2p, f2, in2, p)
    coefficients(COARSE, f2, in2, w, wide, 1, 13)

    def unpack_src(p):
        f1["src"][2 * p], f1["src"][2 * p + 1] = unpack2(MID, s1p[p])

    arrive(parts)
    take_token(0)
    take_token(2)
    pass_token(1)
    u = s["basis"]

    def unpack_z(p):
        for k, v in enumerate(unpack2(COARSE, z2p[p])):
            u[0, 2 * p + k] = jnp.where(inside(COARSE, in2, 2 * p + k, w, wide), v, 0.0)

    def apply_b(k, p):
        v = u[k, p]
        (t,) = near_sum(COARSE, f2, u.at[k], p, [v])
        u[k + 1, p] = v - f2["inv"][p] * t

    lane8 = lane_of(8)
    head = lax.rem(lane8, 4) < 2
    bonds = {j: [None] * 4 for j in range(-3, 3)}

    def gain_of(j, dn, v, keep=None):
        for i in range(2):
            x = v[8 * i : 8 * i + 8]
            if keep is not None:
                x = jnp.where(keep, x, 0.0)
            at = dn + 1 + i
            bonds[j][at] = x if bonds[j][at] is None else bonds[j][at] + x

    for dn in (-1, 0, 1):
        lo = {d: cr.at[slot(d, dn), 0] for d in (-1, 0, 1, 2, 3)}
        hi = {d: cr.at[slot(d, dn), 1] for d in (-3, -2, -1, 0, 1)}
        if dn == 0:
            lo[0], hi[0] = ct.at[0], ct.at[1]
        gain_of(-3, dn, hi[-3][...])
        gain_of(-2, dn, hi[-2][...])
        gain_of(-2, dn, lo[-1][...], head)
        gain_of(-1, dn, hi[-1][...])
        gain_of(-1, dn, lo[0][...])
        gain_of(0, dn, lo[1][...])
        gain_of(0, dn, hi[0][...], ~head)
        gain_of(1, dn, lo[2][...])
        gain_of(1, dn, hi[1][...], ~head)
        gain_of(2, dn, lo[3][...])
    frame = s["frame"]
    for j in range(-2, 3):
        for i in range(4):
            v = jnp.where(head, bonds[j][i], bonds[j - 1][i])
            v = v + jnp.where(head, roll_lanes(v, -2), roll_lanes(v, 2))
            pair = unpack2(MID, v)
            for k in range(2):
                frame[j + 2, k, 8 * i : 8 * i + 8] = pair[k]
    for j in range(-2, 3):
        for k in range(2):
            p = 6 + 2 * j + k
            u[0, p] = roll_rows(frame[j + 2, k], -4)[0:24] * f2["inv"][p]
    z2p[3, 8:16] = pack2(COARSE, u[0, 6, 8:16], u[0, 7, 8:16])
    z2_far = send_coarse(z2p, FAR_COARSE)
    for k in range(4):
        for p in range(3 + k, 11 - k):
            apply_b(k, p)

    row8 = row_of(8)
    sums = [jnp.zeros((8, LANES), F32) for _ in range(16)]
    for p in (6, 7):
        d = f2["diag"][p, 8:16]
        b = [u[k, p, 8:16] for k in range(5)]
        c = [
            b[0],
            b[0] - b[1],
            b[0] - 2.0 * b[1] + b[2],
            b[0] - 3.0 * (b[1] - b[2]) - b[3],
            b[0] - 4.0 * (b[1] + b[3]) + 6.0 * b[2] + b[4],
        ]
        for at, vs in ((0, b), (8, c)):
            for k in range(8):
                sums[at + k] = sums[at + k] + vs[k // 2] * d * vs[(k + 1) // 2]
    tiles = []
    for half in (0, 8):
        m = jnp.zeros((8, LANES), F32)
        for k in range(8):
            m = jnp.where(row8 == k, jnp.sum(sums[half + k], axis=0, keepdims=True), m)
        tiles.append(jnp.sum(m, axis=1, keepdims=True))
    spread = jnp.where(lane8 == row8, tiles[0], 0.0) + jnp.where(lane8 == row8 + 8, tiles[1], 0.0)
    mine, all1, all2 = s["mine"], s["all1"], s["all2"]
    mine[0] = jnp.sum(spread, axis=0, keepdims=True)
    rank = lax.rem(w, 4) * narrow + n
    all1[rank] = mine[0]

    def send_sum(src, dst, peers, at, stage):
        copies = []
        for i, peer in enumerate(peers):
            copy = pltpu.make_async_remote_copy(
                src_ref=src,
                dst_ref=dst,
                send_sem=s["sum_send"].at[at + i],
                recv_sem=s["sum_recv"].at[stage],
                device_id=peer,
                device_id_type=MESH,
            )
            copy.start()
            copies.append(copy)
        return copies

    sums1 = send_sum(mine.at[0], all1.at[rank], plane_peers, 0, 0)

    arrive(cond1_far + src1 + src1_far)
    for p in (0, 1, 8, 9):
        unpack_cond(MID, k1p, f1, in1, p)
    for p in range(10):
        unpack_src(p)
    coefficients(MID, f1, in1, w, wide, 1, 5)
    coefficients(MID, f1, in1, w, wide, 15, 19)
    smooth_down(MID, f1, ([(1, 19)], [(2, 18)], [(3, 17)]))
    arrive(z2_far)
    for p in (0, 6):
        unpack_z(p)
    for k in range(3):
        for p in (1 + k, 2 + k, 11 - k, 12 - k):
            apply_b(k, p)

    xa, xb, xe = s["mid_a"], s["mid_b"], s["mid_e"]

    def start_mid(p):
        xa[0, p] = f1["it"][p]
        for k in range(4):
            t = u[k, p // 2 + 2, 4:20]
            xa[1 + k, p, pl.ds(0, 16, stride=2), :] = t
            xa[1 + k, p, pl.ds(1, 16, stride=2), :] = t

    planes(3, 17, start_mid, 2)
    sweep_up(f1, MID, xa, xb, xe, 4, 16, None, 1.0 / THETA)
    others = all1.at[pl.ds(0, len(plane_peers))]
    pltpu.make_async_copy(others, others, s["sum_recv"].at[0]).wait()
    mine[1] = jnp.sum(all1[...], axis=0)
    all2[z] = mine[1]
    take_token(1)
    sums2 = send_sum(mine.at[1], all2.at[z], stack_peers, len(plane_peers), 1)

    sweep_up(f1, MID, xb, xa, xe, 5, 15, KEEP1, GAIN1)
    sweep_up(f1, MID, xa, xb, xe, 6, 14, KEEP2, GAIN2)
    arrive(its)
    ya, yb, ye = s["fine_a"], s["fine_b"], s["fine_e"]
    edge = s["edge"]

    def own_edge(p):
        edge[p, 8:40] = f0["it"][p, 8:40]

    planes(4, 12, own_edge)

    def start_fine(p):
        for k in range(5):
            t = xb[k, p // 2 + 6, 4:28]
            ya[k, p, pl.ds(0, 24, stride=2), :] = t
            ya[k, p, pl.ds(1, 24, stride=2), :] = t
        ya[0, p] = ya[0, p] + jnp.where(f0["inv"][p] > 0.0, edge[p], 0.0)

    planes(1, 15, start_fine, 2)
    sweep_up(f0, FINE, ya, yb, ye, 2, 14, None, 1.0 / THETA)
    sweep_up(f0, FINE, yb, ya, ye, 3, 13, KEEP1, GAIN1)
    sweep_up(f0, FINE, ya, yb, ye, 4, 12, KEEP2, GAIN2, slice(8, 40))
    for c in sent + sums1:
        c.wait_send()
    others = all2.at[pl.ds(0, len(stack_peers))]
    pltpu.make_async_copy(others, others, s["sum_recv"].at[1]).wait()
    total = jnp.broadcast_to(jnp.sum(all2[...], axis=0), (8, LANES))
    ta = jnp.sum(jnp.where(lane8 == row8, total, 0.0), axis=1, keepdims=True)
    tb = jnp.sum(jnp.where(lane8 == row8 + 8, total, 0.0), axis=1, keepdims=True)
    ta, tb = jnp.broadcast_to(ta, (8, LANES)), jnp.broadcast_to(tb, (8, LANES))
    y = solve4([ta[k : k + 1] for k in range(8)] + [tb[k : k + 1] for k in range(8)])

    def combine(p):
        v = yb[0, p + 4, 8:40]
        for k in range(4):
            v = v + y[k] * yb[1 + k, p + 4, 8:40]
        out[p] = v

    planes(0, 8, combine, 4)
    for c in sums2:
        c.wait_send()


def solution(mesh):
    wide, narrow = mesh.shape["wide"], mesh.shape["narrow"]

    def field(lv, *lead):
        return pltpu.VMEM((*lead, lv.planes, lv.rows, LANES), F32)

    scratch = {}
    for tag, lv in (("f0_", FINE), ("f1_", MID)):
        for k in FIELDS:
            scratch[tag + k] = field(lv)
    for k in ("k", "cx", "cyu", "cyd", "czr", "czl", "inv", "diag"):
        scratch["f2_" + k] = field(COARSE)
    scratch["basis"] = field(COARSE, 5)
    scratch["edge"] = field(FINE)
    for k in ("a", "b", "e"):
        scratch["mid_" + k] = field(MID, 5)
        scratch["fine_" + k] = field(FINE, 5)
    scratch["pack"] = pltpu.VMEM((2, 8, 8, LANES), F32)
    scratch["got"] = pltpu.VMEM((2, 16, 8, LANES), F32)
    scratch["mix0"] = pltpu.VMEM((4, 32, LANES), F32)
    scratch["mix1"] = pltpu.VMEM((2, 16, LANES), F32)
    for k in ("k1p", "s1p"):
        scratch[k] = pltpu.VMEM((10, 32, LANES), F32)
    for k in ("k2p", "z2p"):
        scratch[k] = pltpu.VMEM((7, 24, LANES), F32)
    scratch["mine"] = pltpu.VMEM((2, 1, LANES), F32)
    scratch["all1"] = pltpu.VMEM((4 * narrow, 1, LANES), F32)
    scratch["all2"] = pltpu.VMEM((wide // 4, 1, LANES), F32)
    for k in ("src", "hat", "upd", "tmp", "it", "res"):
        scratch["share_" + k] = field(MID)
    scratch["mix2"] = pltpu.VMEM((6, 32, LANES), F32)
    scratch["ct"] = pltpu.VMEM((2, 16, LANES), F32)
    scratch["cr"] = pltpu.VMEM((21, 2, 16, LANES), F32)
    scratch["frame"] = pltpu.VMEM((5, 2, 32, LANES), F32)
    messages = 10 + len(HALO_FINE) + 2 * len(NEAR_MID + FAR_MID + NEAR_COARSE) + 3 * len(FAR_COARSE)
    scratch["send_sem"] = pltpu.SemaphoreType.DMA((messages,))
    scratch["recv_sem"] = pltpu.SemaphoreType.DMA((messages,))
    scratch["sum_send"] = pltpu.SemaphoreType.DMA((4 * narrow + wide // 4,))
    scratch["sum_recv"] = pltpu.SemaphoreType.DMA((2,))
    scratch["local_sem"] = pltpu.SemaphoreType.DMA((2,))
    for i in range(3):
        scratch[f"token{i}"] = pltpu.SemaphoreType.REGULAR

    def body(heat, cond):
        heat = pltpu.with_memory_space_constraint(heat, pltpu.HBM)
        cond = pltpu.with_memory_space_constraint(cond, pltpu.HBM)
        return pl.pallas_call(
            functools.partial(kernel, wide, narrow, tuple(scratch)),
            out_shape=pltpu.VMEM((8, 32, LANES), F32),
            in_specs=[pl.BlockSpec(memory_space=pltpu.HBM)] * 2,
            out_specs=pl.BlockSpec(memory_space=pltpu.VMEM),
            scratch_shapes=list(scratch.values()),
            compiler_params=pltpu.CompilerParams(
                collective_id=0, has_side_effects=True, vmem_limit_bytes=40 * 2**20
            ),
            cost_estimate=pl.CostEstimate(flops=50_000_000, bytes_accessed=400_000, transcendentals=0),
            name="vcycle",
        )(heat, cond)

    spec = P("wide", "narrow", None)
    return jax.shard_map(body, mesh=mesh, in_specs=(spec, spec), out_specs=spec, check_vma=False)
```

```python
import functools
import jax
import jax.numpy as jnp
from jax import lax
from jax.experimental import pallas as pl
from jax.experimental.pallas import tpu as pltpu
from jax.sharding import PartitionSpec as P

MASS = 0.002
LOW, HIGH = 0.25, 2.0
THETA = 0.5 * (HIGH + LOW)
DELTA = 0.5 * (HIGH - LOW)
SIGMA = THETA / DELTA
RHO1 = 1.0 / SIGMA
RHO2 = 1.0 / (2.0 * SIGMA - RHO1)
RHO3 = 1.0 / (2.0 * SIGMA - RHO2)
KEEP1, GAIN1 = RHO2 * RHO1, 2.0 * RHO2 / DELTA
KEEP2, GAIN2 = RHO3 * RHO2, 2.0 * RHO3 / DELTA
F32 = jnp.float32
LANES = 128
MESH = pl.DeviceIdType.MESH


class Level:
    def __init__(self, planes, first, own, rows, own_rows, repeat, scale):
        self.planes, self.first, self.own = planes, first, own
        self.rows, self.own_rows, self.repeat, self.scale = rows, own_rows, repeat, scale


FINE = Level(16, 4, 8, 48, 32, 1, 1.0)
MID = Level(20, 8, 4, 32, 16, 2, 0.25)
COARSE = Level(14, 6, 2, 24, 8, 4, 1.0 / 16.0)

FIELDS = ("k", "cx", "cyu", "cyd", "czr", "czl", "inv", "diag", "src", "hat", "upd", "it", "tmp", "res")


def planes(lo, hi, fn, unroll=99):
    count = hi - lo
    unroll = min(unroll, count)
    while count % unroll:
        unroll -= 1
    if unroll == count:
        for p in range(lo, hi):
            fn(p)
        return

    def step(i, carry):
        for k in range(unroll):
            fn(lo + i * unroll + k)
        return carry

    lax.fori_loop(0, count // unroll, step, 0)


def roll_rows(x, by):
    return pltpu.roll(x, by % x.shape[0], 0)


def roll_lanes(x, by):
    return pltpu.roll(x, by % LANES, 1)


def lane_of(rows):
    return lax.broadcasted_iota(jnp.int32, (rows, LANES), 1)


def row_of(rows):
    return lax.broadcasted_iota(jnp.int32, (rows, LANES), 0)


def near_sum(lv, f, ref, p, centers):
    cxu, cxd = f["cx"][p], f["cx"][p - 1]
    cyu, cyd, czr, czl = f["cyu"][p], f["cyd"][p], f["czr"][p], f["czl"][p]
    sums = []
    for v, c in enumerate(centers):
        at = ref.at[v] if len(ref.shape) == 4 else ref
        sums.append(
            cxu * at[p + 1]
            + cxd * at[p - 1]
            + cyu * roll_rows(c, -1)
            + cyd * roll_rows(c, 1)
            + czr * roll_lanes(c, -lv.repeat)
            + czl * roll_lanes(c, lv.repeat)
        )
    return sums


def inside_rows(lv, n, narrow):
    rows = row_of(lv.rows) + (n * lv.own_rows - 8)
    return (rows >= 0) & (rows < lv.own_rows * narrow)


def inside(lv, in_rows, p, w, wide):
    if isinstance(p, int) and lv.first <= p < lv.first + lv.own:
        return in_rows
    at = w * lv.own + p - lv.first
    return in_rows & (at >= 0) & (at < lv.own * wide)


def pack2(lv, x, y):
    return jnp.where(lax.rem(lane_of(x.shape[0]) // (lv.repeat // 2), 2) == 0, x, y)


def unpack2(lv, xy):
    half = lv.repeat // 2
    first = lax.rem(lane_of(xy.shape[0]) // half, 2) == 0
    return jnp.where(first, xy, roll_lanes(xy, half)), jnp.where(first, roll_lanes(xy, -half), xy)


def coefficients(lv, f, in_rows, w, wide, lo, hi, unroll=99):
    lane = lane_of(lv.rows)
    last = lane >= LANES - lv.repeat
    edge = last | (lane < lv.repeat)
    f["cx"][lo - 1] = 0.5 * (f["k"][lo - 1] + f["k"][lo])

    def one(p):
        k = f["k"][p]
        cxu = 0.5 * (k + f["k"][p + 1])
        cxd = 0.5 * (k + f["k"][p - 1])
        cyu = 0.5 * (k + roll_rows(k, -1))
        cyd = roll_rows(cyu, 1)
        czr = jnp.where(last, 0.0, 0.5 * (k + roll_lanes(k, -lv.repeat)))
        czl = roll_lanes(czr, lv.repeat)
        d = MASS + (cxu + cxd + cyu + cyd + czr + czl + jnp.where(edge, 0.5 * k, 0.0))
        f["cx"][p] = cxu
        f["cyu"][p] = cyu
        f["cyd"][p] = cyd
        f["czr"][p] = czr
        f["czl"][p] = czl
        f["diag"][p] = d
        f["inv"][p] = jnp.where(inside(lv, in_rows, p, w, wide), 1.0 / d, 0.0)

    planes(lo, hi, one, unroll)


def restrict(lv, read, mix):
    for j in range(lv.own // 2):
        mix[j] = read(2 * j) + read(2 * j + 1)
    half = lv.own_rows // 2
    even = lax.rem(lane_of(half) // lv.repeat, 2) == 0
    found = []
    for j in range(lv.own // 2):
        x = mix[j, pl.ds(0, half, stride=2), :] + mix[j, pl.ds(1, half, stride=2), :]
        x = x + jnp.where(even, roll_lanes(x, -lv.repeat), roll_lanes(x, lv.repeat))
        found.append(0.125 * x)
    return found


def smooth_down(lv, f, steps, unroll=99):
    def first(p):
        hat = f["src"][p] * f["inv"][p]
        f["hat"][p] = hat
        f["upd"][p] = hat * (1.0 / THETA)

    def second(p):
        x = f["upd"][p]
        (s,) = near_sum(lv, f, f["upd"], p, [x])
        z = f["hat"][p] + f["inv"][p] * s - x
        f["tmp"][p] = x + (KEEP1 * x + GAIN1 * z)

    def third(p):
        x = f["tmp"][p]
        (s,) = near_sum(lv, f, f["tmp"], p, [x])
        z = f["hat"][p] + f["inv"][p] * s - x
        f["it"][p] = x + (KEEP2 * (x - f["upd"][p]) + GAIN2 * z)

    for step, ranges in zip((first, second, third), steps):
        for lo, hi in ranges:
            planes(lo, hi, step, unroll)


def sweep_up(f, lv, old, new, e, lo, hi, keep, gain, own=None, unroll=2):
    count = old.shape[0]

    def one(p):
        centers = [old[v, p] for v in range(count)]
        sums = near_sum(lv, f, old, p, centers)
        inv = f["inv"][p]
        for v in range(count):
            z = inv * sums[v] - centers[v]
            if v == 0:
                z = z + f["hat"][p]
            u = gain * z if keep is None else keep * e[v, p] + gain * z
            if own is None:
                e[v, p] = u
                new[v, p] = centers[v] + u
            else:
                new[v, p, own] = (centers[v] + u)[own]

    planes(lo, hi, one, unroll)


def solve4(m):
    small = m[1] < 0.5 * m[0]
    pick = lambda a, b: jnp.where(small, a, b)
    g = [pick(m[k + 1], m[8 + k] - m[9 + k]) for k in range(7)]
    rhs = [pick(m[k], m[8 + k]) for k in range(4)]
    rows = [[g[i + j] for j in range(4)] for i in range(4)]
    inv = []
    for i in range(4):
        piv = rows[i][i]
        good = piv > 1e-7 * g[2 * i]
        inv.append(jnp.where(good, 1.0 / jnp.where(good, piv, 1.0), 0.0))
        for r in range(i + 1, 4):
            factor = rows[i][r] * inv[i]
            rows[r] = [rows[r][j] - factor * rows[i][j] if j >= r else None for j in range(4)]
            rhs[r] = rhs[r] - factor * rhs[i]
    y = [None] * 4
    for i in (3, 2, 1, 0):
        t = rhs[i]
        for j in range(i + 1, 4):
            t = t - rows[i][j] * y[j]
        y[i] = t * inv[i]
    turned = [
        y[0] + y[1] + y[2] + y[3],
        -(y[1] + 2.0 * y[2] + 3.0 * y[3]),
        y[2] + 3.0 * y[3],
        -y[3],
    ]
    return [pick(a, b) for a, b in zip(y, turned)]


def halo(reach):
    return [(dw, dn) for dn in (1, -1, 0) for dw in reach if (dw, dn) != (0, 0)]


NEAR_MID, FAR_MID = halo((1, -1, 0)), halo((2, -2))
NEAR_COARSE, FAR_COARSE = halo((1, -1, 0, 2, -2)), halo((3, -3))
HALO_FINE = halo((1, -1, 0))


def kernel(wide, narrow, names, heat, cond, out, *refs):
    s = dict(zip(names, refs))
    w, n = lax.axis_index("wide"), lax.axis_index("narrow")
    z, ylo, core = w // 4, lax.rem(w // 2, 2), lax.rem(w, 2)
    yhi, x = n // 4, lax.rem(n, 4)
    stacks = wide // 4

    f0 = {k: s["f0_" + k] for k in FIELDS}
    f1 = {k: s["f1_" + k] for k in FIELDS}
    f2 = {k: s["f2_" + k] for k in FIELDS if "f2_" + k in s}

    def near(dw, dn):
        return (lax.rem(w + (dw + wide), wide), lax.rem(n + (dn + narrow), narrow))

    def stack(dz):
        return (lax.rem(w + (4 * dz + wide), wide), n)

    def plane_peer(dx, dhi, dlo, dc):
        to = z * 4 + lax.rem(ylo + dlo, 2) * 2 + lax.rem(core + dc, 2)
        return (to, lax.rem(yhi + dhi, 2) * 4 + lax.rem(x + dx, 4))

    plane_peers = [
        plane_peer(*d)
        for d in sorted(
            [(dx, dhi, dlo, dc) for dx in range(4) for dhi in range(2) for dlo in range(2) for dc in range(2)],
            key=lambda d: -min(d[0], 4 - d[0]) - (1 if d[2] else 2 * d[1]),
        )
        if any(d)
    ]
    stack_peers = [stack(d) for d in sorted(range(1, stacks), key=lambda d: -min(d, stacks - d))]

    barrier = pltpu.get_barrier_semaphore()
    greeted = HALO_FINE + [d for d in NEAR_COARSE + FAR_COARSE if d not in HALO_FINE] + [(8, 0), (-8, 0), (4, 0), (-4, 0)]
    for d in greeted:
        pl.semaphore_signal(barrier, inc=1, device_id=near(*d), device_id_type=MESH)
    own_heat = pltpu.make_async_copy(heat, f0["src"].at[4:12, 8:40], s["local_sem"].at[0])
    own_cond = pltpu.make_async_copy(cond, f0["k"].at[4:12, 8:40], s["local_sem"].at[1])
    own_cond.start()
    own_heat.start()
    share = {k: s["share_" + k] for k in ("src", "hat", "upd", "tmp", "it", "res")}
    for ref in share.values():
        ref[4:16] = jnp.zeros((12, 32, LANES), F32)

    used = [0]
    sent = []

    def send(src, dst, peer):
        i = used[0]
        used[0] += 1
        copy = pltpu.make_async_remote_copy(
            src_ref=src,
            dst_ref=dst,
            send_sem=s["send_sem"].at[i],
            recv_sem=s["recv_sem"].at[i],
            device_id=peer,
            device_id_type=MESH,
        )
        copy.start()
        sent.append(copy)
        return copy

    def send_rows(ref_from, ref_to, first, own, own_rows, reach, depth):
        copies = []
        for dw, dn in reach:
            a, c, b = first, own, first - dw * own
            if depth < own and dw:
                a, b = (first + own - depth, first - depth) if dw > 0 else (first, first + own)
                c = depth
            ra, rc, rb = (8, own_rows, 8) if dn == 0 else (own_rows, 8, 0) if dn > 0 else (8, 8, 8 + own_rows)
            copies.append(
                send(ref_from.at[a : a + c, ra : ra + rc], ref_to.at[b : b + c, rb : rb + rc], near(dw, dn))
            )
        return copies

    def send_mid(ref, reach):
        return send_rows(ref, ref, 4, 2, 16, reach, 2)

    def send_coarse(ref, reach):
        return send_rows(ref, ref, 3, 1, 8, reach, 1)

    def arrive(copies):
        for c in copies:
            c.wait_recv()

    tokens = [s["token0"], s["token1"], s["token2"]]
    heard = [[stack(2), stack(-2)], [stack(4), stack(-4)], [near(0, 2), near(0, -2)]]

    def pass_token(i):
        for peer in heard[i]:
            pl.semaphore_signal(tokens[i], inc=1, device_id=peer, device_id_type=MESH)

    def take_token(i):
        pl.semaphore_wait(tokens[i], 2)

    own_cond.wait()
    own_heat.wait()
    low4 = row_of(8) < 4
    pack, got = s["pack"], s["got"]

    def pack_plane(p):
        h, c = f0["src"][p + 4, 32:40], f0["k"][p + 4, 32:40]
        pack[0, p] = jnp.where(low4, roll_rows(h, 4), c)
        h, c = f0["src"][p + 4, 8:16], f0["k"][p + 4, 8:16]
        pack[1, p] = jnp.where(low4, c, roll_rows(h, 4))

    planes(0, 8, pack_plane, 8)
    pl.semaphore_wait(barrier, len(greeted))
    first = [
        send(pack.at[0, 4:8], got.at[0, 0:4], near(1, 1)),
        send(pack.at[1, 4:8], got.at[1, 0:4], near(1, -1)),
        send(pack.at[0, 0:4], got.at[0, 12:16], near(-1, 1)),
        send(pack.at[1, 0:4], got.at[1, 12:16], near(-1, -1)),
        send(cond.at[4:8], f0["k"].at[0:4, 8:40], near(1, 0)),
        send(cond.at[0:4], f0["k"].at[12:16, 8:40], near(-1, 0)),
        send(pack.at[0], got.at[0, 4:12], near(0, 1)),
        send(pack.at[1], got.at[1, 4:12], near(0, -1)),
        send(heat.at[5:8], f0["src"].at[1:4, 8:40], near(1, 0)),
        send(heat.at[0:3], f0["src"].at[12:15, 8:40], near(-1, 0)),
    ]

    k1p, k2p, s1p, z2p = s["k1p"], s["k2p"], s["s1p"], s["z2p"]
    one_up = restrict(FINE, lambda p: f0["k"][4 + p, 8:40], s["mix0"])
    two_up = restrict(MID, lambda p: one_up[p], s["mix1"])
    for j in range(2):
        k1p[4 + j, 8:24] = pack2(MID, one_up[2 * j], one_up[2 * j + 1])
    k2p[3, 8:16] = pack2(COARSE, two_up[0], two_up[1])

    cond1 = send_mid(k1p, NEAR_MID)
    cond2 = send_coarse(k2p, NEAR_COARSE + FAR_COARSE)
    in0, in1, in2 = (inside_rows(lv, n, narrow) for lv in (FINE, MID, COARSE))

    def unpack_cond(lv, packed, f, in_rows, p):
        for k, v in enumerate(unpack2(lv, packed[p])):
            ok = inside(lv, in_rows, 2 * p + k, w, wide)
            f["k"][2 * p + k] = jnp.where(ok, v * lv.scale, 0.0)

    arrive(first[:8])
    pass_token(0)
    pass_token(2)

    in_low, in_high = in0[0:8] & ~low4, in0[40:48] & low4

    def unpack(p):
        f0["k"][p, 0:8] = jnp.where(in_low, got[0, p], 0.0)
        f0["k"][p, 40:48] = jnp.where(in_high, got[1, p], 0.0)
        f0["src"][p, 0:8] = roll_rows(got[0, p], 4)
        f0["src"][p, 40:48] = roll_rows(got[1, p], 4)
        if not 4 <= p < 12:
            at = w * 8 + p - 4
            f0["k"][p] = jnp.where((at >= 0) & (at < 8 * wide), f0["k"][p], 0.0)

    planes(0, 16, unpack)
    coefficients(FINE, f0, in0, w, wide, 1, 15)
    arrive(first[8:])
    arrive(cond1)
    for p in range(2, 8):
        unpack_cond(MID, k1p, f1, in1, p)
    coefficients(MID, f1, in1, w, wide, 5, 15)
    smooth_down(FINE, f0, ([(1, 15)], [(2, 14)], [(3, 13)]))

    def residual(lv, f, unroll):
        own = slice(8, 8 + lv.own_rows)

        def one(p):
            x = f["it"][p]
            (t,) = near_sum(lv, f, f["it"], p, [x])
            f["res"][p, own] = (f["src"][p] + t - f["diag"][p] * x)[own]

        planes(lv.first, lv.first + lv.own, one, unroll)

    residual(FINE, f0, 8)
    r1 = restrict(FINE, lambda p: f0["res"][4 + p, 8:40], s["mix0"])
    for j in range(2):
        s1p[4 + j, 8:24] = pack2(MID, r1[2 * j], r1[2 * j + 1])

    for j in range(4):
        p, own = MID.first + j, slice(8, 24)
        hat = r1[j] * f1["inv"][p, own]
        share["src"][p, own] = r1[j]
        share["hat"][p, own] = hat
        share["upd"][p, own] = hat * (1.0 / THETA)
    sf = dict(f1, **share)
    smooth_down(MID, sf, ([], [(7, 13)], [(6, 14)]))
    for p in range(5, 15):
        v = sf["it"][p]
        (t,) = near_sum(MID, f1, sf["it"], p, [v])
        v = sf["src"][p] + t - f1["diag"][p] * v
        sf["res"][p] = v if 8 <= p < 12 else jnp.where(f1["inv"][p] > 0.0, v, 0.0)
    for p in range(8, 12):
        for tile in (slice(0, 8), slice(24, 32)):
            sf["res"][p, tile] = jnp.where(f1["inv"][p, tile] > 0.0, sf["res"][p, tile], 0.0)
    mix2 = s["mix2"]
    lane16 = lax.rem(lane_of(16), 4)
    part = []
    for j in range(6):
        mix2[j] = sf["res"][4 + 2 * j] + sf["res"][5 + 2 * j]
    for j in range(6):
        v = mix2[j, pl.ds(0, 16, stride=2), :] + mix2[j, pl.ds(1, 16, stride=2), :]
        part.append(0.125 * (v + jnp.where(lane16 < 2, roll_lanes(v, -2), roll_lanes(v, 2))))
    ct, cr = s["ct"], s["cr"]
    for i in range(2):
        a, b, c, d = part[2 * i : 2 * i + 4]
        ct[i] = jnp.where(lane16 < 2, jnp.where(lane16 == 0, a, b), jnp.where(lane16 == 2, c, d))

    def slot(dw, dn):
        return (dw + 3) * 3 + dn + 1

    parts = []
    for dw, dn in NEAR_COARSE + FAR_COARSE:
        to = cr.at[slot(-dw, -dn)]
        which = pl.ds(1, 1) if dw >= 2 else pl.ds(0, 1) if dw <= -2 else pl.ds(0, 2)
        parts.append(send(ct.at[which], to.at[which], near(dw, dn)))
    src1 = send_mid(s1p, NEAR_MID)
    its = send_rows(f0["it"], s["edge"], 4, 8, 32, HALO_FINE, 3)
    src1_far = send_mid(s1p, FAR_MID)
    cond1_far = send_mid(k1p, FAR_MID)
    arrive(cond2)
    for p in range(7):
        unpack_cond(COARSE, k2p, f2, in2, p)
    coefficients(COARSE, f2, in2, w, wide, 1, 13)

    def unpack_src(p):
        f1["src"][2 * p], f1["src"][2 * p + 1] = unpack2(MID, s1p[p])

    arrive(parts)
    take_token(0)
    take_token(2)
    pass_token(1)
    u = s["basis"]

    def unpack_z(p):
        for k, v in enumerate(unpack2(COARSE, z2p[p])):
            u[0, 2 * p + k] = jnp.where(inside(COARSE, in2, 2 * p + k, w, wide), v, 0.0)

    def apply_b(k, p):
        v = u[k, p]
        (t,) = near_sum(COARSE, f2, u.at[k], p, [v])
        u[k + 1, p] = v - f2["inv"][p] * t

    lane8 = lane_of(8)
    head = lax.rem(lane8, 4) < 2
    bonds = {j: [None] * 4 for j in range(-3, 3)}

    def gain_of(j, dn, v, keep=None):
        for i in range(2):
            x = v[8 * i : 8 * i + 8]
            if keep is not None:
                x = jnp.where(keep, x, 0.0)
            at = dn + 1 + i
            bonds[j][at] = x if bonds[j][at] is None else bonds[j][at] + x

    for dn in (-1, 0, 1):
        lo = {d: cr.at[slot(d, dn), 0] for d in (-1, 0, 1, 2, 3)}
        hi = {d: cr.at[slot(d, dn), 1] for d in (-3, -2, -1, 0, 1)}
        if dn == 0:
            lo[0], hi[0] = ct.at[0], ct.at[1]
        gain_of(-3, dn, hi[-3][...])
        gain_of(-2, dn, hi[-2][...])
        gain_of(-2, dn, lo[-1][...], head)
        gain_of(-1, dn, hi[-1][...])
        gain_of(-1, dn, lo[0][...])
        gain_of(0, dn, lo[1][...])
        gain_of(0, dn, hi[0][...], ~head)
        gain_of(1, dn, lo[2][...])
        gain_of(1, dn, hi[1][...], ~head)
        gain_of(2, dn, lo[3][...])
    frame = s["frame"]
    for j in range(-2, 3):
        for i in range(4):
            v = jnp.where(head, bonds[j][i], bonds[j - 1][i])
            v = v + jnp.where(head, roll_lanes(v, -2), roll_lanes(v, 2))
            pair = unpack2(MID, v)
            for k in range(2):
                frame[j + 2, k, 8 * i : 8 * i + 8] = pair[k]
    for j in range(-2, 3):
        for k in range(2):
            p = 6 + 2 * j + k
            u[0, p] = roll_rows(frame[j + 2, k], -4)[0:24] * f2["inv"][p]
    z2p[3, 8:16] = pack2(COARSE, u[0, 6, 8:16], u[0, 7, 8:16])
    for k in range(4):
        for p in range(3 + k, 11 - k):
            apply_b(k, p)

    row8 = row_of(8)
    sums = [jnp.zeros((8, LANES), F32) for _ in range(16)]
    for p in (6, 7):
        d = f2["diag"][p, 8:16]
        b = [u[k, p, 8:16] for k in range(5)]
        c = [
            b[0],
            b[0] - b[1],
            b[0] - 2.0 * b[1] + b[2],
            b[0] - 3.0 * (b[1] - b[2]) - b[3],
            b[0] - 4.0 * (b[1] + b[3]) + 6.0 * b[2] + b[4],
        ]
        for at, vs in ((0, b), (8, c)):
            for k in range(8):
                sums[at + k] = sums[at + k] + vs[k // 2] * d * vs[(k + 1) // 2]
    tiles = []
    for half in (0, 8):
        m = jnp.zeros((8, LANES), F32)
        for k in range(8):
            m = jnp.where(row8 == k, jnp.sum(sums[half + k], axis=0, keepdims=True), m)
        tiles.append(jnp.sum(m, axis=1, keepdims=True))
    spread = jnp.where(lane8 == row8, tiles[0], 0.0) + jnp.where(lane8 == row8 + 8, tiles[1], 0.0)
    mine, all1, all2 = s["mine"], s["all1"], s["all2"]
    mine[0] = jnp.sum(spread, axis=0, keepdims=True)
    rank = lax.rem(w, 4) * narrow + n
    all1[rank] = mine[0]

    def send_sum(src, dst, peers, at, stage):
        copies = []
        for i, peer in enumerate(peers):
            copy = pltpu.make_async_remote_copy(
                src_ref=src,
                dst_ref=dst,
                send_sem=s["sum_send"].at[at + i],
                recv_sem=s["sum_recv"].at[stage],
                device_id=peer,
                device_id_type=MESH,
            )
            copy.start()
            copies.append(copy)
        return copies

    sums1 = send_sum(mine.at[0], all1.at[rank], plane_peers, 0, 0)
    z2_far = send_coarse(z2p, FAR_COARSE)

    arrive(cond1_far + src1 + src1_far)
    for p in (0, 1, 8, 9):
        unpack_cond(MID, k1p, f1, in1, p)
    for p in range(10):
        unpack_src(p)
    coefficients(MID, f1, in1, w, wide, 1, 5)
    coefficients(MID, f1, in1, w, wide, 15, 19)
    smooth_down(MID, f1, ([(1, 19)], [(2, 18)], [(3, 17)]))
    others = all1.at[pl.ds(0, len(plane_peers))]
    pltpu.make_async_copy(others, others, s["sum_recv"].at[0]).wait()
    mine[1] = jnp.sum(all1[...], axis=0)
    all2[z] = mine[1]
    take_token(1)
    sums2 = send_sum(mine.at[1], all2.at[z], stack_peers, len(plane_peers), 1)
    arrive(z2_far)
    for p in (0, 6):
        unpack_z(p)
    for k in range(3):
        for p in (1 + k, 2 + k, 11 - k, 12 - k):
            apply_b(k, p)

    xa, xb, xe = s["mid_a"], s["mid_b"], s["mid_e"]

    def start_mid(p):
        xa[0, p] = f1["it"][p]
        for k in range(4):
            t = u[k, p // 2 + 2, 4:20]
            xa[1 + k, p, pl.ds(0, 16, stride=2), :] = t
            xa[1 + k, p, pl.ds(1, 16, stride=2), :] = t

    planes(3, 17, start_mid, 2)
    sweep_up(f1, MID, xa, xb, xe, 4, 16, None, 1.0 / THETA)
    sweep_up(f1, MID, xb, xa, xe, 5, 15, KEEP1, GAIN1)
    sweep_up(f1, MID, xa, xb, xe, 6, 14, KEEP2, GAIN2)
    arrive(its)
    ya, yb, ye = s["fine_a"], s["fine_b"], s["fine_e"]
    edge = s["edge"]

    def own_edge(p):
        edge[p, 8:40] = f0["it"][p, 8:40]

    planes(4, 12, own_edge)

    def start_fine(p):
        for k in range(5):
            t = xb[k, p // 2 + 6, 4:28]
            ya[k, p, pl.ds(0, 24, stride=2), :] = t
            ya[k, p, pl.ds(1, 24, stride=2), :] = t
        ya[0, p] = ya[0, p] + jnp.where(f0["inv"][p] > 0.0, edge[p], 0.0)

    planes(1, 15, start_fine, 2)
    sweep_up(f0, FINE, ya, yb, ye, 2, 14, None, 1.0 / THETA)
    sweep_up(f0, FINE, yb, ya, ye, 3, 13, KEEP1, GAIN1)
    sweep_up(f0, FINE, ya, yb, ye, 4, 12, KEEP2, GAIN2, slice(8, 40))
    for c in sent + sums1:
        c.wait_send()
    others = all2.at[pl.ds(0, len(stack_peers))]
    pltpu.make_async_copy(others, others, s["sum_recv"].at[1]).wait()
    total = jnp.broadcast_to(jnp.sum(all2[...], axis=0), (8, LANES))
    ta = jnp.sum(jnp.where(lane8 == row8, total, 0.0), axis=1, keepdims=True)
    tb = jnp.sum(jnp.where(lane8 == row8 + 8, total, 0.0), axis=1, keepdims=True)
    ta, tb = jnp.broadcast_to(ta, (8, LANES)), jnp.broadcast_to(tb, (8, LANES))
    y = solve4([ta[k : k + 1] for k in range(8)] + [tb[k : k + 1] for k in range(8)])

    def combine(p):
        v = yb[0, p + 4, 8:40]
        for k in range(4):
            v = v + y[k] * yb[1 + k, p + 4, 8:40]
        out[p] = v

    planes(0, 8, combine)
    for c in sums2:
        c.wait_send()


def solution(mesh):
    wide, narrow = mesh.shape["wide"], mesh.shape["narrow"]

    def field(lv, *lead):
        return pltpu.VMEM((*lead, lv.planes, lv.rows, LANES), F32)

    scratch = {}
    for tag, lv in (("f0_", FINE), ("f1_", MID)):
        for k in FIELDS:
            scratch[tag + k] = field(lv)
    for k in ("k", "cx", "cyu", "cyd", "czr", "czl", "inv", "diag"):
        scratch["f2_" + k] = field(COARSE)
    scratch["basis"] = field(COARSE, 5)
    scratch["edge"] = field(FINE)
    for k in ("a", "b", "e"):
        scratch["mid_" + k] = field(MID, 5)
        scratch["fine_" + k] = field(FINE, 5)
    scratch["pack"] = pltpu.VMEM((2, 8, 8, LANES), F32)
    scratch["got"] = pltpu.VMEM((2, 16, 8, LANES), F32)
    scratch["mix0"] = pltpu.VMEM((4, 32, LANES), F32)
    scratch["mix1"] = pltpu.VMEM((2, 16, LANES), F32)
    for k in ("k1p", "s1p"):
        scratch[k] = pltpu.VMEM((10, 32, LANES), F32)
    for k in ("k2p", "z2p"):
        scratch[k] = pltpu.VMEM((7, 24, LANES), F32)
    scratch["mine"] = pltpu.VMEM((2, 1, LANES), F32)
    scratch["all1"] = pltpu.VMEM((4 * narrow, 1, LANES), F32)
    scratch["all2"] = pltpu.VMEM((wide // 4, 1, LANES), F32)
    for k in ("src", "hat", "upd", "tmp", "it", "res"):
        scratch["share_" + k] = field(MID)
    scratch["mix2"] = pltpu.VMEM((6, 32, LANES), F32)
    scratch["ct"] = pltpu.VMEM((2, 16, LANES), F32)
    scratch["cr"] = pltpu.VMEM((21, 2, 16, LANES), F32)
    scratch["frame"] = pltpu.VMEM((5, 2, 32, LANES), F32)
    messages = 10 + len(HALO_FINE) + 2 * len(NEAR_MID + FAR_MID + NEAR_COARSE) + 3 * len(FAR_COARSE)
    scratch["send_sem"] = pltpu.SemaphoreType.DMA((messages,))
    scratch["recv_sem"] = pltpu.SemaphoreType.DMA((messages,))
    scratch["sum_send"] = pltpu.SemaphoreType.DMA((4 * narrow + wide // 4,))
    scratch["sum_recv"] = pltpu.SemaphoreType.DMA((2,))
    scratch["local_sem"] = pltpu.SemaphoreType.DMA((2,))
    for i in range(3):
        scratch[f"token{i}"] = pltpu.SemaphoreType.REGULAR

    def body(heat, cond):
        heat = pltpu.with_memory_space_constraint(heat, pltpu.HBM)
        cond = pltpu.with_memory_space_constraint(cond, pltpu.HBM)
        return pl.pallas_call(
            functools.partial(kernel, wide, narrow, tuple(scratch)),
            out_shape=pltpu.VMEM((8, 32, LANES), F32),
            in_specs=[pl.BlockSpec(memory_space=pltpu.HBM)] * 2,
            out_specs=pl.BlockSpec(memory_space=pltpu.VMEM),
            scratch_shapes=list(scratch.values()),
            compiler_params=pltpu.CompilerParams(
                collective_id=0, has_side_effects=True, vmem_limit_bytes=40 * 2**20
            ),
            cost_estimate=pl.CostEstimate(flops=50_000_000, bytes_accessed=400_000, transcendentals=0),
            name="vcycle",
        )(heat, cond)

    spec = P("wide", "narrow", None)
    return jax.shard_map(body, mesh=mesh, in_specs=(spec, spec), out_specs=spec, check_vma=False)
```

```python
import functools
import jax
import jax.numpy as jnp
from jax import lax
from jax.experimental import pallas as pl
from jax.experimental.pallas import tpu as pltpu
from jax.sharding import PartitionSpec as P

MASS = 0.002
LOW, HIGH = 0.25, 2.0
THETA = 0.5 * (HIGH + LOW)
DELTA = 0.5 * (HIGH - LOW)
SIGMA = THETA / DELTA
RHO1 = 1.0 / SIGMA
RHO2 = 1.0 / (2.0 * SIGMA - RHO1)
RHO3 = 1.0 / (2.0 * SIGMA - RHO2)
KEEP1, GAIN1 = RHO2 * RHO1, 2.0 * RHO2 / DELTA
KEEP2, GAIN2 = RHO3 * RHO2, 2.0 * RHO3 / DELTA
F32 = jnp.float32
LANES = 128
MESH = pl.DeviceIdType.MESH


class Level:
    def __init__(self, planes, first, own, rows, own_rows, repeat, scale):
        self.planes, self.first, self.own = planes, first, own
        self.rows, self.own_rows, self.repeat, self.scale = rows, own_rows, repeat, scale


FINE = Level(16, 4, 8, 48, 32, 1, 1.0)
MID = Level(20, 8, 4, 32, 16, 2, 0.25)
COARSE = Level(14, 6, 2, 24, 8, 4, 1.0 / 16.0)

FIELDS = ("k", "cx", "cyu", "cyd", "czr", "czl", "inv", "diag", "src", "hat", "upd", "it", "tmp", "res")


def planes(lo, hi, fn, unroll=99):
    count = hi - lo
    unroll = min(unroll, count)
    while count % unroll:
        unroll -= 1
    if unroll == count:
        for p in range(lo, hi):
            fn(p)
        return

    def step(i, carry):
        for k in range(unroll):
            fn(lo + i * unroll + k)
        return carry

    lax.fori_loop(0, count // unroll, step, 0)


def roll_rows(x, by):
    return pltpu.roll(x, by % x.shape[0], 0)


def roll_lanes(x, by):
    return pltpu.roll(x, by % LANES, 1)


def lane_of(rows):
    return lax.broadcasted_iota(jnp.int32, (rows, LANES), 1)


def row_of(rows):
    return lax.broadcasted_iota(jnp.int32, (rows, LANES), 0)


def near_sum(lv, f, ref, p, centers):
    cxu, cxd = f["cx"][p], f["cx"][p - 1]
    cyu, cyd, czr, czl = f["cyu"][p], f["cyd"][p], f["czr"][p], f["czl"][p]
    sums = []
    for v, c in enumerate(centers):
        at = ref.at[v] if len(ref.shape) == 4 else ref
        sums.append(
            cxu * at[p + 1]
            + cxd * at[p - 1]
            + cyu * roll_rows(c, -1)
            + cyd * roll_rows(c, 1)
            + czr * roll_lanes(c, -lv.repeat)
            + czl * roll_lanes(c, lv.repeat)
        )
    return sums


def inside_rows(lv, n, narrow):
    rows = row_of(lv.rows) + (n * lv.own_rows - 8)
    return (rows >= 0) & (rows < lv.own_rows * narrow)


def inside(lv, in_rows, p, w, wide):
    if isinstance(p, int) and lv.first <= p < lv.first + lv.own:
        return in_rows
    at = w * lv.own + p - lv.first
    return in_rows & (at >= 0) & (at < lv.own * wide)


def pack2(lv, x, y):
    return jnp.where(lax.rem(lane_of(x.shape[0]) // (lv.repeat // 2), 2) == 0, x, y)


def unpack2(lv, xy):
    half = lv.repeat // 2
    first = lax.rem(lane_of(xy.shape[0]) // half, 2) == 0
    return jnp.where(first, xy, roll_lanes(xy, half)), jnp.where(first, roll_lanes(xy, -half), xy)


def coefficients(lv, f, in_rows, w, wide, lo, hi, unroll=99):
    lane = lane_of(lv.rows)
    last = lane >= LANES - lv.repeat
    edge = last | (lane < lv.repeat)
    f["cx"][lo - 1] = 0.5 * (f["k"][lo - 1] + f["k"][lo])

    def one(p):
        k = f["k"][p]
        cxu = 0.5 * (k + f["k"][p + 1])
        cxd = 0.5 * (k + f["k"][p - 1])
        cyu = 0.5 * (k + roll_rows(k, -1))
        cyd = roll_rows(cyu, 1)
        czr = jnp.where(last, 0.0, 0.5 * (k + roll_lanes(k, -lv.repeat)))
        czl = roll_lanes(czr, lv.repeat)
        d = MASS + (cxu + cxd + cyu + cyd + czr + czl + jnp.where(edge, 0.5 * k, 0.0))
        f["cx"][p] = cxu
        f["cyu"][p] = cyu
        f["cyd"][p] = cyd
        f["czr"][p] = czr
        f["czl"][p] = czl
        f["diag"][p] = d
        f["inv"][p] = jnp.where(inside(lv, in_rows, p, w, wide), 1.0 / d, 0.0)

    planes(lo, hi, one, unroll)


def restrict(lv, read, mix):
    for j in range(lv.own // 2):
        mix[j] = read(2 * j) + read(2 * j + 1)
    half = lv.own_rows // 2
    even = lax.rem(lane_of(half) // lv.repeat, 2) == 0
    found = []
    for j in range(lv.own // 2):
        x = mix[j, pl.ds(0, half, stride=2), :] + mix[j, pl.ds(1, half, stride=2), :]
        x = x + jnp.where(even, roll_lanes(x, -lv.repeat), roll_lanes(x, lv.repeat))
        found.append(0.125 * x)
    return found


def smooth_down(lv, f, steps, unroll=99):
    def first(p):
        hat = f["src"][p] * f["inv"][p]
        f["hat"][p] = hat
        f["upd"][p] = hat * (1.0 / THETA)

    def second(p):
        x = f["upd"][p]
        (s,) = near_sum(lv, f, f["upd"], p, [x])
        z = f["hat"][p] + f["inv"][p] * s - x
        f["tmp"][p] = x + (KEEP1 * x + GAIN1 * z)

    def third(p):
        x = f["tmp"][p]
        (s,) = near_sum(lv, f, f["tmp"], p, [x])
        z = f["hat"][p] + f["inv"][p] * s - x
        f["it"][p] = x + (KEEP2 * (x - f["upd"][p]) + GAIN2 * z)

    for step, ranges in zip((first, second, third), steps):
        for lo, hi in ranges:
            planes(lo, hi, step, unroll)


def sweep_up(lv, f, old, new, upd, lo, hi, keep, gain, with_source, own=None):
    for p in range(lo, hi):
        c = old[p]
        (t,) = near_sum(lv, f, old, p, [c])
        z = f["inv"][p] * t - c
        if with_source:
            z = z + f["hat"][p]
        u = gain * z if keep is None else keep * upd[p] + gain * z
        if own is None:
            upd[p] = u
            new[p] = c + u
        else:
            new[p, own] = (c + u)[own]


def smooth_up(lv, f, a, b, upd, lo, hi, with_source, own=None):
    sweep_up(lv, f, a, b, upd, lo + 1, hi - 1, None, 1.0 / THETA, with_source)
    sweep_up(lv, f, b, a, upd, lo + 2, hi - 2, KEEP1, GAIN1, with_source)
    sweep_up(lv, f, a, b, upd, lo + 3, hi - 3, KEEP2, GAIN2, with_source, own)


def solve4(m):
    small = m[1] < 0.5 * m[0]
    pick = lambda a, b: jnp.where(small, a, b)
    g = [pick(m[k + 1], m[8 + k] - m[9 + k]) for k in range(7)]
    rhs = [pick(m[k], m[8 + k]) for k in range(4)]
    rows = [[g[i + j] for j in range(4)] for i in range(4)]
    inv = []
    for i in range(4):
        piv = rows[i][i]
        good = piv > 1e-7 * g[2 * i]
        inv.append(jnp.where(good, 1.0 / jnp.where(good, piv, 1.0), 0.0))
        for r in range(i + 1, 4):
            factor = rows[i][r] * inv[i]
            rows[r] = [rows[r][j] - factor * rows[i][j] if j >= r else None for j in range(4)]
            rhs[r] = rhs[r] - factor * rhs[i]
    y = [None] * 4
    for i in (3, 2, 1, 0):
        t = rhs[i]
        for j in range(i + 1, 4):
            t = t - rows[i][j] * y[j]
        y[i] = t * inv[i]
    turned = [
        y[0] + y[1] + y[2] + y[3],
        -(y[1] + 2.0 * y[2] + 3.0 * y[3]),
        y[2] + 3.0 * y[3],
        -y[3],
    ]
    return [pick(a, b) for a, b in zip(y, turned)]


def halo(reach):
    return [(dw, dn) for dn in (1, -1, 0) for dw in reach if (dw, dn) != (0, 0)]


NEAR_MID, FAR_MID = halo((1, -1, 0)), halo((2, -2))
NEAR_COARSE, FAR_COARSE = halo((1, -1, 0, 2, -2)), halo((3, -3))
HALO_FINE = halo((1, -1, 0))


def kernel(wide, narrow, names, heat, cond, out, *refs):
    s = dict(zip(names, refs))
    w, n = lax.axis_index("wide"), lax.axis_index("narrow")
    z, ylo, core = w // 4, lax.rem(w // 2, 2), lax.rem(w, 2)
    yhi, x = n // 4, lax.rem(n, 4)
    stacks = wide // 4

    f0 = {k: s["f0_" + k] for k in FIELDS}
    f1 = {k: s["f1_" + k] for k in FIELDS}
    f2 = {k: s["f2_" + k] for k in FIELDS if "f2_" + k in s}

    def near(dw, dn):
        return (lax.rem(w + (dw + wide), wide), lax.rem(n + (dn + narrow), narrow))

    def stack(dz):
        return (lax.rem(w + (4 * dz + wide), wide), n)

    def plane_peer(dx, dhi, dlo, dc):
        to = z * 4 + lax.rem(ylo + dlo, 2) * 2 + lax.rem(core + dc, 2)
        return (to, lax.rem(yhi + dhi, 2) * 4 + lax.rem(x + dx, 4))

    plane_peers = [
        plane_peer(*d)
        for d in sorted(
            [(dx, dhi, dlo, dc) for dx in range(4) for dhi in range(2) for dlo in range(2) for dc in range(2)],
            key=lambda d: -min(d[0], 4 - d[0]) - (1 if d[2] else 2 * d[1]),
        )
        if any(d)
    ]
    stack_peers = [stack(d) for d in sorted(range(1, stacks), key=lambda d: -min(d, stacks - d))]

    barrier = pltpu.get_barrier_semaphore()
    greeted = HALO_FINE + [d for d in NEAR_COARSE + FAR_COARSE if d not in HALO_FINE] + [(8, 0), (-8, 0), (4, 0), (-4, 0)]
    for d in greeted:
        pl.semaphore_signal(barrier, inc=1, device_id=near(*d), device_id_type=MESH)
    own_heat = pltpu.make_async_copy(heat, f0["src"].at[4:12, 8:40], s["local_sem"].at[0])
    own_cond = pltpu.make_async_copy(cond, f0["k"].at[4:12, 8:40], s["local_sem"].at[1])
    own_cond.start()
    own_heat.start()
    share = {k: s["share_" + k] for k in ("src", "hat", "upd", "tmp", "it", "res")}
    for ref in share.values():
        ref[4:16] = jnp.zeros((12, 32, LANES), F32)

    used = [0]
    sent = []

    def send(src, dst, peer):
        i = used[0]
        used[0] += 1
        copy = pltpu.make_async_remote_copy(
            src_ref=src,
            dst_ref=dst,
            send_sem=s["send_sem"].at[i],
            recv_sem=s["recv_sem"].at[i],
            device_id=peer,
            device_id_type=MESH,
        )
        copy.start()
        sent.append(copy)
        return copy

    def send_rows(ref_from, ref_to, first, own, own_rows, reach, depth):
        copies = []
        for dw, dn in reach:
            a, c, b = first, own, first - dw * own
            if depth < own and dw:
                a, b = (first + own - depth, first - depth) if dw > 0 else (first, first + own)
                c = depth
            ra, rc, rb = (8, own_rows, 8) if dn == 0 else (own_rows, 8, 0) if dn > 0 else (8, 8, 8 + own_rows)
            copies.append(
                send(ref_from.at[a : a + c, ra : ra + rc], ref_to.at[b : b + c, rb : rb + rc], near(dw, dn))
            )
        return copies

    def send_mid(ref, reach):
        return send_rows(ref, ref, 4, 2, 16, reach, 2)

    def send_coarse(ref, reach):
        return send_rows(ref, ref, 3, 1, 8, reach, 1)

    def arrive(copies):
        for c in copies:
            c.wait_recv()

    tokens = [s["token0"], s["token1"], s["token2"]]
    heard = [[stack(2), stack(-2)], [stack(4), stack(-4)], [near(0, 2), near(0, -2)]]

    def pass_token(i):
        for peer in heard[i]:
            pl.semaphore_signal(tokens[i], inc=1, device_id=peer, device_id_type=MESH)

    def take_token(i):
        pl.semaphore_wait(tokens[i], 2)

    own_cond.wait()
    own_heat.wait()
    low4 = row_of(8) < 4
    pack, got = s["pack"], s["got"]

    def pack_plane(p):
        h, c = f0["src"][p + 4, 32:40], f0["k"][p + 4, 32:40]
        pack[0, p] = jnp.where(low4, roll_rows(h, 4), c)
        h, c = f0["src"][p + 4, 8:16], f0["k"][p + 4, 8:16]
        pack[1, p] = jnp.where(low4, c, roll_rows(h, 4))

    planes(0, 8, pack_plane, 8)
    pl.semaphore_wait(barrier, len(greeted))
    first = [
        send(pack.at[0, 4:8], got.at[0, 0:4], near(1, 1)),
        send(pack.at[1, 4:8], got.at[1, 0:4], near(1, -1)),
        send(pack.at[0, 0:4], got.at[0, 12:16], near(-1, 1)),
        send(pack.at[1, 0:4], got.at[1, 12:16], near(-1, -1)),
        send(cond.at[4:8], f0["k"].at[0:4, 8:40], near(1, 0)),
        send(cond.at[0:4], f0["k"].at[12:16, 8:40], near(-1, 0)),
        send(pack.at[0], got.at[0, 4:12], near(0, 1)),
        send(pack.at[1], got.at[1, 4:12], near(0, -1)),
        send(heat.at[5:8], f0["src"].at[1:4, 8:40], near(1, 0)),
        send(heat.at[0:3], f0["src"].at[12:15, 8:40], near(-1, 0)),
    ]

    k1p, k2p, s1p, z2p = s["k1p"], s["k2p"], s["s1p"], s["z2p"]
    one_up = restrict(FINE, lambda p: f0["k"][4 + p, 8:40], s["mix0"])
    two_up = restrict(MID, lambda p: one_up[p], s["mix1"])
    for j in range(2):
        k1p[4 + j, 8:24] = pack2(MID, one_up[2 * j], one_up[2 * j + 1])
    k2p[3, 8:16] = pack2(COARSE, two_up[0], two_up[1])

    cond1 = send_mid(k1p, NEAR_MID)
    cond2 = send_coarse(k2p, NEAR_COARSE + FAR_COARSE)
    in0, in1, in2 = (inside_rows(lv, n, narrow) for lv in (FINE, MID, COARSE))

    def unpack_cond(lv, packed, f, in_rows, p):
        for k, v in enumerate(unpack2(lv, packed[p])):
            ok = inside(lv, in_rows, 2 * p + k, w, wide)
            f["k"][2 * p + k] = jnp.where(ok, v * lv.scale, 0.0)

    arrive(first[:8])
    pass_token(0)
    pass_token(2)

    in_low, in_high = in0[0:8] & ~low4, in0[40:48] & low4

    def unpack(p):
        f0["k"][p, 0:8] = jnp.where(in_low, got[0, p], 0.0)
        f0["k"][p, 40:48] = jnp.where(in_high, got[1, p], 0.0)
        f0["src"][p, 0:8] = roll_rows(got[0, p], 4)
        f0["src"][p, 40:48] = roll_rows(got[1, p], 4)
        if not 4 <= p < 12:
            at = w * 8 + p - 4
            f0["k"][p] = jnp.where((at >= 0) & (at < 8 * wide), f0["k"][p], 0.0)

    planes(0, 16, unpack)
    coefficients(FINE, f0, in0, w, wide, 1, 15)
    arrive(first[8:])
    arrive(cond1)
    for p in range(2, 8):
        unpack_cond(MID, k1p, f1, in1, p)
    coefficients(MID, f1, in1, w, wide, 5, 15)
    smooth_down(FINE, f0, ([(1, 15)], [(2, 14)], [(3, 13)]))

    def residual(lv, f, unroll):
        own = slice(8, 8 + lv.own_rows)

        def one(p):
            x = f["it"][p]
            (t,) = near_sum(lv, f, f["it"], p, [x])
            f["res"][p, own] = (f["src"][p] + t - f["diag"][p] * x)[own]

        planes(lv.first, lv.first + lv.own, one, unroll)

    residual(FINE, f0, 8)
    r1 = restrict(FINE, lambda p: f0["res"][4 + p, 8:40], s["mix0"])
    for j in range(2):
        s1p[4 + j, 8:24] = pack2(MID, r1[2 * j], r1[2 * j + 1])

    for j in range(4):
        p, own = MID.first + j, slice(8, 24)
        hat = r1[j] * f1["inv"][p, own]
        share["src"][p, own] = r1[j]
        share["hat"][p, own] = hat
        share["upd"][p, own] = hat * (1.0 / THETA)
    sf = dict(f1, **share)
    smooth_down(MID, sf, ([], [(7, 13)], [(6, 14)]))
    for p in range(5, 15):
        v = sf["it"][p]
        (t,) = near_sum(MID, f1, sf["it"], p, [v])
        v = sf["src"][p] + t - f1["diag"][p] * v
        sf["res"][p] = v if 8 <= p < 12 else jnp.where(f1["inv"][p] > 0.0, v, 0.0)
    for p in range(8, 12):
        for tile in (slice(0, 8), slice(24, 32)):
            sf["res"][p, tile] = jnp.where(f1["inv"][p, tile] > 0.0, sf["res"][p, tile], 0.0)
    mix2 = s["mix2"]
    lane16 = lax.rem(lane_of(16), 4)
    part = []
    for j in range(6):
        mix2[j] = sf["res"][4 + 2 * j] + sf["res"][5 + 2 * j]
    for j in range(6):
        v = mix2[j, pl.ds(0, 16, stride=2), :] + mix2[j, pl.ds(1, 16, stride=2), :]
        part.append(0.125 * (v + jnp.where(lane16 < 2, roll_lanes(v, -2), roll_lanes(v, 2))))
    ct, cr = s["ct"], s["cr"]
    for i in range(2):
        a, b, c, d = part[2 * i : 2 * i + 4]
        ct[i] = jnp.where(lane16 < 2, jnp.where(lane16 == 0, a, b), jnp.where(lane16 == 2, c, d))

    def slot(dw, dn):
        return (dw + 3) * 3 + dn + 1

    parts = []
    for dw, dn in NEAR_COARSE + FAR_COARSE:
        to = cr.at[slot(-dw, -dn)]
        which = pl.ds(1, 1) if dw >= 2 else pl.ds(0, 1) if dw <= -2 else pl.ds(0, 2)
        parts.append(send(ct.at[which], to.at[which], near(dw, dn)))
    src1 = send_mid(s1p, NEAR_MID)
    its = send_rows(f0["it"], s["edge"], 4, 8, 32, HALO_FINE, 3)
    src1_far = send_mid(s1p, FAR_MID)
    cond1_far = send_mid(k1p, FAR_MID)
    arrive(cond2)
    for p in range(7):
        unpack_cond(COARSE, k2p, f2, in2, p)
    coefficients(COARSE, f2, in2, w, wide, 1, 13)

    def unpack_src(p):
        f1["src"][2 * p], f1["src"][2 * p + 1] = unpack2(MID, s1p[p])

    arrive(parts)
    take_token(0)
    take_token(2)
    pass_token(1)
    u = s["basis"]

    def unpack_z(p):
        for k, v in enumerate(unpack2(COARSE, z2p[p])):
            u[0, 2 * p + k] = jnp.where(inside(COARSE, in2, 2 * p + k, w, wide), v, 0.0)

    def apply_b(k, p):
        v = u[k, p]
        (t,) = near_sum(COARSE, f2, u.at[k], p, [v])
        u[k + 1, p] = v - f2["inv"][p] * t

    lane8 = lane_of(8)
    head = lax.rem(lane8, 4) < 2
    bonds = {j: [None] * 4 for j in range(-3, 3)}

    def gain_of(j, dn, v, keep=None):
        for i in range(2):
            x = v[8 * i : 8 * i + 8]
            if keep is not None:
                x = jnp.where(keep, x, 0.0)
            at = dn + 1 + i
            bonds[j][at] = x if bonds[j][at] is None else bonds[j][at] + x

    for dn in (-1, 0, 1):
        lo = {d: cr.at[slot(d, dn), 0] for d in (-1, 0, 1, 2, 3)}
        hi = {d: cr.at[slot(d, dn), 1] for d in (-3, -2, -1, 0, 1)}
        if dn == 0:
            lo[0], hi[0] = ct.at[0], ct.at[1]
        gain_of(-3, dn, hi[-3][...])
        gain_of(-2, dn, hi[-2][...])
        gain_of(-2, dn, lo[-1][...], head)
        gain_of(-1, dn, hi[-1][...])
        gain_of(-1, dn, lo[0][...])
        gain_of(0, dn, lo[1][...])
        gain_of(0, dn, hi[0][...], ~head)
        gain_of(1, dn, lo[2][...])
        gain_of(1, dn, hi[1][...], ~head)
        gain_of(2, dn, lo[3][...])
    frame = s["frame"]
    for j in range(-2, 3):
        for i in range(4):
            v = jnp.where(head, bonds[j][i], bonds[j - 1][i])
            v = v + jnp.where(head, roll_lanes(v, -2), roll_lanes(v, 2))
            pair = unpack2(MID, v)
            for k in range(2):
                frame[j + 2, k, 8 * i : 8 * i + 8] = pair[k]
    for j in range(-2, 3):
        for k in range(2):
            p = 6 + 2 * j + k
            u[0, p] = roll_rows(frame[j + 2, k], -4)[0:24] * f2["inv"][p]
    z2p[3, 8:16] = pack2(COARSE, u[0, 6, 8:16], u[0, 7, 8:16])
    for k in range(4):
        for p in range(3 + k, 11 - k):
            apply_b(k, p)

    row8 = row_of(8)
    sums = [jnp.zeros((8, LANES), F32) for _ in range(16)]
    for p in (6, 7):
        d = f2["diag"][p, 8:16]
        b = [u[k, p, 8:16] for k in range(5)]
        c = [
            b[0],
            b[0] - b[1],
            b[0] - 2.0 * b[1] + b[2],
            b[0] - 3.0 * (b[1] - b[2]) - b[3],
            b[0] - 4.0 * (b[1] + b[3]) + 6.0 * b[2] + b[4],
        ]
        for at, vs in ((0, b), (8, c)):
            for k in range(8):
                sums[at + k] = sums[at + k] + vs[k // 2] * d * vs[(k + 1) // 2]
    tiles = []
    for half in (0, 8):
        m = jnp.zeros((8, LANES), F32)
        for k in range(8):
            m = jnp.where(row8 == k, jnp.sum(sums[half + k], axis=0, keepdims=True), m)
        tiles.append(jnp.sum(m, axis=1, keepdims=True))
    spread = jnp.where(lane8 == row8, tiles[0], 0.0) + jnp.where(lane8 == row8 + 8, tiles[1], 0.0)
    mine, all1, all2 = s["mine"], s["all1"], s["all2"]
    mine[0] = jnp.sum(spread, axis=0, keepdims=True)
    rank = lax.rem(w, 4) * narrow + n
    all1[rank] = mine[0]

    def send_sum(src, dst, peers, at, stage):
        copies = []
        for i, peer in enumerate(peers):
            copy = pltpu.make_async_remote_copy(
                src_ref=src,
                dst_ref=dst,
                send_sem=s["sum_send"].at[at + i],
                recv_sem=s["sum_recv"].at[stage],
                device_id=peer,
                device_id_type=MESH,
            )
            copy.start()
            copies.append(copy)
        return copies

    sums1 = send_sum(mine.at[0], all1.at[rank], plane_peers, 0, 0)
    z2_far = send_coarse(z2p, FAR_COARSE)

    arrive(cond1_far + src1 + src1_far)
    for p in (0, 1, 8, 9):
        unpack_cond(MID, k1p, f1, in1, p)
    for p in range(10):
        unpack_src(p)
    coefficients(MID, f1, in1, w, wide, 1, 5)
    coefficients(MID, f1, in1, w, wide, 15, 19)
    smooth_down(MID, f1, ([(1, 19)], [(2, 18)], [(3, 17)]))

    xa, xb, xe = s["mid_a"], s["mid_b"], s["mid_e"]
    ya, yb, ye = s["fine_a"], s["fine_b"], s["fine_e"]
    edge = s["edge"]

    def up_fine(v, with_source):
        for p in range(1, 15):
            t = xb[v, p // 2 + 6, 4:28]
            ya[v, p, pl.ds(0, 24, stride=2), :] = t
            ya[v, p, pl.ds(1, 24, stride=2), :] = t
        if with_source:
            for p in range(1, 15):
                ya[v, p] = ya[v, p] + jnp.where(f0["inv"][p] > 0.0, edge[p], 0.0)
        smooth_up(FINE, f0, ya.at[v], yb.at[v], ye.at[v], 1, 15, with_source, slice(8, 40))

    arrive(its)
    for p in range(4, 12):
        edge[p, 8:40] = f0["it"][p, 8:40]
    for p in range(3, 17):
        xa[0, p] = f1["it"][p]
    smooth_up(MID, f1, xa.at[0], xb.at[0], xe.at[0], 3, 17, True)
    up_fine(0, True)
    others = all1.at[pl.ds(0, len(plane_peers))]
    pltpu.make_async_copy(others, others, s["sum_recv"].at[0]).wait()
    mine[1] = jnp.sum(all1[...], axis=0)
    all2[z] = mine[1]
    take_token(1)
    sums2 = send_sum(mine.at[1], all2.at[z], stack_peers, len(plane_peers), 1)
    arrive(z2_far)
    for p in (0, 6):
        unpack_z(p)
    for k in range(3):
        for p in (1 + k, 2 + k, 11 - k, 12 - k):
            apply_b(k, p)

    def up_basis(k, carry):
        v = k + 1
        for p in range(3, 17):
            t = u[k, p // 2 + 2, 4:20]
            xa[v, p, pl.ds(0, 16, stride=2), :] = t
            xa[v, p, pl.ds(1, 16, stride=2), :] = t
        smooth_up(MID, f1, xa.at[v], xb.at[v], xe.at[v], 3, 17, False)
        up_fine(v, False)
        return carry

    lax.fori_loop(0, 4, up_basis, 0)
    for c in sent + sums1:
        c.wait_send()
    others = all2.at[pl.ds(0, len(stack_peers))]
    pltpu.make_async_copy(others, others, s["sum_recv"].at[1]).wait()
    total = jnp.broadcast_to(jnp.sum(all2[...], axis=0), (8, LANES))
    ta = jnp.sum(jnp.where(lane8 == row8, total, 0.0), axis=1, keepdims=True)
    tb = jnp.sum(jnp.where(lane8 == row8 + 8, total, 0.0), axis=1, keepdims=True)
    ta, tb = jnp.broadcast_to(ta, (8, LANES)), jnp.broadcast_to(tb, (8, LANES))
    y = solve4([ta[k : k + 1] for k in range(8)] + [tb[k : k + 1] for k in range(8)])

    def combine(p):
        v = yb[0, p + 4, 8:40]
        for k in range(4):
            v = v + y[k] * yb[1 + k, p + 4, 8:40]
        out[p] = v

    planes(0, 8, combine)
    for c in sums2:
        c.wait_send()


def solution(mesh):
    wide, narrow = mesh.shape["wide"], mesh.shape["narrow"]

    def field(lv, *lead):
        return pltpu.VMEM((*lead, lv.planes, lv.rows, LANES), F32)

    scratch = {}
    for tag, lv in (("f0_", FINE), ("f1_", MID)):
        for k in FIELDS:
            scratch[tag + k] = field(lv)
    for k in ("k", "cx", "cyu", "cyd", "czr", "czl", "inv", "diag"):
        scratch["f2_" + k] = field(COARSE)
    scratch["basis"] = field(COARSE, 5)
    scratch["edge"] = field(FINE)
    for k in ("a", "b", "e"):
        scratch["mid_" + k] = field(MID, 5)
        scratch["fine_" + k] = field(FINE, 5)
    scratch["pack"] = pltpu.VMEM((2, 8, 8, LANES), F32)
    scratch["got"] = pltpu.VMEM((2, 16, 8, LANES), F32)
    scratch["mix0"] = pltpu.VMEM((4, 32, LANES), F32)
    scratch["mix1"] = pltpu.VMEM((2, 16, LANES), F32)
    for k in ("k1p", "s1p"):
        scratch[k] = pltpu.VMEM((10, 32, LANES), F32)
    for k in ("k2p", "z2p"):
        scratch[k] = pltpu.VMEM((7, 24, LANES), F32)
    scratch["mine"] = pltpu.VMEM((2, 1, LANES), F32)
    scratch["all1"] = pltpu.VMEM((4 * narrow, 1, LANES), F32)
    scratch["all2"] = pltpu.VMEM((wide // 4, 1, LANES), F32)
    for k in ("src", "hat", "upd", "tmp", "it", "res"):
        scratch["share_" + k] = field(MID)
    scratch["mix2"] = pltpu.VMEM((6, 32, LANES), F32)
    scratch["ct"] = pltpu.VMEM((2, 16, LANES), F32)
    scratch["cr"] = pltpu.VMEM((21, 2, 16, LANES), F32)
    scratch["frame"] = pltpu.VMEM((5, 2, 32, LANES), F32)
    messages = 10 + len(HALO_FINE) + 2 * len(NEAR_MID + FAR_MID + NEAR_COARSE) + 3 * len(FAR_COARSE)
    scratch["send_sem"] = pltpu.SemaphoreType.DMA((messages,))
    scratch["recv_sem"] = pltpu.SemaphoreType.DMA((messages,))
    scratch["sum_send"] = pltpu.SemaphoreType.DMA((4 * narrow + wide // 4,))
    scratch["sum_recv"] = pltpu.SemaphoreType.DMA((2,))
    scratch["local_sem"] = pltpu.SemaphoreType.DMA((2,))
    for i in range(3):
        scratch[f"token{i}"] = pltpu.SemaphoreType.REGULAR

    def body(heat, cond):
        heat = pltpu.with_memory_space_constraint(heat, pltpu.HBM)
        cond = pltpu.with_memory_space_constraint(cond, pltpu.HBM)
        return pl.pallas_call(
            functools.partial(kernel, wide, narrow, tuple(scratch)),
            out_shape=pltpu.VMEM((8, 32, LANES), F32),
            in_specs=[pl.BlockSpec(memory_space=pltpu.HBM)] * 2,
            out_specs=pl.BlockSpec(memory_space=pltpu.VMEM),
            scratch_shapes=list(scratch.values()),
            compiler_params=pltpu.CompilerParams(
                collective_id=0, has_side_effects=True, vmem_limit_bytes=40 * 2**20
            ),
            cost_estimate=pl.CostEstimate(flops=50_000_000, bytes_accessed=400_000, transcendentals=0),
            name="vcycle",
        )(heat, cond)

    spec = P("wide", "narrow", None)
    return jax.shard_map(body, mesh=mesh, in_specs=(spec, spec), out_specs=spec, check_vma=False)
```

```python
import functools
import jax
import jax.numpy as jnp
from jax import lax
from jax.experimental import pallas as pl
from jax.experimental.pallas import tpu as pltpu
from jax.sharding import PartitionSpec as P

MASS = 0.002
LOW, HIGH = 0.25, 2.0
THETA = 0.5 * (HIGH + LOW)
DELTA = 0.5 * (HIGH - LOW)
SIGMA = THETA / DELTA
RHO1 = 1.0 / SIGMA
RHO2 = 1.0 / (2.0 * SIGMA - RHO1)
RHO3 = 1.0 / (2.0 * SIGMA - RHO2)
KEEP1, GAIN1 = RHO2 * RHO1, 2.0 * RHO2 / DELTA
KEEP2, GAIN2 = RHO3 * RHO2, 2.0 * RHO3 / DELTA
F32 = jnp.float32
LANES = 128
MESH = pl.DeviceIdType.MESH


class Level:
    def __init__(self, planes, first, own, rows, own_rows, repeat, scale):
        self.planes, self.first, self.own = planes, first, own
        self.rows, self.own_rows, self.repeat, self.scale = rows, own_rows, repeat, scale


FINE = Level(16, 4, 8, 48, 32, 1, 1.0)
MID = Level(20, 8, 4, 32, 16, 2, 0.25)
COARSE = Level(14, 6, 2, 24, 8, 4, 1.0 / 16.0)

FIELDS = ("k", "cx", "cyu", "cyd", "czr", "czl", "inv", "diag", "src", "hat", "upd", "it", "tmp", "res")


def planes(lo, hi, fn, unroll=99):
    count = hi - lo
    unroll = min(unroll, count)
    while count % unroll:
        unroll -= 1
    if unroll == count:
        for p in range(lo, hi):
            fn(p)
        return

    def step(i, carry):
        for k in range(unroll):
            fn(lo + i * unroll + k)
        return carry

    lax.fori_loop(0, count // unroll, step, 0)


def roll_rows(x, by):
    return pltpu.roll(x, by % x.shape[0], 0)


def roll_lanes(x, by):
    return pltpu.roll(x, by % LANES, 1)


def lane_of(rows):
    return lax.broadcasted_iota(jnp.int32, (rows, LANES), 1)


def row_of(rows):
    return lax.broadcasted_iota(jnp.int32, (rows, LANES), 0)


def near_sum(lv, f, ref, p, centers):
    cxu, cxd = f["cx"][p], f["cx"][p - 1]
    cyu, cyd, czr, czl = f["cyu"][p], f["cyd"][p], f["czr"][p], f["czl"][p]
    sums = []
    for v, c in enumerate(centers):
        at = ref.at[v] if len(ref.shape) == 4 else ref
        sums.append(
            cxu * at[p + 1]
            + cxd * at[p - 1]
            + cyu * roll_rows(c, -1)
            + cyd * roll_rows(c, 1)
            + czr * roll_lanes(c, -lv.repeat)
            + czl * roll_lanes(c, lv.repeat)
        )
    return sums


def inside_rows(lv, n, narrow):
    rows = row_of(lv.rows) + (n * lv.own_rows - 8)
    return (rows >= 0) & (rows < lv.own_rows * narrow)


def inside(lv, in_rows, p, w, wide):
    if isinstance(p, int) and lv.first <= p < lv.first + lv.own:
        return in_rows
    at = w * lv.own + p - lv.first
    return in_rows & (at >= 0) & (at < lv.own * wide)


def pack2(lv, x, y):
    return jnp.where(lax.rem(lane_of(x.shape[0]) // (lv.repeat // 2), 2) == 0, x, y)


def unpack2(lv, xy):
    half = lv.repeat // 2
    first = lax.rem(lane_of(xy.shape[0]) // half, 2) == 0
    return jnp.where(first, xy, roll_lanes(xy, half)), jnp.where(first, roll_lanes(xy, -half), xy)


def coefficients(lv, f, in_rows, w, wide, lo, hi, unroll=99):
    lane = lane_of(lv.rows)
    last = lane >= LANES - lv.repeat
    edge = last | (lane < lv.repeat)
    f["cx"][lo - 1] = 0.5 * (f["k"][lo - 1] + f["k"][lo])

    def one(p):
        k = f["k"][p]
        cxu = 0.5 * (k + f["k"][p + 1])
        cxd = 0.5 * (k + f["k"][p - 1])
        cyu = 0.5 * (k + roll_rows(k, -1))
        cyd = roll_rows(cyu, 1)
        czr = jnp.where(last, 0.0, 0.5 * (k + roll_lanes(k, -lv.repeat)))
        czl = roll_lanes(czr, lv.repeat)
        d = MASS + (cxu + cxd + cyu + cyd + czr + czl + jnp.where(edge, 0.5 * k, 0.0))
        f["cx"][p] = cxu
        f["cyu"][p] = cyu
        f["cyd"][p] = cyd
        f["czr"][p] = czr
        f["czl"][p] = czl
        f["diag"][p] = d
        f["inv"][p] = jnp.where(inside(lv, in_rows, p, w, wide), 1.0 / d, 0.0)

    planes(lo, hi, one, unroll)


def restrict(lv, read, mix):
    for j in range(lv.own // 2):
        mix[j] = read(2 * j) + read(2 * j + 1)
    half = lv.own_rows // 2
    even = lax.rem(lane_of(half) // lv.repeat, 2) == 0
    found = []
    for j in range(lv.own // 2):
        x = mix[j, pl.ds(0, half, stride=2), :] + mix[j, pl.ds(1, half, stride=2), :]
        x = x + jnp.where(even, roll_lanes(x, -lv.repeat), roll_lanes(x, lv.repeat))
        found.append(0.125 * x)
    return found


def smooth_down(lv, f, steps, unroll=99):
    def first(p):
        hat = f["src"][p] * f["inv"][p]
        f["hat"][p] = hat
        f["upd"][p] = hat * (1.0 / THETA)

    def second(p):
        x = f["upd"][p]
        (s,) = near_sum(lv, f, f["upd"], p, [x])
        z = f["hat"][p] + f["inv"][p] * s - x
        f["tmp"][p] = x + (KEEP1 * x + GAIN1 * z)

    def third(p):
        x = f["tmp"][p]
        (s,) = near_sum(lv, f, f["tmp"], p, [x])
        z = f["hat"][p] + f["inv"][p] * s - x
        f["it"][p] = x + (KEEP2 * (x - f["upd"][p]) + GAIN2 * z)

    for step, ranges in zip((first, second, third), steps):
        for lo, hi in ranges:
            planes(lo, hi, step, unroll)


def sweep_up(lv, f, old, new, upd, lo, hi, keep, gain, with_source, own=None):
    for p in range(lo, hi):
        c = old[p]
        (t,) = near_sum(lv, f, old, p, [c])
        z = f["inv"][p] * t - c
        if with_source:
            z = z + f["hat"][p]
        u = gain * z if keep is None else keep * upd[p] + gain * z
        if own is None:
            upd[p] = u
            new[p] = c + u
        else:
            new[p, own] = (c + u)[own]


def smooth_up(lv, f, a, b, upd, lo, hi, with_source, own=None):
    sweep_up(lv, f, a, b, upd, lo + 1, hi - 1, None, 1.0 / THETA, with_source)
    sweep_up(lv, f, b, a, upd, lo + 2, hi - 2, KEEP1, GAIN1, with_source)
    sweep_up(lv, f, a, b, upd, lo + 3, hi - 3, KEEP2, GAIN2, with_source, own)


def solve4(m):
    small = m[1] < 0.5 * m[0]
    pick = lambda a, b: jnp.where(small, a, b)
    g = [pick(m[k + 1], m[8 + k] - m[9 + k]) for k in range(7)]
    rhs = [pick(m[k], m[8 + k]) for k in range(4)]
    rows = [[g[i + j] for j in range(4)] for i in range(4)]
    inv = []
    for i in range(4):
        piv = rows[i][i]
        good = piv > 1e-7 * g[2 * i]
        inv.append(jnp.where(good, 1.0 / jnp.where(good, piv, 1.0), 0.0))
        for r in range(i + 1, 4):
            factor = rows[i][r] * inv[i]
            rows[r] = [rows[r][j] - factor * rows[i][j] if j >= r else None for j in range(4)]
            rhs[r] = rhs[r] - factor * rhs[i]
    y = [None] * 4
    for i in (3, 2, 1, 0):
        t = rhs[i]
        for j in range(i + 1, 4):
            t = t - rows[i][j] * y[j]
        y[i] = t * inv[i]
    turned = [
        y[0] + y[1] + y[2] + y[3],
        -(y[1] + 2.0 * y[2] + 3.0 * y[3]),
        y[2] + 3.0 * y[3],
        -y[3],
    ]
    return [pick(a, b) for a, b in zip(y, turned)]


def halo(reach):
    return [(dw, dn) for dn in (1, -1, 0) for dw in reach if (dw, dn) != (0, 0)]


NEAR_MID, FAR_MID = halo((1, -1, 0)), halo((2, -2))
NEAR_COARSE, FAR_COARSE = halo((1, -1, 0, 2, -2)), halo((3, -3))
HALO_FINE = halo((1, -1, 0))


def kernel(wide, narrow, names, heat, cond, out, *refs):
    s = dict(zip(names, refs))
    w, n = lax.axis_index("wide"), lax.axis_index("narrow")
    z, ylo, core = w // 4, lax.rem(w // 2, 2), lax.rem(w, 2)
    yhi, x = n // 4, lax.rem(n, 4)
    stacks = wide // 4

    f0 = {k: s["f0_" + k] for k in FIELDS}
    f1 = {k: s["f1_" + k] for k in FIELDS}
    f2 = {k: s["f2_" + k] for k in FIELDS if "f2_" + k in s}

    def near(dw, dn):
        return (lax.rem(w + (dw + wide), wide), lax.rem(n + (dn + narrow), narrow))

    def stack(dz):
        return (lax.rem(w + (4 * dz + wide), wide), n)

    def plane_peer(dx, dhi, dlo, dc):
        to = z * 4 + lax.rem(ylo + dlo, 2) * 2 + lax.rem(core + dc, 2)
        return (to, lax.rem(yhi + dhi, 2) * 4 + lax.rem(x + dx, 4))

    plane_peers = [
        plane_peer(*d)
        for d in sorted(
            [(dx, dhi, dlo, dc) for dx in range(4) for dhi in range(2) for dlo in range(2) for dc in range(2)],
            key=lambda d: -min(d[0], 4 - d[0]) - (1 if d[2] else 2 * d[1]),
        )
        if any(d)
    ]
    stack_peers = [stack(d) for d in sorted(range(1, stacks), key=lambda d: -min(d, stacks - d))]

    barrier = pltpu.get_barrier_semaphore()
    greeted = HALO_FINE + [d for d in NEAR_COARSE + FAR_COARSE if d not in HALO_FINE] + [(8, 0), (-8, 0), (4, 0), (-4, 0)]
    for d in greeted:
        pl.semaphore_signal(barrier, inc=1, device_id=near(*d), device_id_type=MESH)
    own_heat = pltpu.make_async_copy(heat, f0["src"].at[4:12, 8:40], s["local_sem"].at[0])
    own_cond = pltpu.make_async_copy(cond, f0["k"].at[4:12, 8:40], s["local_sem"].at[1])
    own_cond.start()
    own_heat.start()
    share = {k: s["share_" + k] for k in ("src", "hat", "upd", "tmp", "it", "res")}
    for ref in share.values():
        ref[4:16] = jnp.zeros((12, 32, LANES), F32)

    used = [0]
    sent = []

    def send(src, dst, peer):
        i = used[0]
        used[0] += 1
        copy = pltpu.make_async_remote_copy(
            src_ref=src,
            dst_ref=dst,
            send_sem=s["send_sem"].at[i],
            recv_sem=s["recv_sem"].at[i],
            device_id=peer,
            device_id_type=MESH,
        )
        copy.start()
        sent.append(copy)
        return copy

    def send_rows(ref_from, ref_to, first, own, own_rows, reach, depth):
        copies = []
        for dw, dn in reach:
            a, c, b = first, own, first - dw * own
            if depth < own and dw:
                a, b = (first + own - depth, first - depth) if dw > 0 else (first, first + own)
                c = depth
            ra, rc, rb = (8, own_rows, 8) if dn == 0 else (own_rows, 8, 0) if dn > 0 else (8, 8, 8 + own_rows)
            copies.append(
                send(ref_from.at[a : a + c, ra : ra + rc], ref_to.at[b : b + c, rb : rb + rc], near(dw, dn))
            )
        return copies

    def send_mid(ref, reach):
        return send_rows(ref, ref, 4, 2, 16, reach, 2)

    def send_coarse(ref, reach):
        return send_rows(ref, ref, 3, 1, 8, reach, 1)

    def arrive(copies):
        for c in copies:
            c.wait_recv()

    tokens = [s["token0"], s["token1"], s["token2"]]
    heard = [[stack(2), stack(-2)], [stack(4), stack(-4)], [near(0, 2), near(0, -2)]]

    def pass_token(i):
        for peer in heard[i]:
            pl.semaphore_signal(tokens[i], inc=1, device_id=peer, device_id_type=MESH)

    def take_token(i):
        pl.semaphore_wait(tokens[i], 2)

    own_cond.wait()
    own_heat.wait()
    low4 = row_of(8) < 4
    pack, got = s["pack"], s["got"]

    def pack_plane(p):
        h, c = f0["src"][p + 4, 32:40], f0["k"][p + 4, 32:40]
        pack[0, p] = jnp.where(low4, roll_rows(h, 4), c)
        h, c = f0["src"][p + 4, 8:16], f0["k"][p + 4, 8:16]
        pack[1, p] = jnp.where(low4, c, roll_rows(h, 4))

    planes(0, 8, pack_plane, 8)
    k1p, k2p, s1p, z2p = s["k1p"], s["k2p"], s["s1p"], s["z2p"]
    one_up = restrict(FINE, lambda p: f0["k"][4 + p, 8:40], s["mix0"])
    two_up = restrict(MID, lambda p: one_up[p], s["mix1"])
    for j in range(2):
        k1p[4 + j, 8:24] = pack2(MID, one_up[2 * j], one_up[2 * j + 1])
    k2p[3, 8:16] = pack2(COARSE, two_up[0], two_up[1])

    pl.semaphore_wait(barrier, len(greeted))
    first = [
        send(pack.at[0, 4:8], got.at[0, 0:4], near(1, 1)),
        send(pack.at[1, 4:8], got.at[1, 0:4], near(1, -1)),
        send(pack.at[0, 0:4], got.at[0, 12:16], near(-1, 1)),
        send(pack.at[1, 0:4], got.at[1, 12:16], near(-1, -1)),
        send(cond.at[4:8], f0["k"].at[0:4, 8:40], near(1, 0)),
        send(cond.at[0:4], f0["k"].at[12:16, 8:40], near(-1, 0)),
        send(pack.at[0], got.at[0, 4:12], near(0, 1)),
        send(pack.at[1], got.at[1, 4:12], near(0, -1)),
        send(heat.at[5:8], f0["src"].at[1:4, 8:40], near(1, 0)),
        send(heat.at[0:3], f0["src"].at[12:15, 8:40], near(-1, 0)),
    ]

    cond1 = send_mid(k1p, NEAR_MID)
    cond2 = send_coarse(k2p, NEAR_COARSE + FAR_COARSE)
    in0, in1, in2 = (inside_rows(lv, n, narrow) for lv in (FINE, MID, COARSE))

    def unpack_cond(lv, packed, f, in_rows, p):
        for k, v in enumerate(unpack2(lv, packed[p])):
            ok = inside(lv, in_rows, 2 * p + k, w, wide)
            f["k"][2 * p + k] = jnp.where(ok, v * lv.scale, 0.0)

    arrive(first[:8])
    pass_token(0)
    pass_token(2)

    in_low, in_high = in0[0:8] & ~low4, in0[40:48] & low4

    def unpack(p):
        f0["k"][p, 0:8] = jnp.where(in_low, got[0, p], 0.0)
        f0["k"][p, 40:48] = jnp.where(in_high, got[1, p], 0.0)
        f0["src"][p, 0:8] = roll_rows(got[0, p], 4)
        f0["src"][p, 40:48] = roll_rows(got[1, p], 4)
        if not 4 <= p < 12:
            at = w * 8 + p - 4
            f0["k"][p] = jnp.where((at >= 0) & (at < 8 * wide), f0["k"][p], 0.0)

    planes(0, 16, unpack)
    coefficients(FINE, f0, in0, w, wide, 1, 15)
    arrive(first[8:])
    smooth_down(FINE, f0, ([(1, 15)], [(2, 14)], [(3, 13)]))

    def residual(lv, f, unroll):
        own = slice(8, 8 + lv.own_rows)

        def one(p):
            x = f["it"][p]
            (t,) = near_sum(lv, f, f["it"], p, [x])
            f["res"][p, own] = (f["src"][p] + t - f["diag"][p] * x)[own]

        planes(lv.first, lv.first + lv.own, one, unroll)

    arrive(cond1)
    for p in range(2, 8):
        unpack_cond(MID, k1p, f1, in1, p)
    coefficients(MID, f1, in1, w, wide, 5, 15)
    residual(FINE, f0, 8)
    r1 = restrict(FINE, lambda p: f0["res"][4 + p, 8:40], s["mix0"])
    for j in range(2):
        s1p[4 + j, 8:24] = pack2(MID, r1[2 * j], r1[2 * j + 1])

    for j in range(4):
        p, own = MID.first + j, slice(8, 24)
        hat = r1[j] * f1["inv"][p, own]
        share["src"][p, own] = r1[j]
        share["hat"][p, own] = hat
        share["upd"][p, own] = hat * (1.0 / THETA)
    sf = dict(f1, **share)
    smooth_down(MID, sf, ([], [(7, 13)], [(6, 14)]))
    for p in range(5, 15):
        v = sf["it"][p]
        (t,) = near_sum(MID, f1, sf["it"], p, [v])
        v = sf["src"][p] + t - f1["diag"][p] * v
        sf["res"][p] = v if 8 <= p < 12 else jnp.where(f1["inv"][p] > 0.0, v, 0.0)
    for p in range(8, 12):
        for tile in (slice(0, 8), slice(24, 32)):
            sf["res"][p, tile] = jnp.where(f1["inv"][p, tile] > 0.0, sf["res"][p, tile], 0.0)
    mix2 = s["mix2"]
    lane16 = lax.rem(lane_of(16), 4)
    part = []
    for j in range(6):
        mix2[j] = sf["res"][4 + 2 * j] + sf["res"][5 + 2 * j]
    for j in range(6):
        v = mix2[j, pl.ds(0, 16, stride=2), :] + mix2[j, pl.ds(1, 16, stride=2), :]
        part.append(0.125 * (v + jnp.where(lane16 < 2, roll_lanes(v, -2), roll_lanes(v, 2))))
    ct, cr = s["ct"], s["cr"]
    for i in range(2):
        a, b, c, d = part[2 * i : 2 * i + 4]
        ct[i] = jnp.where(lane16 < 2, jnp.where(lane16 == 0, a, b), jnp.where(lane16 == 2, c, d))

    def slot(dw, dn):
        return (dw + 3) * 3 + dn + 1

    parts = []
    for dw, dn in sorted(NEAR_COARSE + FAR_COARSE, key=lambda d: (-abs(d[1]), -abs(d[0]))):
        to = cr.at[slot(-dw, -dn)]
        which = pl.ds(1, 1) if dw >= 2 else pl.ds(0, 1) if dw <= -2 else pl.ds(0, 2)
        parts.append(send(ct.at[which], to.at[which], near(dw, dn)))
    src1 = send_mid(s1p, NEAR_MID)
    its = send_rows(f0["it"], s["edge"], 4, 8, 32, HALO_FINE, 3)
    src1_far = send_mid(s1p, FAR_MID)
    cond1_far = send_mid(k1p, FAR_MID)
    arrive(cond2)
    for p in range(7):
        unpack_cond(COARSE, k2p, f2, in2, p)
    coefficients(COARSE, f2, in2, w, wide, 1, 13)

    def unpack_src(p):
        f1["src"][2 * p], f1["src"][2 * p + 1] = unpack2(MID, s1p[p])

    arrive(parts)
    take_token(0)
    take_token(2)
    pass_token(1)
    u = s["basis"]

    def unpack_z(p):
        for k, v in enumerate(unpack2(COARSE, z2p[p])):
            u[0, 2 * p + k] = jnp.where(inside(COARSE, in2, 2 * p + k, w, wide), v, 0.0)

    def apply_b(k, p):
        v = u[k, p]
        (t,) = near_sum(COARSE, f2, u.at[k], p, [v])
        u[k + 1, p] = v - f2["inv"][p] * t

    lane8 = lane_of(8)
    head = lax.rem(lane8, 4) < 2
    bonds = {j: [None] * 4 for j in range(-3, 3)}

    def gain_of(j, dn, v, keep=None):
        for i in range(2):
            x = v[8 * i : 8 * i + 8]
            if keep is not None:
                x = jnp.where(keep, x, 0.0)
            at = dn + 1 + i
            bonds[j][at] = x if bonds[j][at] is None else bonds[j][at] + x

    for dn in (-1, 0, 1):
        lo = {d: cr.at[slot(d, dn), 0] for d in (-1, 0, 1, 2, 3)}
        hi = {d: cr.at[slot(d, dn), 1] for d in (-3, -2, -1, 0, 1)}
        if dn == 0:
            lo[0], hi[0] = ct.at[0], ct.at[1]
        gain_of(-3, dn, hi[-3][...])
        gain_of(-2, dn, hi[-2][...])
        gain_of(-2, dn, lo[-1][...], head)
        gain_of(-1, dn, hi[-1][...])
        gain_of(-1, dn, lo[0][...])
        gain_of(0, dn, lo[1][...])
        gain_of(0, dn, hi[0][...], ~head)
        gain_of(1, dn, lo[2][...])
        gain_of(1, dn, hi[1][...], ~head)
        gain_of(2, dn, lo[3][...])
    frame = s["frame"]
    for j in range(-2, 3):
        for i in range(4):
            v = jnp.where(head, bonds[j][i], bonds[j - 1][i])
            v = v + jnp.where(head, roll_lanes(v, -2), roll_lanes(v, 2))
            pair = unpack2(MID, v)
            for k in range(2):
                frame[j + 2, k, 8 * i : 8 * i + 8] = pair[k]
    for j in range(-2, 3):
        for k in range(2):
            p = 6 + 2 * j + k
            u[0, p] = roll_rows(frame[j + 2, k], -4)[0:24] * f2["inv"][p]
    z2p[3, 8:16] = pack2(COARSE, u[0, 6, 8:16], u[0, 7, 8:16])
    for k in range(4):
        for p in range(3 + k, 11 - k):
            apply_b(k, p)

    row8 = row_of(8)
    sums = [jnp.zeros((8, LANES), F32) for _ in range(16)]
    for p in (6, 7):
        d = f2["diag"][p, 8:16]
        b = [u[k, p, 8:16] for k in range(5)]
        c = [
            b[0],
            b[0] - b[1],
            b[0] - 2.0 * b[1] + b[2],
            b[0] - 3.0 * (b[1] - b[2]) - b[3],
            b[0] - 4.0 * (b[1] + b[3]) + 6.0 * b[2] + b[4],
        ]
        for at, vs in ((0, b), (8, c)):
            for k in range(8):
                sums[at + k] = sums[at + k] + vs[k // 2] * d * vs[(k + 1) // 2]
    tiles = []
    for half in (0, 8):
        m = jnp.zeros((8, LANES), F32)
        for k in range(8):
            m = jnp.where(row8 == k, jnp.sum(sums[half + k], axis=0, keepdims=True), m)
        tiles.append(jnp.sum(m, axis=1, keepdims=True))
    spread = jnp.where(lane8 == row8, tiles[0], 0.0) + jnp.where(lane8 == row8 + 8, tiles[1], 0.0)
    mine, all1, all2 = s["mine"], s["all1"], s["all2"]
    mine[0] = jnp.sum(spread, axis=0, keepdims=True)
    rank = lax.rem(w, 4) * narrow + n
    all1[rank] = mine[0]

    def send_sum(src, dst, peers, stage):
        for peer in peers:
            copy = pltpu.make_async_remote_copy(
                src_ref=src,
                dst_ref=dst,
                send_sem=s["sum_send"].at[stage],
                recv_sem=s["sum_recv"].at[stage],
                device_id=peer,
                device_id_type=MESH,
            )
            copy.start()

    early = list(sent)
    send_sum(mine.at[0], all1.at[rank], plane_peers, 0)
    z2_far = send_coarse(z2p, FAR_COARSE)

    arrive(cond1_far + src1 + src1_far)
    for p in (0, 1, 8, 9):
        unpack_cond(MID, k1p, f1, in1, p)
    for p in range(10):
        unpack_src(p)
    coefficients(MID, f1, in1, w, wide, 1, 5)
    coefficients(MID, f1, in1, w, wide, 15, 19)
    smooth_down(MID, f1, ([(1, 19)], [(2, 18)], [(3, 17)]))

    xa, xb, xe = s["mid_a"], s["mid_b"], s["mid_e"]
    ya, yb, ye = s["fine_a"], s["fine_b"], s["fine_e"]
    edge = s["edge"]

    def up_fine(v, with_source):
        for p in range(1, 15):
            t = xb[v, p // 2 + 6, 4:28]
            ya[v, p, pl.ds(0, 24, stride=2), :] = t
            ya[v, p, pl.ds(1, 24, stride=2), :] = t
        if with_source:
            for p in range(1, 15):
                ya[v, p] = ya[v, p] + jnp.where(f0["inv"][p] > 0.0, edge[p], 0.0)
        smooth_up(FINE, f0, ya.at[v], yb.at[v], ye.at[v], 1, 15, with_source, slice(8, 40))

    arrive(its)
    for p in range(4, 12):
        edge[p, 8:40] = f0["it"][p, 8:40]
    for p in range(3, 17):
        xa[0, p] = f1["it"][p]
    smooth_up(MID, f1, xa.at[0], xb.at[0], xe.at[0], 3, 17, True)
    up_fine(0, True)
    for c in early:
        c.wait_send()
    others = all1.at[pl.ds(0, len(plane_peers))]
    pltpu.make_async_copy(others, others, s["sum_recv"].at[0]).wait()
    mine[1] = jnp.sum(all1[...], axis=0)
    all2[z] = mine[1]
    take_token(1)
    send_sum(mine.at[1], all2.at[z], stack_peers, 1)
    arrive(z2_far)
    for p in (0, 6):
        unpack_z(p)
    for k in range(3):
        for p in (1 + k, 2 + k, 11 - k, 12 - k):
            apply_b(k, p)

    def up_basis(k, carry):
        v = k + 1
        for p in range(3, 17):
            t = u[k, p // 2 + 2, 4:20]
            xa[v, p, pl.ds(0, 16, stride=2), :] = t
            xa[v, p, pl.ds(1, 16, stride=2), :] = t
        smooth_up(MID, f1, xa.at[v], xb.at[v], xe.at[v], 3, 17, False)
        up_fine(v, False)
        return carry

    lax.fori_loop(0, 4, up_basis, 0)
    for c in z2_far:
        c.wait_send()
    others = all1.at[pl.ds(0, len(plane_peers))]
    pltpu.make_async_copy(others, others, s["sum_send"].at[0]).wait()
    others = all2.at[pl.ds(0, len(stack_peers))]
    pltpu.make_async_copy(others, others, s["sum_recv"].at[1]).wait()
    total = jnp.broadcast_to(jnp.sum(all2[...], axis=0), (8, LANES))
    ta = jnp.sum(jnp.where(lane8 == row8, total, 0.0), axis=1, keepdims=True)
    tb = jnp.sum(jnp.where(lane8 == row8 + 8, total, 0.0), axis=1, keepdims=True)
    ta, tb = jnp.broadcast_to(ta, (8, LANES)), jnp.broadcast_to(tb, (8, LANES))
    y = solve4([ta[k : k + 1] for k in range(8)] + [tb[k : k + 1] for k in range(8)])

    def combine(p):
        v = yb[0, p + 4, 8:40]
        for k in range(4):
            v = v + y[k] * yb[1 + k, p + 4, 8:40]
        out[p] = v

    planes(0, 8, combine)
    pltpu.make_async_copy(others, others, s["sum_send"].at[1]).wait()


def solution(mesh):
    wide, narrow = mesh.shape["wide"], mesh.shape["narrow"]

    def field(lv, *lead):
        return pltpu.VMEM((*lead, lv.planes, lv.rows, LANES), F32)

    scratch = {}
    for tag, lv in (("f0_", FINE), ("f1_", MID)):
        for k in FIELDS:
            scratch[tag + k] = field(lv)
    for k in ("k", "cx", "cyu", "cyd", "czr", "czl", "inv", "diag"):
        scratch["f2_" + k] = field(COARSE)
    scratch["basis"] = field(COARSE, 5)
    scratch["edge"] = field(FINE)
    for k in ("a", "b", "e"):
        scratch["mid_" + k] = field(MID, 5)
        scratch["fine_" + k] = field(FINE, 5)
    scratch["pack"] = pltpu.VMEM((2, 8, 8, LANES), F32)
    scratch["got"] = pltpu.VMEM((2, 16, 8, LANES), F32)
    scratch["mix0"] = pltpu.VMEM((4, 32, LANES), F32)
    scratch["mix1"] = pltpu.VMEM((2, 16, LANES), F32)
    for k in ("k1p", "s1p"):
        scratch[k] = pltpu.VMEM((10, 32, LANES), F32)
    for k in ("k2p", "z2p"):
        scratch[k] = pltpu.VMEM((7, 24, LANES), F32)
    scratch["mine"] = pltpu.VMEM((2, 1, LANES), F32)
    scratch["all1"] = pltpu.VMEM((4 * narrow, 1, LANES), F32)
    scratch["all2"] = pltpu.VMEM((wide // 4, 1, LANES), F32)
    for k in ("src", "hat", "upd", "tmp", "it", "res"):
        scratch["share_" + k] = field(MID)
    scratch["mix2"] = pltpu.VMEM((6, 32, LANES), F32)
    scratch["ct"] = pltpu.VMEM((2, 16, LANES), F32)
    scratch["cr"] = pltpu.VMEM((21, 2, 16, LANES), F32)
    scratch["frame"] = pltpu.VMEM((5, 2, 32, LANES), F32)
    messages = 10 + len(HALO_FINE) + 2 * len(NEAR_MID + FAR_MID + NEAR_COARSE) + 3 * len(FAR_COARSE)
    scratch["send_sem"] = pltpu.SemaphoreType.DMA((messages,))
    scratch["recv_sem"] = pltpu.SemaphoreType.DMA((messages,))
    scratch["sum_send"] = pltpu.SemaphoreType.DMA((2,))
    scratch["sum_recv"] = pltpu.SemaphoreType.DMA((2,))
    scratch["local_sem"] = pltpu.SemaphoreType.DMA((2,))
    for i in range(3):
        scratch[f"token{i}"] = pltpu.SemaphoreType.REGULAR

    def body(heat, cond):
        heat = pltpu.with_memory_space_constraint(heat, pltpu.HBM)
        cond = pltpu.with_memory_space_constraint(cond, pltpu.HBM)
        return pl.pallas_call(
            functools.partial(kernel, wide, narrow, tuple(scratch)),
            out_shape=pltpu.VMEM((8, 32, LANES), F32),
            in_specs=[pl.BlockSpec(memory_space=pltpu.HBM)] * 2,
            out_specs=pl.BlockSpec(memory_space=pltpu.VMEM),
            scratch_shapes=list(scratch.values()),
            compiler_params=pltpu.CompilerParams(
                collective_id=0, has_side_effects=True, vmem_limit_bytes=40 * 2**20
            ),
            cost_estimate=pl.CostEstimate(flops=50_000_000, bytes_accessed=400_000, transcendentals=0),
            name="vcycle",
        )(heat, cond)

    spec = P("wide", "narrow", None)
    return jax.shard_map(body, mesh=mesh, in_specs=(spec, spec), out_specs=spec, check_vma=False)
```

```python
import functools
import jax
import jax.numpy as jnp
from jax import lax
from jax.experimental import pallas as pl
from jax.experimental.pallas import tpu as pltpu
from jax.sharding import PartitionSpec as P

MASS = 0.002
LOW, HIGH = 0.25, 2.0
THETA = 0.5 * (HIGH + LOW)
DELTA = 0.5 * (HIGH - LOW)
SIGMA = THETA / DELTA
RHO1 = 1.0 / SIGMA
RHO2 = 1.0 / (2.0 * SIGMA - RHO1)
RHO3 = 1.0 / (2.0 * SIGMA - RHO2)
KEEP1, GAIN1 = RHO2 * RHO1, 2.0 * RHO2 / DELTA
KEEP2, GAIN2 = RHO3 * RHO2, 2.0 * RHO3 / DELTA
F32 = jnp.float32
LANES = 128
MESH = pl.DeviceIdType.MESH


class Level:
    def __init__(self, planes, first, own, rows, own_rows, repeat, scale):
        self.planes, self.first, self.own = planes, first, own
        self.rows, self.own_rows, self.repeat, self.scale = rows, own_rows, repeat, scale


FINE = Level(16, 4, 8, 48, 32, 1, 1.0)
MID = Level(20, 8, 4, 32, 16, 2, 0.25)
COARSE = Level(14, 6, 2, 24, 8, 4, 1.0 / 16.0)

FIELDS = ("k", "cx", "cyu", "cyd", "czr", "czl", "inv", "diag", "src", "hat", "upd", "it", "tmp", "res")


def planes(lo, hi, fn, unroll=99):
    count = hi - lo
    unroll = min(unroll, count)
    while count % unroll:
        unroll -= 1
    if unroll == count:
        for p in range(lo, hi):
            fn(p)
        return

    def step(i, carry):
        for k in range(unroll):
            fn(lo + i * unroll + k)
        return carry

    lax.fori_loop(0, count // unroll, step, 0)


def roll_rows(x, by):
    return pltpu.roll(x, by % x.shape[0], 0)


def roll_lanes(x, by):
    return pltpu.roll(x, by % LANES, 1)


def lane_of(rows):
    return lax.broadcasted_iota(jnp.int32, (rows, LANES), 1)


def row_of(rows):
    return lax.broadcasted_iota(jnp.int32, (rows, LANES), 0)


def near_sum(lv, f, ref, p, centers):
    cxu, cxd = f["cx"][p], f["cx"][p - 1]
    cyu, cyd, czr, czl = f["cyu"][p], f["cyd"][p], f["czr"][p], f["czl"][p]
    sums = []
    for v, c in enumerate(centers):
        at = ref.at[v] if len(ref.shape) == 4 else ref
        sums.append(
            cxu * at[p + 1]
            + cxd * at[p - 1]
            + cyu * roll_rows(c, -1)
            + cyd * roll_rows(c, 1)
            + czr * roll_lanes(c, -lv.repeat)
            + czl * roll_lanes(c, lv.repeat)
        )
    return sums


def inside_rows(lv, n, narrow):
    rows = row_of(lv.rows) + (n * lv.own_rows - 8)
    return (rows >= 0) & (rows < lv.own_rows * narrow)


def inside(lv, in_rows, p, w, wide):
    if isinstance(p, int) and lv.first <= p < lv.first + lv.own:
        return in_rows
    at = w * lv.own + p - lv.first
    return in_rows & (at >= 0) & (at < lv.own * wide)


def pack2(lv, x, y):
    return jnp.where(lax.rem(lane_of(x.shape[0]) // (lv.repeat // 2), 2) == 0, x, y)


def unpack2(lv, xy):
    half = lv.repeat // 2
    first = lax.rem(lane_of(xy.shape[0]) // half, 2) == 0
    return jnp.where(first, xy, roll_lanes(xy, half)), jnp.where(first, roll_lanes(xy, -half), xy)


def coefficients(lv, f, in_rows, w, wide, lo, hi, unroll=99):
    lane = lane_of(lv.rows)
    last = lane >= LANES - lv.repeat
    edge = last | (lane < lv.repeat)
    f["cx"][lo - 1] = 0.5 * (f["k"][lo - 1] + f["k"][lo])

    def one(p):
        k = f["k"][p]
        cxu = 0.5 * (k + f["k"][p + 1])
        cxd = 0.5 * (k + f["k"][p - 1])
        cyu = 0.5 * (k + roll_rows(k, -1))
        cyd = roll_rows(cyu, 1)
        czr = jnp.where(last, 0.0, 0.5 * (k + roll_lanes(k, -lv.repeat)))
        czl = roll_lanes(czr, lv.repeat)
        d = MASS + (cxu + cxd + cyu + cyd + czr + czl + jnp.where(edge, 0.5 * k, 0.0))
        f["cx"][p] = cxu
        f["cyu"][p] = cyu
        f["cyd"][p] = cyd
        f["czr"][p] = czr
        f["czl"][p] = czl
        f["diag"][p] = d
        f["inv"][p] = jnp.where(inside(lv, in_rows, p, w, wide), 1.0 / d, 0.0)

    planes(lo, hi, one, unroll)


def restrict(lv, read, mix):
    for j in range(lv.own // 2):
        mix[j] = read(2 * j) + read(2 * j + 1)
    half = lv.own_rows // 2
    even = lax.rem(lane_of(half) // lv.repeat, 2) == 0
    found = []
    for j in range(lv.own // 2):
        x = mix[j, pl.ds(0, half, stride=2), :] + mix[j, pl.ds(1, half, stride=2), :]
        x = x + jnp.where(even, roll_lanes(x, -lv.repeat), roll_lanes(x, lv.repeat))
        found.append(0.125 * x)
    return found


def smooth_down(lv, f, steps, unroll=99):
    def first(p):
        hat = f["src"][p] * f["inv"][p]
        f["hat"][p] = hat
        f["upd"][p] = hat * (1.0 / THETA)

    def second(p):
        x = f["upd"][p]
        (s,) = near_sum(lv, f, f["upd"], p, [x])
        z = f["hat"][p] + f["inv"][p] * s - x
        f["tmp"][p] = x + (KEEP1 * x + GAIN1 * z)

    def third(p):
        x = f["tmp"][p]
        (s,) = near_sum(lv, f, f["tmp"], p, [x])
        z = f["hat"][p] + f["inv"][p] * s - x
        f["it"][p] = x + (KEEP2 * (x - f["upd"][p]) + GAIN2 * z)

    for step, ranges in zip((first, second, third), steps):
        for lo, hi in ranges:
            planes(lo, hi, step, unroll)


def sweep_up(lv, f, old, new, upd, lo, hi, keep, gain, with_source, own=None):
    for p in range(lo, hi):
        c = old[p]
        (t,) = near_sum(lv, f, old, p, [c])
        z = f["inv"][p] * t - c
        if with_source:
            z = z + f["hat"][p]
        u = gain * z if keep is None else keep * upd[p] + gain * z
        if own is None:
            upd[p] = u
            new[p] = c + u
        else:
            new[p, own] = (c + u)[own]


def smooth_up(lv, f, a, b, upd, lo, hi, with_source, own=None):
    sweep_up(lv, f, a, b, upd, lo + 1, hi - 1, None, 1.0 / THETA, with_source)
    sweep_up(lv, f, b, a, upd, lo + 2, hi - 2, KEEP1, GAIN1, with_source)
    sweep_up(lv, f, a, b, upd, lo + 3, hi - 3, KEEP2, GAIN2, with_source, own)


def solve4(m):
    small = m[1] < 0.5 * m[0]
    pick = lambda a, b: jnp.where(small, a, b)
    g = [pick(m[k + 1], m[8 + k] - m[9 + k]) for k in range(7)]
    rhs = [pick(m[k], m[8 + k]) for k in range(4)]
    rows = [[g[i + j] for j in range(4)] for i in range(4)]
    inv = []
    for i in range(4):
        piv = rows[i][i]
        good = piv > 1e-7 * g[2 * i]
        inv.append(jnp.where(good, 1.0 / jnp.where(good, piv, 1.0), 0.0))
        for r in range(i + 1, 4):
            factor = rows[i][r] * inv[i]
            rows[r] = [rows[r][j] - factor * rows[i][j] if j >= r else None for j in range(4)]
            rhs[r] = rhs[r] - factor * rhs[i]
    y = [None] * 4
    for i in (3, 2, 1, 0):
        t = rhs[i]
        for j in range(i + 1, 4):
            t = t - rows[i][j] * y[j]
        y[i] = t * inv[i]
    turned = [
        y[0] + y[1] + y[2] + y[3],
        -(y[1] + 2.0 * y[2] + 3.0 * y[3]),
        y[2] + 3.0 * y[3],
        -y[3],
    ]
    return [pick(a, b) for a, b in zip(y, turned)]


def halo(reach):
    return [(dw, dn) for dn in (1, -1, 0) for dw in reach if (dw, dn) != (0, 0)]


NEAR_MID, FAR_MID = halo((1, -1, 0)), halo((2, -2))
NEAR_COARSE, FAR_COARSE = halo((1, -1, 0, 2, -2)), halo((3, -3))
HALO_FINE = halo((1, -1, 0))


def kernel(wide, narrow, names, heat, cond, out, *refs):
    s = dict(zip(names, refs))
    w, n = lax.axis_index("wide"), lax.axis_index("narrow")
    z, ylo, core = w // 4, lax.rem(w // 2, 2), lax.rem(w, 2)
    yhi, x = n // 4, lax.rem(n, 4)
    stacks = wide // 4

    f0 = {k: s["f0_" + k] for k in FIELDS}
    f1 = {k: s["f1_" + k] for k in FIELDS}
    f2 = {k: s["f2_" + k] for k in FIELDS if "f2_" + k in s}

    def near(dw, dn):
        return (lax.rem(w + (dw + wide), wide), lax.rem(n + (dn + narrow), narrow))

    def stack(dz):
        return (lax.rem(w + (4 * dz + wide), wide), n)

    def plane_peer(dx, dhi, dlo, dc):
        to = z * 4 + lax.rem(ylo + dlo, 2) * 2 + lax.rem(core + dc, 2)
        return (to, lax.rem(yhi + dhi, 2) * 4 + lax.rem(x + dx, 4))

    plane_peers = [
        plane_peer(*d)
        for d in sorted(
            [(dx, dhi, dlo, dc) for dx in range(4) for dhi in range(2) for dlo in range(2) for dc in range(2)],
            key=lambda d: -min(d[0], 4 - d[0]) - (1 if d[2] else 2 * d[1]),
        )
        if any(d)
    ]
    stack_peers = [stack(d) for d in sorted(range(1, stacks), key=lambda d: -min(d, stacks - d))]

    barrier = pltpu.get_barrier_semaphore()
    greeted = HALO_FINE + [d for d in NEAR_COARSE + FAR_COARSE if d not in HALO_FINE] + [(8, 0), (-8, 0), (4, 0), (-4, 0)]
    for d in greeted[:8]:
        pl.semaphore_signal(barrier, inc=1, device_id=near(*d), device_id_type=MESH)
    own_heat = pltpu.make_async_copy(heat, f0["src"].at[4:12, 8:40], s["local_sem"].at[0])
    own_cond = pltpu.make_async_copy(cond, f0["k"].at[4:12, 8:40], s["local_sem"].at[1])
    own_cond.start()
    own_heat.start()
    for d in greeted[8:]:
        pl.semaphore_signal(barrier, inc=1, device_id=near(*d), device_id_type=MESH)
    share = {k: s["share_" + k] for k in ("src", "hat", "upd", "tmp", "it", "res")}
    for ref in share.values():
        ref[4:16] = jnp.zeros((12, 32, LANES), F32)

    used = [0]
    sent = []

    def send(src, dst, peer):
        i = used[0]
        used[0] += 1
        copy = pltpu.make_async_remote_copy(
            src_ref=src,
            dst_ref=dst,
            send_sem=s["send_sem"].at[i],
            recv_sem=s["recv_sem"].at[i],
            device_id=peer,
            device_id_type=MESH,
        )
        copy.start()
        sent.append(copy)
        return copy

    def send_rows(ref_from, ref_to, first, own, own_rows, reach, depth):
        copies = []
        for dw, dn in reach:
            a, c, b = first, own, first - dw * own
            if depth < own and dw:
                a, b = (first + own - depth, first - depth) if dw > 0 else (first, first + own)
                c = depth
            ra, rc, rb = (8, own_rows, 8) if dn == 0 else (own_rows, 8, 0) if dn > 0 else (8, 8, 8 + own_rows)
            copies.append(
                send(ref_from.at[a : a + c, ra : ra + rc], ref_to.at[b : b + c, rb : rb + rc], near(dw, dn))
            )
        return copies

    def send_mid(ref, reach):
        return send_rows(ref, ref, 4, 2, 16, reach, 2)

    def send_coarse(ref, reach):
        return send_rows(ref, ref, 3, 1, 8, reach, 1)

    def arrive(copies):
        for c in copies:
            c.wait_recv()

    tokens = [s["token0"], s["token1"], s["token2"]]
    heard = [[stack(2), stack(-2)], [stack(4), stack(-4)], [near(0, 2), near(0, -2)]]

    def pass_token(i):
        for peer in heard[i]:
            pl.semaphore_signal(tokens[i], inc=1, device_id=peer, device_id_type=MESH)

    def take_token(i):
        pl.semaphore_wait(tokens[i], 2)

    own_cond.wait()
    own_heat.wait()
    low4 = row_of(8) < 4
    pack, got = s["pack"], s["got"]

    def pack_plane(p):
        h, c = f0["src"][p + 4, 32:40], f0["k"][p + 4, 32:40]
        pack[0, p] = jnp.where(low4, roll_rows(h, 4), c)
        h, c = f0["src"][p + 4, 8:16], f0["k"][p + 4, 8:16]
        pack[1, p] = jnp.where(low4, c, roll_rows(h, 4))

    planes(0, 8, pack_plane, 8)
    k1p, k2p, s1p, z2p = s["k1p"], s["k2p"], s["s1p"], s["z2p"]
    one_up = restrict(FINE, lambda p: f0["k"][4 + p, 8:40], s["mix0"])
    two_up = restrict(MID, lambda p: one_up[p], s["mix1"])
    for j in range(2):
        k1p[4 + j, 8:24] = pack2(MID, one_up[2 * j], one_up[2 * j + 1])
    k2p[3, 8:16] = pack2(COARSE, two_up[0], two_up[1])

    pl.semaphore_wait(barrier, len(greeted))
    first = [
        send(pack.at[0, 4:8], got.at[0, 0:4], near(1, 1)),
        send(pack.at[1, 4:8], got.at[1, 0:4], near(1, -1)),
        send(pack.at[0, 0:4], got.at[0, 12:16], near(-1, 1)),
        send(pack.at[1, 0:4], got.at[1, 12:16], near(-1, -1)),
        send(cond.at[4:8], f0["k"].at[0:4, 8:40], near(1, 0)),
        send(cond.at[0:4], f0["k"].at[12:16, 8:40], near(-1, 0)),
        send(pack.at[0], got.at[0, 4:12], near(0, 1)),
        send(pack.at[1], got.at[1, 4:12], near(0, -1)),
        send(heat.at[5:8], f0["src"].at[1:4, 8:40], near(1, 0)),
        send(heat.at[0:3], f0["src"].at[12:15, 8:40], near(-1, 0)),
    ]

    cond1 = send_mid(k1p, NEAR_MID)
    cond2 = send_coarse(k2p, NEAR_COARSE + FAR_COARSE)
    in0, in1, in2 = (inside_rows(lv, n, narrow) for lv in (FINE, MID, COARSE))

    def unpack_cond(lv, packed, f, in_rows, p):
        for k, v in enumerate(unpack2(lv, packed[p])):
            ok = inside(lv, in_rows, 2 * p + k, w, wide)
            f["k"][2 * p + k] = jnp.where(ok, v * lv.scale, 0.0)

    arrive(first[:8])
    pass_token(0)
    pass_token(2)

    in_low, in_high = in0[0:8] & ~low4, in0[40:48] & low4

    def unpack(p):
        f0["k"][p, 0:8] = jnp.where(in_low, got[0, p], 0.0)
        f0["k"][p, 40:48] = jnp.where(in_high, got[1, p], 0.0)
        f0["src"][p, 0:8] = roll_rows(got[0, p], 4)
        f0["src"][p, 40:48] = roll_rows(got[1, p], 4)
        if not 4 <= p < 12:
            at = w * 8 + p - 4
            f0["k"][p] = jnp.where((at >= 0) & (at < 8 * wide), f0["k"][p], 0.0)

    planes(0, 16, unpack)
    coefficients(FINE, f0, in0, w, wide, 1, 15)
    arrive(first[8:])
    smooth_down(FINE, f0, ([(1, 15)], [(2, 14)], [(3, 13)]))

    def residual(lv, f, unroll):
        own = slice(8, 8 + lv.own_rows)

        def one(p):
            x = f["it"][p]
            (t,) = near_sum(lv, f, f["it"], p, [x])
            f["res"][p, own] = (f["src"][p] + t - f["diag"][p] * x)[own]

        planes(lv.first, lv.first + lv.own, one, unroll)

    arrive(cond1)
    for p in range(2, 8):
        unpack_cond(MID, k1p, f1, in1, p)
    coefficients(MID, f1, in1, w, wide, 5, 15)
    residual(FINE, f0, 8)
    r1 = restrict(FINE, lambda p: f0["res"][4 + p, 8:40], s["mix0"])
    for j in range(2):
        s1p[4 + j, 8:24] = pack2(MID, r1[2 * j], r1[2 * j + 1])

    for j in range(4):
        p, own = MID.first + j, slice(8, 24)
        hat = r1[j] * f1["inv"][p, own]
        share["src"][p, own] = r1[j]
        share["hat"][p, own] = hat
        share["upd"][p, own] = hat * (1.0 / THETA)
    sf = dict(f1, **share)
    smooth_down(MID, sf, ([], [(7, 13)], [(6, 14)]))
    for p in range(5, 15):
        v = sf["it"][p]
        (t,) = near_sum(MID, f1, sf["it"], p, [v])
        v = sf["src"][p] + t - f1["diag"][p] * v
        sf["res"][p] = v if 8 <= p < 12 else jnp.where(f1["inv"][p] > 0.0, v, 0.0)
    for p in range(8, 12):
        for tile in (slice(0, 8), slice(24, 32)):
            sf["res"][p, tile] = jnp.where(f1["inv"][p, tile] > 0.0, sf["res"][p, tile], 0.0)
    mix2 = s["mix2"]
    lane16 = lax.rem(lane_of(16), 4)
    part = []
    for j in range(6):
        mix2[j] = sf["res"][4 + 2 * j] + sf["res"][5 + 2 * j]
    for j in range(6):
        v = mix2[j, pl.ds(0, 16, stride=2), :] + mix2[j, pl.ds(1, 16, stride=2), :]
        part.append(0.125 * (v + jnp.where(lane16 < 2, roll_lanes(v, -2), roll_lanes(v, 2))))
    ct, cr = s["ct"], s["cr"]
    for i in range(2):
        a, b, c, d = part[2 * i : 2 * i + 4]
        ct[i] = jnp.where(lane16 < 2, jnp.where(lane16 == 0, a, b), jnp.where(lane16 == 2, c, d))

    def slot(dw, dn):
        return (dw + 3) * 3 + dn + 1

    parts = []
    for dw, dn in sorted(NEAR_COARSE + FAR_COARSE, key=lambda d: (-abs(d[1]), -abs(d[0]))):
        to = cr.at[slot(-dw, -dn)]
        which = pl.ds(1, 1) if dw >= 2 else pl.ds(0, 1) if dw <= -2 else pl.ds(0, 2)
        parts.append(send(ct.at[which], to.at[which], near(dw, dn)))
    src1 = send_mid(s1p, NEAR_MID)
    its = send_rows(f0["it"], s["edge"], 4, 8, 32, HALO_FINE, 3)
    src1_far = send_mid(s1p, FAR_MID)
    cond1_far = send_mid(k1p, FAR_MID)
    arrive(cond2)
    for p in range(7):
        unpack_cond(COARSE, k2p, f2, in2, p)
    coefficients(COARSE, f2, in2, w, wide, 1, 13)

    def unpack_src(p):
        f1["src"][2 * p], f1["src"][2 * p + 1] = unpack2(MID, s1p[p])

    arrive(parts)
    take_token(0)
    take_token(2)
    pass_token(1)
    u = s["basis"]

    def unpack_z(p):
        for k, v in enumerate(unpack2(COARSE, z2p[p])):
            u[0, 2 * p + k] = jnp.where(inside(COARSE, in2, 2 * p + k, w, wide), v, 0.0)

    def apply_b(k, p):
        v = u[k, p]
        (t,) = near_sum(COARSE, f2, u.at[k], p, [v])
        u[k + 1, p] = v - f2["inv"][p] * t

    lane8 = lane_of(8)
    head = lax.rem(lane8, 4) < 2
    bonds = {j: [None] * 4 for j in range(-3, 3)}

    def gain_of(j, dn, v, keep=None):
        for i in range(2):
            x = v[8 * i : 8 * i + 8]
            if keep is not None:
                x = jnp.where(keep, x, 0.0)
            at = dn + 1 + i
            bonds[j][at] = x if bonds[j][at] is None else bonds[j][at] + x

    for dn in (-1, 0, 1):
        lo = {d: cr.at[slot(d, dn), 0] for d in (-1, 0, 1, 2, 3)}
        hi = {d: cr.at[slot(d, dn), 1] for d in (-3, -2, -1, 0, 1)}
        if dn == 0:
            lo[0], hi[0] = ct.at[0], ct.at[1]
        gain_of(-3, dn, hi[-3][...])
        gain_of(-2, dn, hi[-2][...])
        gain_of(-2, dn, lo[-1][...], head)
        gain_of(-1, dn, hi[-1][...])
        gain_of(-1, dn, lo[0][...])
        gain_of(0, dn, lo[1][...])
        gain_of(0, dn, hi[0][...], ~head)
        gain_of(1, dn, lo[2][...])
        gain_of(1, dn, hi[1][...], ~head)
        gain_of(2, dn, lo[3][...])
    frame = s["frame"]
    for j in range(-2, 3):
        for i in range(4):
            v = jnp.where(head, bonds[j][i], bonds[j - 1][i])
            v = v + jnp.where(head, roll_lanes(v, -2), roll_lanes(v, 2))
            pair = unpack2(MID, v)
            for k in range(2):
                frame[j + 2, k, 8 * i : 8 * i + 8] = pair[k]
    for j in range(-2, 3):
        for k in range(2):
            p = 6 + 2 * j + k
            u[0, p] = roll_rows(frame[j + 2, k], -4)[0:24] * f2["inv"][p]
    z2p[3, 8:16] = pack2(COARSE, u[0, 6, 8:16], u[0, 7, 8:16])
    for k in range(4):
        for p in range(3 + k, 11 - k):
            apply_b(k, p)

    row8 = row_of(8)
    sums = [jnp.zeros((8, LANES), F32) for _ in range(16)]
    for p in (6, 7):
        d = f2["diag"][p, 8:16]
        b = [u[k, p, 8:16] for k in range(5)]
        c = [
            b[0],
            b[0] - b[1],
            b[0] - 2.0 * b[1] + b[2],
            b[0] - 3.0 * (b[1] - b[2]) - b[3],
            b[0] - 4.0 * (b[1] + b[3]) + 6.0 * b[2] + b[4],
        ]
        for at, vs in ((0, b), (8, c)):
            for k in range(8):
                sums[at + k] = sums[at + k] + vs[k // 2] * d * vs[(k + 1) // 2]
    tiles = []
    for half in (0, 8):
        m = jnp.zeros((8, LANES), F32)
        for k in range(8):
            m = jnp.where(row8 == k, jnp.sum(sums[half + k], axis=0, keepdims=True), m)
        tiles.append(jnp.sum(m, axis=1, keepdims=True))
    spread = jnp.where(lane8 == row8, tiles[0], 0.0) + jnp.where(lane8 == row8 + 8, tiles[1], 0.0)
    mine, all1, all2 = s["mine"], s["all1"], s["all2"]
    mine[0] = jnp.sum(spread, axis=0, keepdims=True)
    rank = lax.rem(w, 4) * narrow + n
    all1[rank] = mine[0]

    def send_sum(src, dst, peers, stage):
        for peer in peers:
            copy = pltpu.make_async_remote_copy(
                src_ref=src,
                dst_ref=dst,
                send_sem=s["sum_send"].at[stage],
                recv_sem=s["sum_recv"].at[stage],
                device_id=peer,
                device_id_type=MESH,
            )
            copy.start()

    early = list(sent)
    send_sum(mine.at[0], all1.at[rank], plane_peers, 0)
    z2_far = send_coarse(z2p, FAR_COARSE)

    arrive(cond1_far + src1 + src1_far)
    for p in (0, 1, 8, 9):
        unpack_cond(MID, k1p, f1, in1, p)
    for p in range(10):
        unpack_src(p)
    coefficients(MID, f1, in1, w, wide, 1, 5)
    coefficients(MID, f1, in1, w, wide, 15, 19)
    smooth_down(MID, f1, ([(1, 19)], [(2, 18)], [(3, 17)]))

    xa, xb, xe = s["mid_a"], s["mid_b"], s["mid_e"]
    ya, yb, ye = s["fine_a"], s["fine_b"], s["fine_e"]
    edge = s["edge"]

    def up_fine(v, with_source):
        for p in range(1, 15):
            t = xb[v, p // 2 + 6, 4:28]
            ya[v, p, pl.ds(0, 24, stride=2), :] = t
            ya[v, p, pl.ds(1, 24, stride=2), :] = t
        if with_source:
            for p in range(1, 15):
                ya[v, p] = ya[v, p] + jnp.where(f0["inv"][p] > 0.0, edge[p], 0.0)
        smooth_up(FINE, f0, ya.at[v], yb.at[v], ye.at[v], 1, 15, with_source, slice(8, 40))

    arrive(its)
    for p in range(4, 12):
        edge[p, 8:40] = f0["it"][p, 8:40]
    for p in range(3, 17):
        xa[0, p] = f1["it"][p]
    smooth_up(MID, f1, xa.at[0], xb.at[0], xe.at[0], 3, 17, True)
    up_fine(0, True)
    for c in early:
        c.wait_send()
    others = all1.at[pl.ds(0, len(plane_peers))]
    pltpu.make_async_copy(others, others, s["sum_recv"].at[0]).wait()
    mine[1] = jnp.sum(all1[...], axis=0)
    all2[z] = mine[1]
    take_token(1)
    send_sum(mine.at[1], all2.at[z], stack_peers, 1)
    arrive(z2_far)
    for p in (0, 6):
        unpack_z(p)
    for k in range(3):
        for p in (1 + k, 2 + k, 11 - k, 12 - k):
            apply_b(k, p)

    def up_basis(k, carry):
        v = k + 1
        for p in range(3, 17):
            t = u[k, p // 2 + 2, 4:20]
            xa[v, p, pl.ds(0, 16, stride=2), :] = t
            xa[v, p, pl.ds(1, 16, stride=2), :] = t
        smooth_up(MID, f1, xa.at[v], xb.at[v], xe.at[v], 3, 17, False)
        up_fine(v, False)
        return carry

    lax.fori_loop(0, 4, up_basis, 0)
    for c in z2_far:
        c.wait_send()
    others = all1.at[pl.ds(0, len(plane_peers))]
    pltpu.make_async_copy(others, others, s["sum_send"].at[0]).wait()
    others = all2.at[pl.ds(0, len(stack_peers))]
    pltpu.make_async_copy(others, others, s["sum_recv"].at[1]).wait()
    total = jnp.broadcast_to(jnp.sum(all2[...], axis=0), (8, LANES))
    ta = jnp.sum(jnp.where(lane8 == row8, total, 0.0), axis=1, keepdims=True)
    tb = jnp.sum(jnp.where(lane8 == row8 + 8, total, 0.0), axis=1, keepdims=True)
    ta, tb = jnp.broadcast_to(ta, (8, LANES)), jnp.broadcast_to(tb, (8, LANES))
    y = solve4([ta[k : k + 1] for k in range(8)] + [tb[k : k + 1] for k in range(8)])

    def combine(p):
        v = yb[0, p + 4, 8:40]
        for k in range(4):
            v = v + y[k] * yb[1 + k, p + 4, 8:40]
        out[p] = v

    planes(0, 8, combine)
    pltpu.make_async_copy(others, others, s["sum_send"].at[1]).wait()


def solution(mesh):
    wide, narrow = mesh.shape["wide"], mesh.shape["narrow"]

    def field(lv, *lead):
        return pltpu.VMEM((*lead, lv.planes, lv.rows, LANES), F32)

    scratch = {}
    for tag, lv in (("f0_", FINE), ("f1_", MID)):
        for k in FIELDS:
            scratch[tag + k] = field(lv)
    for k in ("k", "cx", "cyu", "cyd", "czr", "czl", "inv", "diag"):
        scratch["f2_" + k] = field(COARSE)
    scratch["basis"] = field(COARSE, 5)
    scratch["edge"] = field(FINE)
    for k in ("a", "b", "e"):
        scratch["mid_" + k] = field(MID, 5)
        scratch["fine_" + k] = field(FINE, 5)
    scratch["pack"] = pltpu.VMEM((2, 8, 8, LANES), F32)
    scratch["got"] = pltpu.VMEM((2, 16, 8, LANES), F32)
    scratch["mix0"] = pltpu.VMEM((4, 32, LANES), F32)
    scratch["mix1"] = pltpu.VMEM((2, 16, LANES), F32)
    for k in ("k1p", "s1p"):
        scratch[k] = pltpu.VMEM((10, 32, LANES), F32)
    for k in ("k2p", "z2p"):
        scratch[k] = pltpu.VMEM((7, 24, LANES), F32)
    scratch["mine"] = pltpu.VMEM((2, 1, LANES), F32)
    scratch["all1"] = pltpu.VMEM((4 * narrow, 1, LANES), F32)
    scratch["all2"] = pltpu.VMEM((wide // 4, 1, LANES), F32)
    for k in ("src", "hat", "upd", "tmp", "it", "res"):
        scratch["share_" + k] = field(MID)
    scratch["mix2"] = pltpu.VMEM((6, 32, LANES), F32)
    scratch["ct"] = pltpu.VMEM((2, 16, LANES), F32)
    scratch["cr"] = pltpu.VMEM((21, 2, 16, LANES), F32)
    scratch["frame"] = pltpu.VMEM((5, 2, 32, LANES), F32)
    messages = 10 + len(HALO_FINE) + 2 * len(NEAR_MID + FAR_MID + NEAR_COARSE) + 3 * len(FAR_COARSE)
    scratch["send_sem"] = pltpu.SemaphoreType.DMA((messages,))
    scratch["recv_sem"] = pltpu.SemaphoreType.DMA((messages,))
    scratch["sum_send"] = pltpu.SemaphoreType.DMA((2,))
    scratch["sum_recv"] = pltpu.SemaphoreType.DMA((2,))
    scratch["local_sem"] = pltpu.SemaphoreType.DMA((2,))
    for i in range(3):
        scratch[f"token{i}"] = pltpu.SemaphoreType.REGULAR

    def body(heat, cond):
        heat = pltpu.with_memory_space_constraint(heat, pltpu.HBM)
        cond = pltpu.with_memory_space_constraint(cond, pltpu.HBM)
        return pl.pallas_call(
            functools.partial(kernel, wide, narrow, tuple(scratch)),
            out_shape=pltpu.VMEM((8, 32, LANES), F32),
            in_specs=[pl.BlockSpec(memory_space=pltpu.HBM)] * 2,
            out_specs=pl.BlockSpec(memory_space=pltpu.VMEM),
            scratch_shapes=list(scratch.values()),
            compiler_params=pltpu.CompilerParams(
                collective_id=0, has_side_effects=True, vmem_limit_bytes=40 * 2**20
            ),
            cost_estimate=pl.CostEstimate(flops=50_000_000, bytes_accessed=400_000, transcendentals=0),
            name="vcycle",
        )(heat, cond)

    spec = P("wide", "narrow", None)
    return jax.shard_map(body, mesh=mesh, in_specs=(spec, spec), out_specs=spec, check_vma=False)
```
